32 devices in a mesh: fsdp: 8 (over y, x, core), replica: 4 (over z).
Axes of the slice: x: 2, y: 2, z: 4, core: 2. Of those that a mesh axis runs over, the one named last changes fastest.
Arguments:
- tokens: bfloat16 [6144, 2048], P(('fsdp', 'replica')), may hold values from -6 to 6
- cotangent: bfloat16 [6144, 2048], P(('fsdp', 'replica')), may hold values from -6 to 6
- w_qkv: bfloat16 [2048, 4096], P('fsdp'), may hold values from -0.125 to 0.125
- w_out: bfloat16 [2048, 2048], P('fsdp'), may hold values from -0.375 to 0.375
- w_gate: bfloat16 [2048, 6144], P('fsdp'), may hold values from -0.125 to 0.125
- w_up: bfloat16 [2048, 6144], P('fsdp'), may hold values from -0.125 to 0.125
- w_down_t: bfloat16 [2048, 6144], P('fsdp'), may hold values from -0.078125 to 0.078125
- gain_attn: float32 [2048], replicated, may hold values from 0.5 to 1.5
- gain_mlp: float32 [2048], replicated, may hold values from 0.5 to 1.5
- gain_query: float32 [128], replicated, may hold values from 0.25 to 1.75
- gain_key: float32 [128], replicated, may hold values from 0.25 to 1.75
- dealt_lens: int32 [8, 4, 4], P('fsdp'), may hold values from 1 to 96, 192 in all within a row
- seq_order: int32 [8, 16], P('fsdp'), may hold values from 0 to 15, each once within a row
Outputs:
- output: bfloat16 [6144, 2048], P(('fsdp', 'replica'))
- input_grad: bfloat16 [6144, 2048], P(('fsdp', 'replica'))
- grad_qkv: float32 [2048, 4096], P('fsdp')
- grad_out: float32 [2048, 2048], P('fsdp')
- grad_gate: float32 [2048, 6144], P('fsdp')
- grad_up: float32 [2048, 6144], P('fsdp')
- grad_down_t: float32 [2048, 6144], P('fsdp')
- grad_gain_attn: float32 [2048], replicated
- grad_gain_mlp: float32 [2048], replicated
- grad_gain_query: float32 [128], replicated
- grad_gain_key: float32 [128], replicated
The draws below stay inside these ranges and needn't reach their ends.
Inputs may be any that keep to these rules, and one draw needn't show every extreme that they name: Each row dealt_lens[f, r, :] sums to 192: the sequences that device r of group f receives, in its order. The longest sequence of every device has exactly 96 tokens. Each row seq_order[f, :] is a permutation; entry r * 4 + s is the place in the group's initial order of device r's s-th sequence.
All inputs are finite; a program needn't handle non-finite values.
Results may differ from the reference program's by a relative error of at most 0.02.
Values may be sent and summed in bfloat16 or wider, within the bound.
A program may use at most 640 MiB of HBM per device.

```python
import math
import jax
import jax.numpy as jnp
import numpy as np
from jax import lax

D = 2048
QUERY_HEADS = 16
KEY_VALUE_HEADS = 8
HEAD_WIDTH = 128
FF = 6144
DEVICE_TOKENS = 192
SEQ_DEV = 4
LMAX = 96
SEQ_GROUP = 16
QKV = 4096
TOKENS = 6144
N_FSDP = 8
N_REPLICA = 4


def levels(rng, extent, split, smallest, largest):
    level, own = 1.0, jax.random.fold_in(rng, 6)
    for dim, parts in split:
        heights = jnp.exp(jax.random.uniform(jax.random.fold_in(own, dim), (parts,), jnp.float32, smallest / len(split), largest / len(split)))
        level = level * jnp.repeat(heights, extent[dim] // parts).reshape([-1 if axis == dim else 1 for axis in range(len(extent))])
    return level


def split_up(count, total, most, lean):
    weights = [(1 << 20) // math.isqrt(standing ** lean) + 1 for standing in range(2, count + 1)]
    spare, holding = total - most - (count - 1), [1] * (count - 1)
    while spare > 0:
        free = [i for i in range(count - 1) if holding[i] < most]
        whole, left = sum([weights[i] for i in free]), spare
        for i in free:
            addition = min(most - holding[i], max(1, left * weights[i] // whole), spare)
            holding[i] = holding[i] + addition
            spare = spare - addition
    return np.array([most] + holding)


def uneven(key, number_of, total, limit, slope):
    if number_of == 2:
        one = jax.random.randint(key, (), max(1, total - limit), min(limit, total - 1) + 1)
        return jnp.stack([one, total - one])
    sizes = jnp.asarray(split_up(number_of, total, limit, slope), jnp.int32)
    pairs = (number_of - 1) // 2
    source_of, taker = sizes[1:1 + 2 * pairs:2], sizes[2:2 + 2 * pairs:2]
    room = jnp.minimum(source_of - 1, limit - taker)
    moved = jax.random.randint(jax.random.fold_in(key, 1), (pairs,), 0, 1 << 20) % (room + 1)
    sizes = sizes.at[1:1 + 2 * pairs:2].set(source_of - moved).at[2:2 + 2 * pairs:2].set(taker + moved)
    return sizes[jax.random.permutation(jax.random.fold_in(key, 2), number_of)]


def noise(own_key, dims, deviation, reach, cuts=(), kind=jnp.bfloat16):
    gain = levels(own_key, dims, cuts, -0.22, 0.18) if cuts else 1.0
    values = jax.random.normal(own_key, dims, jnp.float32) * deviation * gain
    return jnp.minimum(jnp.maximum(values, -reach), reach).astype(kind)


def setup_inputs(seed: int = 0) -> dict:
    keys = jax.random.split(jax.random.key(seed), 14)
    return {
        "tokens": noise(keys[0], (TOKENS, D), 1.0, 6.0, ((0, 32),)),
        "cotangent": noise(keys[1], (TOKENS, D), 1.0, 6.0, ((0, 32),)),
        "w_qkv": noise(keys[2], (D, QKV), D ** -0.5, 0.125, ((0, 8),)),
        "w_out": noise(keys[3], (QUERY_HEADS * HEAD_WIDTH, D), (QUERY_HEADS * HEAD_WIDTH // 8) ** -0.5, 0.375, ((0, 8),)),
        "w_gate": noise(keys[4], (D, FF), D ** -0.5, 0.125, ((0, 8),)),
        "w_up": noise(keys[5], (D, FF), D ** -0.5, 0.125, ((0, 8),)),
        "w_down_t": noise(keys[6], (D, FF), FF ** -0.5, 0.078125, ((0, 8),)),
        "gain_attn": jnp.clip(1.0 + 0.1 * jax.random.normal(keys[7], (D,), jnp.float32), 0.5, 1.5),
        "gain_mlp": jnp.clip(1.0 + 0.1 * jax.random.normal(keys[8], (D,), jnp.float32), 0.5, 1.5),
        "gain_query": jnp.clip(1.0 + 0.15 * jax.random.normal(keys[9], (HEAD_WIDTH,), jnp.float32), 0.25, 1.75),
        "gain_key": jnp.clip(1.0 + 0.15 * jax.random.normal(keys[10], (HEAD_WIDTH,), jnp.float32), 0.25, 1.75),
        "dealt_lens": jax.vmap(lambda own: uneven(own, SEQ_DEV, DEVICE_TOKENS, LMAX, 2))(jax.random.split(keys[11], N_FSDP * N_REPLICA)).reshape((N_FSDP, N_REPLICA, SEQ_DEV)).astype(jnp.int32),
        "seq_order": jax.vmap(lambda own: jax.random.permutation(own, SEQ_GROUP))(jax.random.split(keys[12], N_FSDP)).reshape((N_FSDP, SEQ_GROUP)).astype(jnp.int32),
    }


EPSILON = 1e-06
ROPE_BASE = 1000000.0
NEG_FILL = -1e+30

@jax.custom_vjp
def low(v):
    return lax.optimization_barrier(v.astype(jnp.bfloat16)).astype(jnp.float32)

@jax.custom_vjp
def low_back(v):
    return v

def low_keep(v):
    return (low(v), None)

def low_pass(kept, grad):
    return (grad,)

def back_keep(v):
    return (v, None)

def back_low(kept, grad):
    return (low(grad),)
low.defvjp(low_keep, low_pass)
low_back.defvjp(back_keep, back_low)

def matmul(left, right):
    return jnp.dot(left, right, precision=lax.Precision.HIGHEST)

def rope_tables(positions, head_size):
    half_size = head_size // 2
    steps_up = jnp.arange(half_size, dtype=jnp.float32)
    inverse = ROPE_BASE ** (-(2.0 * steps_up) / head_size)
    angles = positions.astype(jnp.float32)[:, None] * inverse[None, :]
    return (jnp.cos(angles)[:, None, :], jnp.sin(angles)[:, None, :])

def rotate(values, cosine, sine):
    half_size = values.shape[-1] // 2
    first = values[..., :half_size]
    second = values[..., half_size:]
    return jnp.concatenate([first * cosine - second * sine, second * cosine + first * sine], axis=-1)

def dealt_index(own_lens, own_starts, token_count):
    local_end = jnp.cumsum(own_lens).astype(jnp.int32)
    local_start = (local_end - own_lens).astype(jnp.int32)
    row_index = jnp.arange(token_count, dtype=jnp.int32)
    segment_index = lax.optimization_barrier(jnp.sum((row_index[:, None] >= local_end[None, :]).astype(jnp.int32), axis=1)).astype(jnp.int32)
    one_hot = (segment_index[:, None] == jnp.arange(own_lens.shape[0], dtype=jnp.int32)[None, :]).astype(jnp.int32)
    positions = (row_index - lax.optimization_barrier(jnp.sum(one_hot * local_start[None, :], axis=1))).astype(jnp.int32)
    source = (lax.optimization_barrier(jnp.sum(one_hot * own_starts[None, :], axis=1)) + positions).astype(jnp.int32)
    return (segment_index, positions, source)

def group_starts(flat_lens, ranks):
    earlier = (ranks[:, None] < ranks[None, :]).astype(jnp.int32)
    return lax.optimization_barrier(jnp.sum(flat_lens[:, None] * earlier, axis=0)).astype(jnp.int32)

def attend_packed(pieces):
    query_rows, keys_all, values_all, segment_index = pieces
    item_count = query_rows.shape[0]
    grouped_rows = query_rows.reshape(item_count, KEY_VALUE_HEADS, QUERY_HEADS // KEY_VALUE_HEADS, HEAD_WIDTH)
    scores = jnp.einsum('qkgd,tkd->kgqt', grouped_rows, keys_all, precision=lax.Precision.HIGHEST) * HEAD_WIDTH ** (-0.5)
    scores = low_back(scores)
    row_index = jnp.arange(item_count, dtype=jnp.int32)
    key_mask = (segment_index[:, None] == segment_index[None, :]) & (row_index[None, :] <= row_index[:, None])
    scores = jnp.where(key_mask, scores, NEG_FILL)
    row_top = lax.optimization_barrier(jnp.max(scores, axis=3, keepdims=True))
    exp_terms = jnp.exp(scores - row_top)
    probs = low(exp_terms / lax.optimization_barrier(jnp.sum(exp_terms, axis=3, keepdims=True)))
    context_rows = jnp.einsum('kgqt,tkd->qkgd', probs, values_all, precision=lax.Precision.HIGHEST)
    return context_rows.reshape(item_count, QUERY_HEADS * HEAD_WIDTH)

def forward(inputs, wqkv, wout, wgate, wup, wdown, gain_one, gain_two, gain_q, gain_k, segment_index, positions):
    token_rows = inputs.shape[0]
    rms_one = lax.rsqrt(lax.optimization_barrier(jnp.mean(inputs * inputs, axis=1, keepdims=True)) + EPSILON)
    normed_one = low(inputs * rms_one * gain_one)
    projected_rows = low_back(matmul(normed_one, wqkv))
    query_width = QUERY_HEADS * HEAD_WIDTH
    key_width = KEY_VALUE_HEADS * HEAD_WIDTH
    query_rows = projected_rows[:, :query_width].reshape(token_rows, QUERY_HEADS, HEAD_WIDTH)
    key_rows_unnormed = projected_rows[:, query_width:query_width + key_width].reshape(token_rows, KEY_VALUE_HEADS, HEAD_WIDTH)
    value_rows_unnormed = projected_rows[:, query_width + key_width:].reshape(token_rows, KEY_VALUE_HEADS, HEAD_WIDTH)
    q_hat = query_rows * lax.rsqrt(lax.optimization_barrier(jnp.mean(query_rows * query_rows, axis=2, keepdims=True)) + EPSILON)
    k_hat = key_rows_unnormed * lax.rsqrt(lax.optimization_barrier(jnp.mean(key_rows_unnormed * key_rows_unnormed, axis=2, keepdims=True)) + EPSILON)
    cosine, sine = rope_tables(positions, HEAD_WIDTH)
    query_reduced = low(rotate(q_hat * gain_q, cosine, sine))
    key_reduced = low(rotate(k_hat * gain_k, cosine, sine))
    value_reduced = low(value_rows_unnormed)
    block_list = token_rows // DEVICE_TOKENS
    context_rows = lax.map(jax.checkpoint(attend_packed), (query_reduced.reshape(block_list, DEVICE_TOKENS, QUERY_HEADS, HEAD_WIDTH), key_reduced.reshape(block_list, DEVICE_TOKENS, KEY_VALUE_HEADS, HEAD_WIDTH), value_reduced.reshape(block_list, DEVICE_TOKENS, KEY_VALUE_HEADS, HEAD_WIDTH), segment_index.reshape(block_list, DEVICE_TOKENS)))
    context_rows = low_back(low(context_rows.reshape(token_rows, QUERY_HEADS * HEAD_WIDTH)))
    attn_out = low_back(matmul(context_rows, wout))
    resid = inputs + attn_out
    rms_two = lax.rsqrt(lax.optimization_barrier(jnp.mean(resid * resid, axis=1, keepdims=True)) + EPSILON)
    normed_two = low(resid * rms_two * gain_two)
    gate_proj = low_back(matmul(normed_two, wgate))
    up_proj = low_back(matmul(normed_two, wup))
    activated = low(jax.nn.silu(gate_proj) * up_proj)
    mlp_out = low_back(matmul(activated, wdown.T))
    return resid + mlp_out

def reference(tokens, cotangent, w_qkv, w_out, w_gate, w_up, w_down_t, gain_attn, gain_mlp, gain_query, gain_key, dealt_lens, seq_order):
    groups = dealt_lens.shape[0]
    replicas = dealt_lens.shape[1]
    per_dev = dealt_lens.shape[2]

    def one_group(lens_group, order_group):
        starts = group_starts(lens_group.reshape(-1), order_group)
        return jax.vmap(lambda own_lens, own_starts: dealt_index(own_lens, own_starts, DEVICE_TOKENS))(lens_group, starts.reshape(replicas, per_dev))
    segment_index, positions, source = jax.vmap(one_group)(dealt_lens, seq_order)
    offsets = (jnp.arange(groups, dtype=jnp.int32) * (replicas * DEVICE_TOKENS))[:, None, None]
    index = (source + offsets).reshape(-1).astype(jnp.int32)
    segment_index = segment_index.reshape(-1)
    positions = positions.reshape(-1)
    inputs = tokens.astype(jnp.float32)[index]
    grad_rows = cotangent.astype(jnp.float32)[index]

    def forward_fn(inputs, wqkv, wout, wgate, wup, wdown, gain_one, gain_two, gain_q, gain_k):
        return forward(inputs, wqkv, wout, wgate, wup, wdown, gain_one, gain_two, gain_q, gain_k, segment_index, positions)
    result, pull = jax.vjp(forward_fn, inputs, w_qkv.astype(jnp.float32), w_out.astype(jnp.float32), w_gate.astype(jnp.float32), w_up.astype(jnp.float32), w_down_t.astype(jnp.float32), gain_attn, gain_mlp, gain_query, gain_key)
    grads = pull(grad_rows)
    blank = jnp.zeros(tokens.shape, jnp.float32)
    output = blank.at[index].set(result).astype(jnp.bfloat16)
    input_grad = blank.at[index].set(grads[0]).astype(jnp.bfloat16)
    return (output, input_grad, grads[1], grads[2], grads[3], grads[4], grads[5], grads[6], grads[7], grads[8], grads[9])
```

```python
import jax
import jax.numpy as jnp
from jax import lax
from jax.sharding import PartitionSpec as P

QUERY_HEADS = 16
KEY_VALUE_HEADS = 8
HEAD_WIDTH = 128
LMAX = 96

EPSILON = 1e-06
ROPE_BASE = 1000000.0
NEG_FILL = -1e30
BF = jnp.bfloat16
F32 = jnp.float32


def dot(left, right):
    return jnp.dot(left, right, preferred_element_type=F32)


def dot_rows(left, right):
    return lax.dot_general(left, right, (((0,), (0,)), ((), ())), preferred_element_type=F32)


def dot_cols(left, right):
    return lax.dot_general(left, right, (((1,), (1,)), ((), ())), preferred_element_type=F32)


def rope_tables(positions):
    half_size = HEAD_WIDTH // 2
    steps_up = jnp.arange(half_size, dtype=F32)
    inverse = ROPE_BASE ** (-(2.0 * steps_up) / HEAD_WIDTH)
    angles = positions.astype(F32)[:, None] * inverse[None, :]
    return jnp.cos(angles), jnp.sin(angles)


def rotate(values, cosine, sine):
    half_size = HEAD_WIDTH // 2
    first, second = values[..., :half_size], values[..., half_size:]
    return jnp.concatenate([first * cosine - second * sine, second * cosine + first * sine], axis=-1)


def norm_back(d_normed, normed, rms):
    return rms * (d_normed - normed * jnp.mean(d_normed * normed, axis=-1, keepdims=True))


def row_positions(flat_lens, ranks, first_row, count):
    earlier = (ranks[:, None] < ranks[None, :]).astype(jnp.int32)
    starts = jnp.sum(flat_lens[:, None] * earlier, axis=0)
    rows = first_row + jnp.arange(count, dtype=jnp.int32)
    begun = jnp.where(starts[None, :] <= rows[:, None], starts[None, :], 0)
    return rows - jnp.max(begun, axis=1)


def per_device(
    n_replica, tokens, cotangent, w_qkv, w_out, w_gate, w_up, w_down_t,
    gain_attn, gain_mlp, gain_query, gain_key, dealt_lens, seq_order,
):
    rows, width = tokens.shape
    n_fsdp = width // w_qkv.shape[0]
    q_w = QUERY_HEADS * HEAD_WIDTH
    k_w = KEY_VALUE_HEADS * HEAD_WIDTH
    replica = lax.axis_index("replica")
    shared = n_fsdp // KEY_VALUE_HEADS
    heads = QUERY_HEADS // n_fsdp
    qw = heads * HEAD_WIDTH

    pos = row_positions(dealt_lens[0].reshape(-1), seq_order[0], replica * rows, rows)
    pos_all = lax.all_gather(pos, "fsdp", axis=0, tiled=True)

    def scatter_cols(w):
        return lax.all_to_all(w, "fsdp", split_axis=1, concat_axis=0, tiled=True)

    depth = w_qkv.shape[0]
    wq = w_qkv[:, :q_w].reshape(depth, n_fsdp, qw)
    wk = jnp.repeat(w_qkv[:, q_w:q_w + k_w].reshape(depth, KEY_VALUE_HEADS, HEAD_WIDTH), shared, axis=1)
    wv = jnp.repeat(w_qkv[:, q_w + k_w:].reshape(depth, KEY_VALUE_HEADS, HEAD_WIDTH), shared, axis=1)
    w_qkv_c = scatter_cols(jnp.concatenate([wq, wk, wv], axis=2).reshape(depth, -1))
    gate_c, up_c, down_c = scatter_cols(w_gate), scatter_cols(w_up), scatter_cols(w_down_t)

    def gather(a):
        return lax.all_gather(a, "fsdp", axis=0, tiled=True)

    def scatter_sum(a):
        return lax.psum_scatter(a.astype(BF), "fsdp", scatter_dimension=0, tiled=True).astype(F32)

    x = tokens.astype(F32)
    g = cotangent.astype(F32)
    r1 = lax.rsqrt(jnp.mean(x * x, axis=1, keepdims=True) + EPSILON)
    u1 = x * r1
    n1 = gather((u1 * gain_attn).astype(BF))
    g_all = gather(cotangent)
    total = n1.shape[0]

    proj = dot(n1, w_qkv_c)
    q_rows = proj[:, :qw].reshape(total, heads, HEAD_WIDTH)
    k_rows = proj[:, qw:qw + HEAD_WIDTH]
    v_low = proj[:, qw + HEAD_WIDTH:].astype(BF)
    rq = lax.rsqrt(jnp.mean(q_rows * q_rows, axis=2, keepdims=True) + EPSILON)
    q_hat = q_rows * rq
    rk = lax.rsqrt(jnp.mean(k_rows * k_rows, axis=1, keepdims=True) + EPSILON)
    k_hat = k_rows * rk
    cosine, sine = rope_tables(pos_all)
    q_low = rotate(q_hat * gain_query, cosine[:, None], sine[:, None]).astype(BF)
    k_low = rotate(k_hat * gain_key, cosine, sine).astype(BF)

    groups = n_fsdp
    halo = LMAX
    kv = jnp.concatenate([k_low, v_low], axis=1).reshape(groups, rows, 2 * HEAD_WIDTH)
    up_pairs = [(i, i + 1) for i in range(n_replica - 1)]
    down_pairs = [(i + 1, i) for i in range(n_replica - 1)]
    kv_before = lax.ppermute(kv[:, rows - halo:], "replica", up_pairs)
    kv_window = jnp.concatenate([kv_before, kv], axis=1)
    k_win, v_win = kv_window[..., :HEAD_WIDTH], kv_window[..., HEAD_WIDTH:]
    q_grp = q_low.reshape(groups, rows, heads, HEAD_WIDTH)
    pos_grp = pos_all.reshape(groups, rows)
    i_at = halo + jnp.arange(rows, dtype=jnp.int32)
    j_at = jnp.arange(halo + rows, dtype=jnp.int32)
    mask = (j_at[None, None, :] <= i_at[None, :, None]) & (
        j_at[None, None, :] >= i_at[None, :, None] - pos_grp[:, :, None])
    mask = mask[:, None]
    scale = HEAD_WIDTH ** (-0.5)
    scores = jnp.einsum("gqhd,gkd->ghqk", q_grp, k_win, preferred_element_type=F32) * scale
    scores = jnp.where(mask, scores, NEG_FILL)
    top = jnp.max(scores, axis=3, keepdims=True)
    terms = jnp.exp(scores - top)
    probs = terms / jnp.sum(terms, axis=3, keepdims=True)
    probs_low = probs.astype(BF)
    ctx = jnp.einsum("ghqk,gkd->gqhd", probs_low, v_win, preferred_element_type=F32)
    ctx_low = ctx.reshape(total, qw).astype(BF)
    h = x + scatter_sum(dot(ctx_low, w_out))

    r2 = lax.rsqrt(jnp.mean(h * h, axis=1, keepdims=True) + EPSILON)
    u2 = h * r2
    n2 = gather((u2 * gain_mlp).astype(BF))
    gate = dot(n2, gate_c)
    up = dot(n2, up_c)
    sg = jax.nn.sigmoid(gate)
    silu = gate * sg
    act = (silu * up).astype(BF)
    output = (h + scatter_sum(dot_cols(act, down_c))).astype(BF)

    d_act = dot(g_all, down_c)
    d_gate = (d_act * up * sg * (1.0 + gate * (1.0 - sg))).astype(BF)
    d_up = (d_act * silu).astype(BF)

    d_n2 = scatter_sum(dot_cols(d_gate, gate_c) + dot_cols(d_up, up_c))
    d_gain_mlp = jnp.sum(d_n2 * u2, axis=0)
    d_h = g + norm_back(d_n2 * gain_mlp, u2, r2)
    dh_all = gather(d_h.astype(BF))
    d_ctx = dot_cols(dh_all, w_out).astype(BF).reshape(groups, rows, heads, HEAD_WIDTH)
    d_v = jnp.einsum("ghqk,gqhd->gkd", probs_low, d_ctx, preferred_element_type=F32)
    d_p = jnp.einsum("gqhd,gkd->ghqk", d_ctx, v_win, preferred_element_type=F32)
    delta = jnp.sum(probs * d_p, axis=3, keepdims=True)
    d_s = (probs * (d_p - delta)).astype(BF)
    d_q = jnp.einsum("ghqk,gkd->gqhd", d_s, k_win, preferred_element_type=F32) * scale
    d_k = jnp.einsum("ghqk,gqhd->gkd", d_s, q_grp, preferred_element_type=F32) * scale
    d_kv = jnp.concatenate([d_k, d_v], axis=2)
    d_kv_after = lax.ppermute(d_kv[:, :halo].astype(BF), "replica", down_pairs).astype(F32)
    d_kv = d_kv[:, halo:]
    d_kv = jnp.concatenate([d_kv[:, :rows - halo], d_kv[:, rows - halo:] + d_kv_after], axis=1)
    d_k = d_kv[..., :HEAD_WIDTH].reshape(total, HEAD_WIDTH)
    d_v = d_kv[..., HEAD_WIDTH:].reshape(total, HEAD_WIDTH)
    d_q = d_q.reshape(total, heads, HEAD_WIDTH)
    dq_g = rotate(d_q, cosine[:, None], -sine[:, None])
    dk_g = rotate(d_k, cosine, -sine)
    d_gain_query = jnp.sum(dq_g * q_hat, axis=(0, 1))
    d_gain_key = jnp.sum(dk_g * k_hat, axis=0)
    dq = norm_back(dq_g * gain_query, q_hat, rq)
    dk = norm_back(dk_g * gain_key, k_hat, rk)
    d_proj = jnp.concatenate([dq.reshape(total, qw), dk, d_v], axis=1).astype(BF)
    d_n1 = scatter_sum(dot_cols(d_proj, w_qkv_c))
    d_gain_attn = jnp.sum(d_n1 * u1, axis=0)
    input_grad = (d_h + norm_back(d_n1 * gain_attn, u1, r1)).astype(BF)

    def reduce_cols(grad):
        share = grad.shape[1]
        low = grad.astype(BF).reshape(n_fsdp, n_replica, width // n_fsdp // n_replica, share)
        low = low.transpose(1, 0, 2, 3).reshape(width, share)
        part = lax.psum_scatter(low, "replica", scatter_dimension=0, tiled=True)
        part = lax.all_to_all(part.reshape(n_fsdp, -1, share), "fsdp", split_axis=0, concat_axis=1)
        whole = lax.all_gather(part, "replica", axis=0, tiled=True)
        return whole.astype(F32)

    def reduce_rows(grad):
        low = lax.psum_scatter(grad.astype(BF), "replica", scatter_dimension=0, tiled=True)
        return lax.all_gather(low, "replica", axis=0, tiled=True).astype(F32)

    g_down = reduce_cols(dot_rows(g_all, act)).reshape(depth, -1)
    g_gate = reduce_cols(dot_rows(n2, d_gate)).reshape(depth, -1)
    g_up = reduce_cols(dot_rows(n2, d_up)).reshape(depth, -1)
    g_out = reduce_rows(dot_rows(ctx_low, dh_all))
    g_qkv = reduce_cols(dot_rows(n1, d_proj))

    def of_key_heads(part):
        return jnp.sum(part.reshape(depth, KEY_VALUE_HEADS, shared, HEAD_WIDTH), axis=2).reshape(depth, k_w)

    g_qkv = jnp.concatenate([
        g_qkv[:, :, :qw].reshape(depth, q_w),
        of_key_heads(g_qkv[:, :, qw:qw + HEAD_WIDTH]),
        of_key_heads(g_qkv[:, :, qw + HEAD_WIDTH:])], axis=1)
    sums = lax.psum((d_gain_attn, d_gain_mlp, d_gain_query, d_gain_key), ("fsdp", "replica"))
    return (output, input_grad, g_qkv, g_out, g_gate, g_up, g_down) + tuple(sums)


def solution(mesh):
    n_replica = mesh.shape["replica"]

    def program(*args):
        return per_device(n_replica, *args)

    rows = P(("fsdp", "replica"), None)
    weight = P("fsdp", None)
    return jax.shard_map(
        program,
        mesh=mesh,
        in_specs=(rows, rows) + (weight,) * 5 + (P(),) * 4 + (P("fsdp", None, None), P("fsdp", None)),
        out_specs=(rows, rows) + (weight,) * 5 + (P(),) * 4,
        check_vma=False,
    )
```

```python
import functools

import jax
import jax.numpy as jnp
from jax import lax
from jax.experimental import pallas as pl
from jax.experimental.pallas import tpu as pltpu
from jax.sharding import PartitionSpec as P

QUERY_HEADS = 16
KEY_VALUE_HEADS = 8
HEAD_WIDTH = 128
LMAX = 96

EPSILON = 1e-06
ROPE_BASE = 1000000.0
NEG_FILL = -1e30
BF = jnp.bfloat16
F32 = jnp.float32


MESH = pl.DeviceIdType.MESH
ANY = pl.BlockSpec(memory_space=pl.ANY)
VMEM = pl.BlockSpec(memory_space=pltpu.VMEM)
DMA = pltpu.SemaphoreType.DMA
STRIP = 16
LAG = 3


class Place:
    def __init__(self, n, n_z):
        self.n, self.chips, self.n_z = n, n // 2, n_z
        self.f = lax.axis_index("fsdp")
        self.chip, self.core = self.f // 2, lax.rem(self.f, 2)
        self.sib = self.f + 1 - 2 * self.core
        self.z = lax.axis_index("replica")
        low = (self.z < n_z // 2).astype(jnp.int32)
        self.inner = self.z - 1 + 2 * low
        self.outer = self.z + 1 - 2 * low
        self.mid = (self.z == n_z // 2 - 1) | (self.z == n_z // 2)
        self.has_outer = (self.z > 0) & (self.z < n_z - 1)

    def to(self, k):
        return lax.rem(self.f + k, self.n)

    def chip_at(self, k):
        return lax.rem(self.chip + k, self.chips)

    def greet(self, line):
        barrier = pltpu.get_barrier_semaphore()
        for k in range(1, self.n):
            pl.semaphore_signal(barrier, inc=1, device_id={"fsdp": self.to(k)}, device_id_type=MESH)
        if line:
            pl.semaphore_signal(barrier, inc=1, device_id={"replica": self.inner}, device_id_type=MESH)

            @pl.when(self.has_outer)
            def _():
                pl.semaphore_signal(barrier, inc=1, device_id={"replica": self.outer}, device_id_type=MESH)
                pl.semaphore_wait(barrier, 1)

        pl.semaphore_wait(barrier, self.n - 1 + int(line))


def remote(src, dst, send, recv, axis, index):
    return pltpu.make_async_remote_copy(
        src_ref=src, dst_ref=dst, send_sem=send, recv_sem=recv, device_id={axis: index}, device_id_type=MESH)


def strips(rows, body):
    def step(i, carry):
        body(pl.ds(pl.multiple_of(i * STRIP, STRIP), STRIP))
        return carry

    lax.fori_loop(0, rows // STRIP, step, 0)


class Exchange:
    def __init__(self, at, pieces, send, recv):
        self.copies, self.local = [], []
        for i, (src, dst) in enumerate(pieces):
            self.local.append(pltpu.make_async_copy(src(at.f), dst(at.f), recv.at[i, 0]))
            for k in range(1, at.n):
                self.copies.append(remote(src(at.to(k)), dst(at.f), send.at[i, k], recv.at[i, k], "fsdp", at.to(k)))

    def start(self):
        for c in self.copies + self.local:
            c.start()

    def wait(self):
        for c in self.copies + self.local:
            c.wait()


class Gather:
    def __init__(self, at, own, whole, sem):
        rows = own.shape[0]

        def block(i):
            return whole.at[pl.ds(pl.multiple_of(i * rows, rows), rows)]

        self.local = pltpu.make_async_copy(own, block(at.f), sem.at[0, 0])
        self.across = [remote(own, block(at.f), sem.at[0, 1], sem.at[1, 0], "fsdp", at.sib)]
        self.far, self.on = [], []
        for k in range(1, at.chips):
            to = 2 * at.chip_at(k) + at.core
            self.far.append(remote(own, block(at.f), sem.at[2, k], sem.at[3, k], "fsdp", to))
            came = 2 * at.chip_at(at.chips - k) + at.core
            self.on.append(remote(block(came), block(came), sem.at[4, k], sem.at[5, k], "fsdp", at.sib))

    def start(self):
        for c in self.far + self.across + [self.local]:
            c.start()

    def forward(self):
        for far, on in zip(self.far, self.on):
            far.wait_recv()
            on.start()

    def wait(self):
        for c in self.far:
            c.wait_send()
        for c in self.across + self.on + [self.local]:
            c.wait()


class ScatterSum:
    def __init__(self, at, part, near, own, far, sem):
        self.at, self.near, self.own, self.far = at, near, own, far
        rows = own.shape[1]
        self.rows = rows

        def block(i):
            return part.at[pl.ds(pl.multiple_of(i * rows, rows), rows)]

        self.across, self.load, self.send = [], [], []
        for k in range(at.chips):
            q = at.chip_at(k)
            self.across.append(remote(block(2 * q + 1 - at.core), near.at[k], sem.at[0, k], sem.at[1, k], "fsdp", at.sib))
            self.load.append(pltpu.make_async_copy(block(2 * q + at.core), own.at[k], sem.at[2, k]))
            if k:
                self.send.append(
                    remote(own.at[k], far.at[k - 1], sem.at[3, k], sem.at[4, k], "fsdp", 2 * q + at.core))

    def start(self):
        for k in list(range(1, self.at.chips)) + [0]:
            self.across[k].start()
            self.load[k].start()

    def forward(self):
        for k in list(range(1, self.at.chips)) + [0]:
            self.across[k].wait()
            self.load[k].wait()

            def add(at, k=k):
                self.own[k, at] = (self.own[k, at].astype(F32) + self.near[k, at].astype(F32)).astype(BF)

            strips(self.rows, add)
            if k:
                self.send[k - 1].start()

    def wait(self):
        for c in self.send:
            c.wait()

    def total(self, at):
        out = self.own[0, at].astype(F32)
        for k in range(self.at.chips - 1):
            out += self.far[k, at].astype(F32)
        return out


class LineSum:
    def __init__(self, at, chunk, came, arrive, send, recv, out, out_sem):
        self.at, self.chunk, self.came, self.arrive = at, chunk, came, arrive
        self.send, self.recv, self.out, self.out_sem = send, recv, out, out_sem
        self.count = chunk.shape[0]
        self.kind = at.mid.astype(jnp.int32)

    def inward(self, j):
        return remote(self.chunk.at[j], self.came.at[self.kind, j], self.send.at[0, j], self.recv.at[self.kind, j],
                      "replica", self.at.inner)

    def outward(self, j, src):
        return remote(src, self.came.at[1, j], self.send.at[1, j], self.recv.at[1, j], "replica", self.at.outer)

    def here(self, kind, j):
        return pltpu.make_async_copy(self.came.at[kind, j], self.came.at[kind, j], self.recv.at[kind, j])

    def up(self, j):
        pltpu.make_async_copy(self.chunk.at[j], self.chunk.at[j], self.arrive.at[j]).wait()

        @pl.when(self.at.has_outer)
        def _():
            self.here(0, j).wait()
            self.chunk[j] = (self.chunk[j].astype(F32) + self.came[0, j].astype(F32)).astype(BF)

        self.inward(j).start()

    def down(self, j):
        self.here(1, j).wait()

        @pl.when(self.at.mid)
        def _():
            self.came[1, j] = (self.chunk[j].astype(F32) + self.came[1, j].astype(F32)).astype(BF)

        @pl.when(self.at.has_outer)
        def _():
            self.outward(j, self.came.at[1, j]).start()

        pltpu.make_async_copy(self.came.at[1, j], self.out(j), self.out_sem.at[j]).start()

    def settle(self):
        def step(j, carry):
            self.inward(j).wait_send()

            @pl.when(self.at.has_outer)
            def _():
                self.outward(j, self.came.at[1, j]).wait_send()

            pltpu.make_async_copy(self.came.at[1, j], self.out(j), self.out_sem.at[j]).wait()
            return carry

        lax.fori_loop(0, self.count, step, 0)


def run_line(line, first, last):
    lag = min(LAG, last - first)

    def head(j, carry):
        line.up(j)
        return carry

    def body(j, carry):
        line.up(j)
        line.down(j - lag)
        return carry

    def tail(j, carry):
        line.down(j)
        return carry

    lax.fori_loop(first, first + lag, head, 0)
    lax.fori_loop(first + lag, last, body, 0)
    lax.fori_loop(last - lag, last, tail, 0)


def rms_of(values):
    return lax.rsqrt(jnp.mean(values * values, axis=-1, keepdims=True) + EPSILON)


def qkv_pieces(at, w, wc, qw):
    q_w, k_w = QUERY_HEADS * HEAD_WIDTH, KEY_VALUE_HEADS * HEAD_WIDTH
    shared = at.n // KEY_VALUE_HEADS
    depth = w.shape[0]

    def cols(start, width):
        return pl.ds(pl.multiple_of(start, HEAD_WIDTH), width)

    def rows(s):
        return pl.ds(pl.multiple_of(s * depth, depth), depth)

    return [
        (lambda t: w.at[:, cols(t * qw, qw)], lambda s: wc.at[rows(s), pl.ds(0, qw)]),
        (lambda t: w.at[:, cols(q_w + t // shared * HEAD_WIDTH, HEAD_WIDTH)],
         lambda s: wc.at[rows(s), pl.ds(qw, HEAD_WIDTH)]),
        (lambda t: w.at[:, cols(q_w + k_w + t // shared * HEAD_WIDTH, HEAD_WIDTH)],
         lambda s: wc.at[rows(s), pl.ds(qw + HEAD_WIDTH, HEAD_WIDTH)]),
    ]


def col_piece(w, wc, share):
    depth = w.shape[0]
    return (lambda t: w.at[:, pl.ds(pl.multiple_of(t * share, HEAD_WIDTH), share)],
            lambda s: wc.at[pl.ds(pl.multiple_of(s * depth, depth), depth)])


def begin_kernel(n, n_z, x_ref, gain_ref, place_ref, wqkv_ref, n1_ref, wc_ref, places_ref,
                 own, s_x, r_x, s_g, s_p, r_p):
    at = Place(n, n_z)
    rows = x_ref.shape[0]
    at.greet(False)
    weights = Exchange(at, qkv_pieces(at, wqkv_ref, wc_ref, QUERY_HEADS * HEAD_WIDTH // n), s_x, r_x)
    place = Exchange(at, [(lambda t: place_ref, lambda s: places_ref.at[s])], s_p, r_p)
    place.start()
    weights.start()

    def norm(strip):
        x = x_ref[strip].astype(F32)
        own[strip] = (x * rms_of(x) * gain_ref[...]).astype(BF)

    strips(rows, norm)
    gather = Gather(at, own, n1_ref, s_g)
    gather.start()
    gather.forward()
    gather.wait()
    place.wait()
    weights.wait()


def middle_kernel(n, n_z, part_ref, x_ref, gain_ref, g_ref, gate_ref, up_ref, down_ref,
                  h_ref, n2_ref, gall_ref, gate_c, up_c, down_c,
                  near, mine, far, own, s_r, s_a, s_b, s_x, r_x, s_y, r_y):
    at = Place(n, n_z)
    share = gate_c.shape[1]
    at.greet(False)
    total = ScatterSum(at, part_ref, near, mine, far, s_r)
    total.start()
    total.forward()
    first = Exchange(at, [col_piece(gate_ref, gate_c, share), col_piece(up_ref, up_c, share)], s_x, r_x)
    second = Exchange(at, [col_piece(down_ref, down_c, share)], s_y, r_y)
    first.start()
    total.wait()

    def norm(strip):
        h = x_ref[strip].astype(F32) + total.total(strip)
        h_ref[strip] = h
        own[strip] = (h * rms_of(h) * gain_ref[...]).astype(BF)

    strips(x_ref.shape[0], norm)
    n2 = Gather(at, own, n2_ref, s_a)
    g_all = Gather(at, g_ref, gall_ref, s_b)
    n2.start()
    g_all.start()
    second.start()
    n2.forward()
    g_all.forward()
    n2.wait()
    g_all.wait()
    first.wait()
    second.wait()


def dot(left, right):
    return jnp.dot(left, right, preferred_element_type=F32)


def dot_rows(left, right):
    return lax.dot_general(left, right, (((0,), (0,)), ((), ())), preferred_element_type=F32)


def dot_cols(left, right):
    return lax.dot_general(left, right, (((1,), (1,)), ((), ())), preferred_element_type=F32)


def rope_tables(positions):
    half_size = HEAD_WIDTH // 2
    steps_up = jnp.arange(half_size, dtype=F32)
    inverse = ROPE_BASE ** (-(2.0 * steps_up) / HEAD_WIDTH)
    angles = positions.astype(F32)[:, None] * inverse[None, :]
    return jnp.cos(angles), jnp.sin(angles)


def rotate(values, cosine, sine):
    half_size = HEAD_WIDTH // 2
    first, second = values[..., :half_size], values[..., half_size:]
    return jnp.concatenate([first * cosine - second * sine, second * cosine + first * sine], axis=-1)


def norm_back(d_normed, normed, rms):
    return rms * (d_normed - normed * jnp.mean(d_normed * normed, axis=-1, keepdims=True))


def begin(n, n_z, x, gain, place, w_qkv):
    rows, width = x.shape
    total, wide = n * rows, (QUERY_HEADS // n + 2) * HEAD_WIDTH
    return pl.pallas_call(
        functools.partial(begin_kernel, n, n_z),
        out_shape=(
            jax.ShapeDtypeStruct((total, width), BF),
            jax.ShapeDtypeStruct((width, wide), BF),
            jax.ShapeDtypeStruct((n,) + place.shape, place.dtype),
        ),
        in_specs=[VMEM, VMEM, ANY, ANY],
        out_specs=(ANY, ANY, ANY),
        scratch_shapes=[
            pltpu.VMEM((rows, width), BF), DMA((3, n)), DMA((3, n)), DMA((6, n)), DMA((1, n)), DMA((1, n))],
        compiler_params=pltpu.CompilerParams(collective_id=0, has_side_effects=True, vmem_limit_bytes=32 << 20),
        name="begin",
    )(x, gain, place, w_qkv)


def middle(n, n_z, part, x, gain, g, gate, up, down):
    rows, width = x.shape
    total, share, chips = n * rows, gate.shape[1] // n, n // 2
    columns = jax.ShapeDtypeStruct((width, share), BF)
    return pl.pallas_call(
        functools.partial(middle_kernel, n, n_z),
        out_shape=(
            jax.ShapeDtypeStruct((rows, width), F32),
            jax.ShapeDtypeStruct((total, width), BF),
            jax.ShapeDtypeStruct((total, width), BF),
            columns, columns, columns,
        ),
        in_specs=[ANY, VMEM, VMEM, ANY, ANY, ANY, ANY],
        out_specs=(VMEM, ANY, ANY, ANY, ANY, ANY),
        scratch_shapes=[
            pltpu.VMEM((chips, rows, width), BF), pltpu.VMEM((chips, rows, width), BF),
            pltpu.VMEM((chips - 1, rows, width), BF), pltpu.VMEM((rows, width), BF),
            DMA((5, n)), DMA((6, n)), DMA((6, n)), DMA((2, n)), DMA((2, n)), DMA((1, n)), DMA((1, n))],
        compiler_params=pltpu.CompilerParams(collective_id=1, has_side_effects=True, vmem_limit_bytes=48 << 20),
        name="middle",
    )(part, x, gain, g, gate, up, down)


def row_positions(flat_lens, ranks, first_row, count):
    earlier = (ranks[:, None] < ranks[None, :]).astype(jnp.int32)
    starts = jnp.sum(flat_lens[:, None] * earlier, axis=0)
    rows = first_row + jnp.arange(count, dtype=jnp.int32)
    begun = jnp.where(starts[None, :] <= rows[:, None], starts[None, :], 0)
    return rows - jnp.max(begun, axis=1)


def per_device(
    n_replica, tokens, cotangent, w_qkv, w_out, w_gate, w_up, w_down_t,
    gain_attn, gain_mlp, gain_query, gain_key, dealt_lens, seq_order,
):
    rows, width = tokens.shape
    n_fsdp = width // w_qkv.shape[0]
    q_w = QUERY_HEADS * HEAD_WIDTH
    k_w = KEY_VALUE_HEADS * HEAD_WIDTH
    replica = lax.axis_index("replica")
    shared = n_fsdp // KEY_VALUE_HEADS
    heads = QUERY_HEADS // n_fsdp
    qw = heads * HEAD_WIDTH

    pos = row_positions(dealt_lens[0].reshape(-1), seq_order[0], replica * rows, rows)
    depth = w_qkv.shape[0]
    place = jnp.zeros((8, HEAD_WIDTH), jnp.int32).reshape(-1).at[:rows].set(pos).reshape(8, HEAD_WIDTH)
    n1, w_qkv_c, places = begin(n_fsdp, n_replica, tokens, gain_attn[None], place, w_qkv)
    pos_all = places.reshape(n_fsdp, -1)[:, :rows].reshape(-1)

    def gather(a):
        return lax.all_gather(a, "fsdp", axis=0, tiled=True)

    def scatter_sum(a):
        return lax.psum_scatter(a.astype(BF), "fsdp", scatter_dimension=0, tiled=True).astype(F32)

    x = tokens.astype(F32)
    g = cotangent.astype(F32)
    r1 = lax.rsqrt(jnp.mean(x * x, axis=1, keepdims=True) + EPSILON)
    u1 = x * r1
    total = n1.shape[0]

    proj = dot(n1, w_qkv_c)
    q_rows = proj[:, :qw].reshape(total, heads, HEAD_WIDTH)
    k_rows = proj[:, qw:qw + HEAD_WIDTH]
    v_low = proj[:, qw + HEAD_WIDTH:].astype(BF)
    rq = lax.rsqrt(jnp.mean(q_rows * q_rows, axis=2, keepdims=True) + EPSILON)
    q_hat = q_rows * rq
    rk = lax.rsqrt(jnp.mean(k_rows * k_rows, axis=1, keepdims=True) + EPSILON)
    k_hat = k_rows * rk
    cosine, sine = rope_tables(pos_all)
    q_low = rotate(q_hat * gain_query, cosine[:, None], sine[:, None]).astype(BF)
    k_low = rotate(k_hat * gain_key, cosine, sine).astype(BF)

    groups = n_fsdp
    halo = LMAX
    kv = jnp.concatenate([k_low, v_low], axis=1).reshape(groups, rows, 2 * HEAD_WIDTH)
    up_pairs = [(i, i + 1) for i in range(n_replica - 1)]
    down_pairs = [(i + 1, i) for i in range(n_replica - 1)]
    kv_before = lax.ppermute(kv[:, rows - halo:], "replica", up_pairs)
    kv_window = jnp.concatenate([kv_before, kv], axis=1)
    k_win, v_win = kv_window[..., :HEAD_WIDTH], kv_window[..., HEAD_WIDTH:]
    q_grp = q_low.reshape(groups, rows, heads, HEAD_WIDTH)
    pos_grp = pos_all.reshape(groups, rows)
    i_at = halo + jnp.arange(rows, dtype=jnp.int32)
    j_at = jnp.arange(halo + rows, dtype=jnp.int32)
    mask = (j_at[None, None, :] <= i_at[None, :, None]) & (
        j_at[None, None, :] >= i_at[None, :, None] - pos_grp[:, :, None])
    mask = mask[:, None]
    scale = HEAD_WIDTH ** (-0.5)
    scores = jnp.einsum("gqhd,gkd->ghqk", q_grp, k_win, preferred_element_type=F32) * scale
    scores = jnp.where(mask, scores, NEG_FILL)
    top = jnp.max(scores, axis=3, keepdims=True)
    terms = jnp.exp(scores - top)
    probs = terms / jnp.sum(terms, axis=3, keepdims=True)
    probs_low = probs.astype(BF)
    ctx = jnp.einsum("ghqk,gkd->gqhd", probs_low, v_win, preferred_element_type=F32)
    ctx_low = ctx.reshape(total, qw).astype(BF)
    h, n2, g_all, gate_c, up_c, down_c = middle(
        n_fsdp, n_replica, dot(ctx_low, w_out).astype(BF), tokens, gain_mlp[None], cotangent, w_gate, w_up, w_down_t)

    r2 = lax.rsqrt(jnp.mean(h * h, axis=1, keepdims=True) + EPSILON)
    u2 = h * r2
    gate = dot(n2, gate_c)
    up = dot(n2, up_c)
    sg = jax.nn.sigmoid(gate)
    silu = gate * sg
    act = (silu * up).astype(BF)
    output = (h + scatter_sum(dot_cols(act, down_c))).astype(BF)

    d_act = dot(g_all, down_c)
    d_gate = (d_act * up * sg * (1.0 + gate * (1.0 - sg))).astype(BF)
    d_up = (d_act * silu).astype(BF)

    d_n2 = scatter_sum(dot_cols(d_gate, gate_c) + dot_cols(d_up, up_c))
    d_gain_mlp = jnp.sum(d_n2 * u2, axis=0)
    d_h = g + norm_back(d_n2 * gain_mlp, u2, r2)
    dh_all = gather(d_h.astype(BF))
    d_ctx = dot_cols(dh_all, w_out).astype(BF).reshape(groups, rows, heads, HEAD_WIDTH)
    d_v = jnp.einsum("ghqk,gqhd->gkd", probs_low, d_ctx, preferred_element_type=F32)
    d_p = jnp.einsum("gqhd,gkd->ghqk", d_ctx, v_win, preferred_element_type=F32)
    delta = jnp.sum(probs * d_p, axis=3, keepdims=True)
    d_s = (probs * (d_p - delta)).astype(BF)
    d_q = jnp.einsum("ghqk,gkd->gqhd", d_s, k_win, preferred_element_type=F32) * scale
    d_k = jnp.einsum("ghqk,gqhd->gkd", d_s, q_grp, preferred_element_type=F32) * scale
    d_kv = jnp.concatenate([d_k, d_v], axis=2)
    d_kv_after = lax.ppermute(d_kv[:, :halo].astype(BF), "replica", down_pairs).astype(F32)
    d_kv = d_kv[:, halo:]
    d_kv = jnp.concatenate([d_kv[:, :rows - halo], d_kv[:, rows - halo:] + d_kv_after], axis=1)
    d_k = d_kv[..., :HEAD_WIDTH].reshape(total, HEAD_WIDTH)
    d_v = d_kv[..., HEAD_WIDTH:].reshape(total, HEAD_WIDTH)
    d_q = d_q.reshape(total, heads, HEAD_WIDTH)
    dq_g = rotate(d_q, cosine[:, None], -sine[:, None])
    dk_g = rotate(d_k, cosine, -sine)
    d_gain_query = jnp.sum(dq_g * q_hat, axis=(0, 1))
    d_gain_key = jnp.sum(dk_g * k_hat, axis=0)
    dq = norm_back(dq_g * gain_query, q_hat, rq)
    dk = norm_back(dk_g * gain_key, k_hat, rk)
    d_proj = jnp.concatenate([dq.reshape(total, qw), dk, d_v], axis=1).astype(BF)
    d_n1 = scatter_sum(dot_cols(d_proj, w_qkv_c))
    d_gain_attn = jnp.sum(d_n1 * u1, axis=0)
    input_grad = (d_h + norm_back(d_n1 * gain_attn, u1, r1)).astype(BF)

    def reduce_cols(grad):
        share = grad.shape[1]
        low = grad.astype(BF).reshape(n_fsdp, n_replica, width // n_fsdp // n_replica, share)
        low = low.transpose(1, 0, 2, 3).reshape(width, share)
        part = lax.psum_scatter(low, "replica", scatter_dimension=0, tiled=True)
        part = lax.all_to_all(part.reshape(n_fsdp, -1, share), "fsdp", split_axis=0, concat_axis=1)
        whole = lax.all_gather(part, "replica", axis=0, tiled=True)
        return whole.astype(F32)

    def reduce_rows(grad):
        low = lax.psum_scatter(grad.astype(BF), "replica", scatter_dimension=0, tiled=True)
        return lax.all_gather(low, "replica", axis=0, tiled=True).astype(F32)

    g_down = reduce_cols(dot_rows(g_all, act)).reshape(depth, -1)
    g_gate = reduce_cols(dot_rows(n2, d_gate)).reshape(depth, -1)
    g_up = reduce_cols(dot_rows(n2, d_up)).reshape(depth, -1)
    g_out = reduce_rows(dot_rows(ctx_low, dh_all))
    g_qkv = reduce_cols(dot_rows(n1, d_proj))

    def of_key_heads(part):
        return jnp.sum(part.reshape(depth, KEY_VALUE_HEADS, shared, HEAD_WIDTH), axis=2).reshape(depth, k_w)

    g_qkv = jnp.concatenate([
        g_qkv[:, :, :qw].reshape(depth, q_w),
        of_key_heads(g_qkv[:, :, qw:qw + HEAD_WIDTH]),
        of_key_heads(g_qkv[:, :, qw + HEAD_WIDTH:])], axis=1)
    sums = lax.psum((d_gain_attn, d_gain_mlp, d_gain_query, d_gain_key), ("fsdp", "replica"))
    return (output, input_grad, g_qkv, g_out, g_gate, g_up, g_down) + tuple(sums)


def solution(mesh):
    n_replica = mesh.shape["replica"]

    def program(*args):
        return per_device(n_replica, *args)

    rows = P(("fsdp", "replica"), None)
    weight = P("fsdp", None)
    return jax.shard_map(
        program,
        mesh=mesh,
        in_specs=(rows, rows) + (weight,) * 5 + (P(),) * 4 + (P("fsdp", None, None), P("fsdp", None)),
        out_specs=(rows, rows) + (weight,) * 5 + (P(),) * 4,
        check_vma=False,
    )
```

```python
import functools

import jax
import jax.numpy as jnp
from jax import lax
from jax.experimental import pallas as pl
from jax.experimental.pallas import tpu as pltpu
from jax.sharding import PartitionSpec as P

QUERY_HEADS = 16
KEY_VALUE_HEADS = 8
HEAD_WIDTH = 128
LMAX = 96

EPSILON = 1e-06
ROPE_BASE = 1000000.0
NEG_FILL = -1e30
BF = jnp.bfloat16
F32 = jnp.float32


MESH = pl.DeviceIdType.MESH
ANY = pl.BlockSpec(memory_space=pl.ANY)
VMEM = pl.BlockSpec(memory_space=pltpu.VMEM)
DMA = pltpu.SemaphoreType.DMA
STRIP = 16
LAG_MID = 2
LAG_END = 6


class Place:
    def __init__(self, n, n_z):
        self.n, self.chips, self.n_z = n, n // 2, n_z
        self.f = lax.axis_index("fsdp")
        self.chip, self.core = self.f // 2, lax.rem(self.f, 2)
        self.sib = self.f + 1 - 2 * self.core
        self.z = lax.axis_index("replica")
        low = (self.z < n_z // 2).astype(jnp.int32)
        self.inner = self.z - 1 + 2 * low
        self.outer = self.z + 1 - 2 * low
        self.mid = (self.z == n_z // 2 - 1) | (self.z == n_z // 2)
        self.has_outer = (self.z > 0) & (self.z < n_z - 1)

    def to(self, k):
        return lax.rem(self.f + k, self.n)

    def near(self, j):
        return 2 * lax.rem(self.chip + j // 2, self.chips) + lax.rem(self.core + lax.rem(j, 2), 2)

    def near_from(self, j):
        return 2 * lax.rem(self.chip + self.chips - j // 2, self.chips) + lax.rem(self.core + lax.rem(j, 2), 2)

    def plane(self, k):
        return lax.rem(self.z + k, self.n_z)

    def chip_at(self, k):
        return lax.rem(self.chip + k, self.chips)

    def greet(self, line):
        barrier = pltpu.get_barrier_semaphore()
        for k in range(1, self.n):
            pl.semaphore_signal(barrier, inc=1, device_id={"fsdp": self.to(k)}, device_id_type=MESH)
        if line:
            for k in range(1, self.n_z):
                pl.semaphore_signal(barrier, inc=1, device_id={"replica": self.plane(k)}, device_id_type=MESH)

        pl.semaphore_wait(barrier, self.n - 1 + (self.n_z - 1 if line else 0))


def remote(src, dst, send, recv, axis, index):
    return pltpu.make_async_remote_copy(
        src_ref=src, dst_ref=dst, send_sem=send, recv_sem=recv, device_id={axis: index}, device_id_type=MESH)


def strips(rows, body):
    def step(i, carry):
        body(pl.ds(pl.multiple_of(i * STRIP, STRIP), STRIP))
        return carry

    lax.fori_loop(0, rows // STRIP, step, 0)


class Exchange:
    def __init__(self, at, pieces, send, recv):
        self.copies, self.local = [], []
        for i, (src, dst) in enumerate(pieces):
            self.local.append(pltpu.make_async_copy(src(at.f), dst(at.f), recv.at[i, 0]))
            for k in range(1, at.n):
                self.copies.append(remote(src(at.to(k)), dst(at.f), send.at[i, k], recv.at[i, k], "fsdp", at.to(k)))

    def start(self):
        for c in self.copies + self.local:
            c.start()

    def wait(self):
        for c in self.copies + self.local:
            c.wait()


class Gather:
    def __init__(self, at, own, whole, sem):
        rows = own.shape[0]

        def block(i):
            return whole.at[pl.ds(pl.multiple_of(i * rows, rows), rows)]

        self.local = pltpu.make_async_copy(own, block(at.f), sem.at[0, 0])
        self.across = [remote(own, block(at.f), sem.at[0, 1], sem.at[1, 0], "fsdp", at.sib)]
        self.far, self.on = [], []
        for k in range(1, at.chips):
            to = 2 * at.chip_at(k) + at.core
            self.far.append(remote(own, block(at.f), sem.at[2, k], sem.at[3, k], "fsdp", to))
            came = 2 * at.chip_at(at.chips - k) + at.core
            self.on.append(remote(block(came), block(came), sem.at[4, k], sem.at[5, k], "fsdp", at.sib))

    def start(self):
        for c in self.far + self.across + [self.local]:
            c.start()

    def forward(self):
        for far, on in zip(self.far, self.on):
            far.wait_recv()
            on.start()

    def wait(self):
        for c in self.far:
            c.wait_send()
        for c in self.across + self.on + [self.local]:
            c.wait()


class ScatterSum:
    def __init__(self, at, part, near, own, far, sem):
        self.at, self.near, self.own, self.far = at, near, own, far
        rows = own.shape[1]
        self.rows = rows

        def block(i):
            return part.at[pl.ds(pl.multiple_of(i * rows, rows), rows)]

        self.across, self.load, self.send = [], [], []
        for k in range(at.chips):
            q = at.chip_at(k)
            self.across.append(remote(block(2 * q + 1 - at.core), near.at[k], sem.at[0, k], sem.at[1, k], "fsdp", at.sib))
            self.load.append(pltpu.make_async_copy(block(2 * q + at.core), own.at[k], sem.at[2, k]))
            if k:
                self.send.append(
                    remote(own.at[k], far.at[k - 1], sem.at[3, k], sem.at[4, k], "fsdp", 2 * q + at.core))

    def start(self):
        for k in list(range(1, self.at.chips)) + [0]:
            self.across[k].start()
            self.load[k].start()

    def forward(self):
        for k in list(range(1, self.at.chips)) + [0]:
            self.across[k].wait()
            self.load[k].wait()

            def add(at, k=k):
                self.own[k, at] = (self.own[k, at].astype(F32) + self.near[k, at].astype(F32)).astype(BF)

            strips(self.rows, add)
            if k:
                self.send[k - 1].start()

    def wait(self):
        for c in self.send:
            c.wait()

    def total(self, at):
        out = self.own[0, at].astype(F32)
        for k in range(self.at.chips - 1):
            out += self.far[k, at].astype(F32)
        return out


class LineSum:
    def __init__(self, at, chunk, came, arrive, send, recv, out, out_sem):
        self.at, self.chunk, self.came, self.arrive = at, chunk, came, arrive
        self.send, self.recv, self.out, self.out_sem = send, recv, out, out_sem
        self.count = chunk.shape[0]
        self.kind = at.mid.astype(jnp.int32)

    def inward(self, j):
        return remote(self.chunk.at[j], self.came.at[self.kind, j], self.send.at[0, j], self.recv.at[self.kind, j],
                      "replica", self.at.inner)

    def outward(self, j, src):
        return remote(src, self.came.at[1, j], self.send.at[1, j], self.recv.at[1, j], "replica", self.at.outer)

    def here(self, kind, j):
        return pltpu.make_async_copy(self.came.at[kind, j], self.came.at[kind, j], self.recv.at[kind, j])

    def up(self, j):
        pltpu.make_async_copy(self.chunk.at[j], self.chunk.at[j], self.arrive.at[j]).wait()

        @pl.when(self.at.has_outer)
        def _():
            self.here(0, j).wait()
            self.chunk[j] = (self.chunk[j].astype(F32) + self.came[0, j].astype(F32)).astype(BF)

        self.inward(j).start()

    def meet(self, j):
        self.here(1, j).wait()
        self.came[1, j] = (self.chunk[j].astype(F32) + self.came[1, j].astype(F32)).astype(BF)
        self.pass_on(j)

    def take(self, j):
        self.here(1, j).wait()
        self.pass_on(j)

    def pass_on(self, j):
        @pl.when(self.at.has_outer)
        def _():
            self.outward(j, self.came.at[1, j]).start()

        pltpu.make_async_copy(self.came.at[1, j], self.out(j), self.out_sem.at[j]).start()

    def settle(self):
        def step(j, carry):
            self.inward(j).wait_send()

            @pl.when(self.at.has_outer)
            def _():
                self.outward(j, self.came.at[1, j]).wait_send()

            pltpu.make_async_copy(self.came.at[1, j], self.out(j), self.out_sem.at[j]).wait()
            return carry

        lax.fori_loop(0, self.count, step, 0)


class Lines:
    def __init__(self, *lines):
        self.lines = lines
        self.order = [(i, j) for i, line in enumerate(lines) for j in range(line.count)]
        self.at = 0

    def run(self, steps=None):
        last = len(self.order) + LAG_END
        stop = last if steps is None else min(self.at + steps, len(self.order))
        while self.at < stop:
            first, size = self.at, 1
            now = self.parts(first)
            while first + size < stop and self.kinds(first + size) == self.kinds(first):
                size += 1

            def step(m, carry, now=now):
                up, mid, rest = now
                if up:
                    self.lines[up[0]].up(up[1] + m)
                if mid:
                    @pl.when(self.lines[mid[0]].at.mid)
                    def _():
                        self.lines[mid[0]].meet(mid[1] + m)
                if rest:
                    @pl.when(jnp.logical_not(self.lines[rest[0]].at.mid))
                    def _():
                        self.lines[rest[0]].take(rest[1] + m)
                return carry

            lax.fori_loop(0, size, step, 0)
            self.at += size

    def parts(self, t):
        return [self.order[i] if 0 <= i < len(self.order) else None for i in (t, t - LAG_MID, t - LAG_END)]

    def kinds(self, t):
        return [part and part[0] for part in self.parts(t)]

    def settle(self):
        for line in self.lines:
            line.settle()


def rms_of(values):
    return lax.rsqrt(jnp.mean(values * values, axis=-1, keepdims=True) + EPSILON)


def qkv_pieces(at, w, wc, qw):
    q_w, k_w = QUERY_HEADS * HEAD_WIDTH, KEY_VALUE_HEADS * HEAD_WIDTH
    shared = at.n // KEY_VALUE_HEADS
    depth = w.shape[0]

    def cols(start, width):
        return pl.ds(pl.multiple_of(start, HEAD_WIDTH), width)

    def rows(s):
        return pl.ds(pl.multiple_of(s * depth, depth), depth)

    return [
        (lambda t: w.at[:, cols(t * qw, qw)], lambda s: wc.at[rows(s), pl.ds(0, qw)]),
        (lambda t: w.at[:, cols(q_w + t // shared * HEAD_WIDTH, HEAD_WIDTH)],
         lambda s: wc.at[rows(s), pl.ds(qw, HEAD_WIDTH)]),
        (lambda t: w.at[:, cols(q_w + k_w + t // shared * HEAD_WIDTH, HEAD_WIDTH)],
         lambda s: wc.at[rows(s), pl.ds(qw + HEAD_WIDTH, HEAD_WIDTH)]),
    ]


def col_piece(w, wc, share):
    depth = w.shape[0]
    return (lambda t: w.at[:, pl.ds(pl.multiple_of(t * share, HEAD_WIDTH), share)],
            lambda s: wc.at[pl.ds(pl.multiple_of(s * depth, depth), depth)])


def begin_kernel(n, n_z, x_ref, gain_ref, place_ref, wqkv_ref, n1_ref, wc_ref, places_ref,
                 own, s_x, r_x, s_g, s_p, r_p):
    at = Place(n, n_z)
    rows = x_ref.shape[0]
    at.greet(False)
    weights = Exchange(at, qkv_pieces(at, wqkv_ref, wc_ref, QUERY_HEADS * HEAD_WIDTH // n), s_x, r_x)
    place = Exchange(at, [(lambda t: place_ref, lambda s: places_ref.at[s])], s_p, r_p)
    place.start()
    weights.start()

    def norm(strip):
        x = x_ref[strip].astype(F32)
        own[strip] = (x * rms_of(x) * gain_ref[...]).astype(BF)

    strips(rows, norm)
    gather = Gather(at, own, n1_ref, s_g)
    gather.start()
    gather.forward()
    gather.wait()
    place.wait()
    weights.wait()


def middle_kernel(n, n_z, part_ref, x_ref, gain_ref, g_ref, gate_ref, up_ref, down_ref,
                  h_ref, n2_ref, gall_ref, gate_c, up_c, down_c,
                  near, mine, far, own, s_r, s_a, s_b, s_x, r_x, s_y, r_y):
    at = Place(n, n_z)
    share = gate_c.shape[1]
    at.greet(False)
    total = ScatterSum(at, part_ref, near, mine, far, s_r)
    total.start()
    total.forward()
    first = Exchange(at, [col_piece(gate_ref, gate_c, share), col_piece(up_ref, up_c, share)], s_x, r_x)
    second = Exchange(at, [col_piece(down_ref, down_c, share)], s_y, r_y)
    first.start()
    total.wait()

    def norm(strip):
        h = x_ref[strip].astype(F32) + total.total(strip)
        h_ref[strip] = h
        own[strip] = (h * rms_of(h) * gain_ref[...]).astype(BF)

    strips(x_ref.shape[0], norm)
    n2 = Gather(at, own, n2_ref, s_a)
    g_all = Gather(at, g_ref, gall_ref, s_b)
    n2.start()
    g_all.start()
    second.start()
    n2.forward()
    g_all.forward()
    n2.wait()
    g_all.wait()
    first.wait()
    second.wait()


def dot(left, right):
    return jnp.dot(left, right, preferred_element_type=F32)


def dot_rows(left, right):
    return lax.dot_general(left, right, (((0,), (0,)), ((), ())), preferred_element_type=F32)


def dot_cols(left, right):
    return lax.dot_general(left, right, (((1,), (1,)), ((), ())), preferred_element_type=F32)


def rope_tables(positions):
    half_size = HEAD_WIDTH // 2
    steps_up = jnp.arange(half_size, dtype=F32)
    inverse = ROPE_BASE ** (-(2.0 * steps_up) / HEAD_WIDTH)
    angles = positions.astype(F32)[:, None] * inverse[None, :]
    return jnp.cos(angles), jnp.sin(angles)


def rotate(values, cosine, sine):
    half_size = HEAD_WIDTH // 2
    first, second = values[..., :half_size], values[..., half_size:]
    return jnp.concatenate([first * cosine - second * sine, second * cosine + first * sine], axis=-1)


def norm_back(d_normed, normed, rms):
    return rms * (d_normed - normed * jnp.mean(d_normed * normed, axis=-1, keepdims=True))


def grad_chunks(at, grad, chunk, send, recv):
    depth = chunk.shape[1]

    def rows(t):
        return grad.at[pl.ds(pl.multiple_of(t * depth, depth), depth)]

    copies = [pltpu.make_async_copy(rows(at.f), chunk.at[0], recv.at[0])]
    for j in range(1, at.n):
        copies.append(remote(rows(at.near(j)), chunk.at[j], send.at[j], recv.at[j], "fsdp", at.near(j)))
    return copies


def start_all(copies):
    for c in copies:
        c.start()


def sends_done(copies):
    for c in copies[1:]:
        c.wait_send()


def turn_kernel(n, n_z, part_ref, h_ref, g_ref, gain_ref, down_ref,
                dh_ref, dhall_ref, dgain_ref, gdown_ref,
                near, mine, far, own, chunk, came, s_r, s_a, s_c, r_c, s_z, r_z, s_o):
    at = Place(n, n_z)
    share = chunk.shape[2]
    at.greet(True)
    total = ScatterSum(at, part_ref, near, mine, far, s_r)
    down = grad_chunks(at, down_ref, chunk, s_c, r_c)
    lines = Lines(LineSum(at, chunk, came, r_c, s_z, r_z, by_sender(at, gdown_ref, share), s_o))
    half = at.n // 2
    total.start()
    start_all(down[:half])
    lines.run(2)
    total.forward()
    lines.run(half - 2)
    total.wait()
    start_all(down[half:])
    dgain_ref[...] = jnp.zeros_like(dgain_ref)

    def back(strip):
        d_n2 = total.total(strip)
        h = h_ref[strip]
        r2 = rms_of(h)
        u2 = h * r2
        dgain_ref[...] += jnp.sum(d_n2 * u2, axis=0, keepdims=True)
        d_h = g_ref[strip].astype(F32) + norm_back(d_n2 * gain_ref[...], u2, r2)
        dh_ref[strip] = d_h
        own[strip] = d_h.astype(BF)

    strips(h_ref.shape[0], back)
    gather = Gather(at, own, dhall_ref, s_a)
    gather.start()
    lines.run(half)
    gather.forward()
    lines.run()
    gather.wait()
    sends_done(down)
    lines.settle()


def by_sender(at, ref, share):
    def place(j):
        return ref.at[:, pl.ds(pl.multiple_of(at.near_from(j) * share, HEAD_WIDTH), share)]

    return place


def end_kernel(n, n_z, part_ref, party_ref, x_ref, h_ref, dh_ref, gain_ref, dgain_ref, dheads_ref,
               gate_ref, up_ref, qkv_ref, gout_ref,
               dx_ref, y_ref, gains_ref, ggate_ref, gup_ref, gqkv_ref, ggout_ref,
               near, mine, far, ynear, ymine, yfar, own_gain, plane_gain, line_gain, all_gain,
               gate_k, gate_m, up_k, up_m, qkv_k, qkv_m, out_k, out_m,
               s_r, s_y, s_p, r_p, s_q, r_q, s_c, r_c, s_z, r_z, s_o, s_l, r_l):
    at = Place(n, n_z)
    share, share_out = gate_k.shape[2], out_k.shape[2]
    rows = x_ref.shape[0]
    at.greet(True)

    def line(i, chunk, came, place, arrive):
        return LineSum(at, chunk, came, arrive, s_z.at[i], r_z.at[i], place, s_o.at[i])

    gate = grad_chunks(at, gate_ref, gate_k, s_c.at[0], r_c.at[0])
    up = grad_chunks(at, up_ref, up_k, s_c.at[1], r_c.at[1])
    qkv = grad_chunks(at, qkv_ref, qkv_k, s_c.at[2], r_c.at[2])

    def out_cols(ref):
        return lambda j: ref.at[:, pl.ds(pl.multiple_of(j * share_out, HEAD_WIDTH), share_out)]

    outs = [pltpu.make_async_copy(out_cols(gout_ref)(j), out_k.at[j], r_l.at[j]) for j in range(out_k.shape[0])]

    def qkv_place(j):
        return gqkv_ref.at[at.near_from(j)]

    lines = Lines(
        line(3, out_k, out_m, out_cols(ggout_ref), r_l),
        line(0, gate_k, gate_m, by_sender(at, ggate_ref, share), r_c.at[0]),
        line(1, up_k, up_m, by_sender(at, gup_ref, share), r_c.at[1]),
        line(2, qkv_k, qkv_m, qkv_place, r_c.at[2]),
    )
    start_all(outs)
    total = ScatterSum(at, part_ref, near, mine, far, s_r)
    y = ScatterSum(at, party_ref, ynear, ymine, yfar, s_y)
    start_all(gate)
    total.start()
    lines.run(out_k.shape[0])
    total.forward()
    start_all(up)
    lines.run(n - 2)
    total.wait()
    own_gain[...] = jnp.zeros_like(own_gain)
    own_gain[1:2] = dgain_ref[...]
    own_gain[2:3, :2 * HEAD_WIDTH] = dheads_ref[...]

    def back(strip):
        d_n1 = total.total(strip)
        x = x_ref[strip].astype(F32)
        r1 = rms_of(x)
        u1 = x * r1
        own_gain[0:1] += jnp.sum(d_n1 * u1, axis=0, keepdims=True)
        dx_ref[strip] = (dh_ref[strip] + norm_back(d_n1 * gain_ref[...], u1, r1)).astype(BF)

    strips(rows, back)
    gains = Exchange(at, [(lambda t: own_gain, lambda s: plane_gain.at[s])], s_p, r_p)
    gains.start()
    y.start()
    lines.run(4)
    y.forward()
    start_all(qkv)
    lines.run(4)
    gains.wait()
    line_gain[...] = jnp.sum(plane_gain[...], axis=0)
    others = [
        remote(line_gain, all_gain.at[at.z], s_q.at[k], r_q.at[k], "replica", at.plane(k)) for k in range(1, n_z)]
    start_all(others)
    all_gain[at.z] = line_gain[...]
    y.wait()

    def finish(strip):
        y_ref[strip] = (h_ref[strip] + y.total(strip)).astype(BF)

    strips(rows, finish)
    lines.run()
    for c in others:
        c.wait()
    gains_ref[...] = jnp.sum(all_gain[...], axis=0)
    for copies in (gate, up, qkv):
        sends_done(copies)
    lines.settle()


def begin(n, n_z, x, gain, place, w_qkv):
    rows, width = x.shape
    total, wide = n * rows, (QUERY_HEADS // n + 2) * HEAD_WIDTH
    return pl.pallas_call(
        functools.partial(begin_kernel, n, n_z),
        out_shape=(
            jax.ShapeDtypeStruct((total, width), BF),
            jax.ShapeDtypeStruct((width, wide), BF),
            jax.ShapeDtypeStruct((n,) + place.shape, place.dtype),
        ),
        in_specs=[VMEM, VMEM, ANY, ANY],
        out_specs=(ANY, ANY, ANY),
        scratch_shapes=[
            pltpu.VMEM((rows, width), BF), DMA((3, n)), DMA((3, n)), DMA((6, n)), DMA((1, n)), DMA((1, n))],
        compiler_params=pltpu.CompilerParams(collective_id=0, has_side_effects=True, vmem_limit_bytes=32 << 20),
        name="begin",
    )(x, gain, place, w_qkv)


def middle(n, n_z, part, x, gain, g, gate, up, down):
    rows, width = x.shape
    total, share, chips = n * rows, gate.shape[1] // n, n // 2
    columns = jax.ShapeDtypeStruct((width, share), BF)
    return pl.pallas_call(
        functools.partial(middle_kernel, n, n_z),
        out_shape=(
            jax.ShapeDtypeStruct((rows, width), F32),
            jax.ShapeDtypeStruct((total, width), BF),
            jax.ShapeDtypeStruct((total, width), BF),
            columns, columns, columns,
        ),
        in_specs=[ANY, VMEM, VMEM, ANY, ANY, ANY, ANY],
        out_specs=(VMEM, ANY, ANY, ANY, ANY, ANY),
        scratch_shapes=[
            pltpu.VMEM((chips, rows, width), BF), pltpu.VMEM((chips, rows, width), BF),
            pltpu.VMEM((chips - 1, rows, width), BF), pltpu.VMEM((rows, width), BF),
            DMA((5, n)), DMA((6, n)), DMA((6, n)), DMA((2, n)), DMA((2, n)), DMA((1, n)), DMA((1, n))],
        compiler_params=pltpu.CompilerParams(collective_id=1, has_side_effects=True, vmem_limit_bytes=48 << 20),
        name="middle",
    )(part, x, gain, g, gate, up, down)


def turn(n, n_z, part, h, g, gain, down):
    rows, width = h.shape
    chips, share, depth = n // 2, down.shape[1], width // n
    block = functools.partial(pltpu.VMEM, dtype=BF)
    return pl.pallas_call(
        functools.partial(turn_kernel, n, n_z),
        out_shape=(
            jax.ShapeDtypeStruct((rows, width), F32),
            jax.ShapeDtypeStruct((n * rows, width), BF),
            jax.ShapeDtypeStruct((1, width), F32),
            jax.ShapeDtypeStruct((depth, n * share), BF),
        ),
        in_specs=[ANY, VMEM, VMEM, VMEM, ANY],
        out_specs=(VMEM, ANY, VMEM, ANY),
        scratch_shapes=[
            block((chips, rows, width)), block((chips, rows, width)), block((chips - 1, rows, width)), block((rows, width)),
            block((n, depth, share)), block((2, n, depth, share)),
            DMA((5, n)), DMA((6, n)), DMA((n,)), DMA((n,)), DMA((2, n)), DMA((2, n)), DMA((n,))],
        compiler_params=pltpu.CompilerParams(collective_id=2, has_side_effects=True, vmem_limit_bytes=56 << 20),
        name="turn",
    )(part, h, g, gain, down)


def end(n, n_z, part, part_y, x, h, d_h, gain, d_gain, d_heads, gate, up, qkv, out):
    rows, width = x.shape
    chips, share, share_qkv, depth = n // 2, gate.shape[1], qkv.shape[1], width // n
    share_out = 4 * HEAD_WIDTH
    outs = width // share_out
    block = functools.partial(pltpu.VMEM, dtype=BF)
    sums = [block((chips, rows, width)), block((chips, rows, width)), block((chips - 1, rows, width))]
    gains = (8, width)
    return pl.pallas_call(
        functools.partial(end_kernel, n, n_z),
        out_shape=(
            jax.ShapeDtypeStruct((rows, width), BF),
            jax.ShapeDtypeStruct((rows, width), BF),
            jax.ShapeDtypeStruct(gains, F32),
            jax.ShapeDtypeStruct((depth, n * share), BF),
            jax.ShapeDtypeStruct((depth, n * share), BF),
            jax.ShapeDtypeStruct((n, depth, share_qkv), BF),
            jax.ShapeDtypeStruct((depth, width), BF),
        ),
        in_specs=[ANY, ANY] + [VMEM] * 6 + [ANY] * 4,
        out_specs=(VMEM, VMEM, VMEM, ANY, ANY, ANY, ANY),
        scratch_shapes=sums + sums + [
            pltpu.VMEM(gains, F32), pltpu.VMEM((n,) + gains, F32), pltpu.VMEM(gains, F32), pltpu.VMEM((n_z,) + gains, F32),
            block((n, depth, share)), block((2, n, depth, share)), block((n, depth, share)), block((2, n, depth, share)),
            block((n, depth, share_qkv)), block((2, n, depth, share_qkv)),
            block((outs, depth, share_out)), block((2, outs, depth, share_out)),
            DMA((5, n)), DMA((5, n)), DMA((1, n)), DMA((1, n)), DMA((n_z,)), DMA((n_z,)),
            DMA((3, n)), DMA((3, n)), DMA((4, 2, n)), DMA((4, 2, n)), DMA((4, n)), DMA((outs,)), DMA((outs,))],
        compiler_params=pltpu.CompilerParams(collective_id=3, has_side_effects=True, vmem_limit_bytes=60 << 20),
        name="end",
    )(part, part_y, x, h, d_h, gain, d_gain, d_heads, gate, up, qkv, out)


def row_positions(flat_lens, ranks, first_row, count):
    earlier = (ranks[:, None] < ranks[None, :]).astype(jnp.int32)
    starts = jnp.sum(flat_lens[:, None] * earlier, axis=0)
    rows = first_row + jnp.arange(count, dtype=jnp.int32)
    begun = jnp.where(starts[None, :] <= rows[:, None], starts[None, :], 0)
    return rows - jnp.max(begun, axis=1)


def per_device(
    n_replica, tokens, cotangent, w_qkv, w_out, w_gate, w_up, w_down_t,
    gain_attn, gain_mlp, gain_query, gain_key, dealt_lens, seq_order,
):
    rows, width = tokens.shape
    n_fsdp = width // w_qkv.shape[0]
    q_w = QUERY_HEADS * HEAD_WIDTH
    k_w = KEY_VALUE_HEADS * HEAD_WIDTH
    replica = lax.axis_index("replica")
    shared = n_fsdp // KEY_VALUE_HEADS
    heads = QUERY_HEADS // n_fsdp
    qw = heads * HEAD_WIDTH

    pos = row_positions(dealt_lens[0].reshape(-1), seq_order[0], replica * rows, rows)
    depth = w_qkv.shape[0]
    place = jnp.zeros((8, HEAD_WIDTH), jnp.int32).reshape(-1).at[:rows].set(pos).reshape(8, HEAD_WIDTH)
    n1, w_qkv_c, places = begin(n_fsdp, n_replica, tokens, gain_attn[None], place, w_qkv)
    pos_all = places.reshape(n_fsdp, -1)[:, :rows].reshape(-1)

    total = n1.shape[0]

    proj = dot(n1, w_qkv_c)
    q_rows = proj[:, :qw].reshape(total, heads, HEAD_WIDTH)
    k_rows = proj[:, qw:qw + HEAD_WIDTH]
    v_low = proj[:, qw + HEAD_WIDTH:].astype(BF)
    rq = lax.rsqrt(jnp.mean(q_rows * q_rows, axis=2, keepdims=True) + EPSILON)
    q_hat = q_rows * rq
    rk = lax.rsqrt(jnp.mean(k_rows * k_rows, axis=1, keepdims=True) + EPSILON)
    k_hat = k_rows * rk
    cosine, sine = rope_tables(pos_all)
    q_low = rotate(q_hat * gain_query, cosine[:, None], sine[:, None]).astype(BF)
    k_low = rotate(k_hat * gain_key, cosine, sine).astype(BF)

    groups = n_fsdp
    halo = LMAX
    kv = jnp.concatenate([k_low, v_low], axis=1).reshape(groups, rows, 2 * HEAD_WIDTH)
    up_pairs = [(i, i + 1) for i in range(n_replica - 1)]
    down_pairs = [(i + 1, i) for i in range(n_replica - 1)]
    kv_before = lax.ppermute(kv[:, rows - halo:], "replica", up_pairs)
    kv_window = jnp.concatenate([kv_before, kv], axis=1)
    k_win, v_win = kv_window[..., :HEAD_WIDTH], kv_window[..., HEAD_WIDTH:]
    q_grp = q_low.reshape(groups, rows, heads, HEAD_WIDTH)
    pos_grp = pos_all.reshape(groups, rows)
    i_at = halo + jnp.arange(rows, dtype=jnp.int32)
    j_at = jnp.arange(halo + rows, dtype=jnp.int32)
    mask = (j_at[None, None, :] <= i_at[None, :, None]) & (
        j_at[None, None, :] >= i_at[None, :, None] - pos_grp[:, :, None])
    mask = mask[:, None]
    scale = HEAD_WIDTH ** (-0.5)
    scores = jnp.einsum("gqhd,gkd->ghqk", q_grp, k_win, preferred_element_type=F32) * scale
    scores = jnp.where(mask, scores, NEG_FILL)
    top = jnp.max(scores, axis=3, keepdims=True)
    terms = jnp.exp(scores - top)
    probs = terms / jnp.sum(terms, axis=3, keepdims=True)
    probs_low = probs.astype(BF)
    ctx = jnp.einsum("ghqk,gkd->gqhd", probs_low, v_win, preferred_element_type=F32)
    ctx_low = ctx.reshape(total, qw).astype(BF)
    h, n2, g_all, gate_c, up_c, down_c = middle(
        n_fsdp, n_replica, dot(ctx_low, w_out).astype(BF), tokens, gain_mlp[None], cotangent, w_gate, w_up, w_down_t)

    gate = dot(n2, gate_c)
    up = dot(n2, up_c)
    sg = jax.nn.sigmoid(gate)
    silu = gate * sg
    act = (silu * up).astype(BF)
    part_y = dot_cols(act, down_c).astype(BF)

    d_act = dot(g_all, down_c)
    d_gate = (d_act * up * sg * (1.0 + gate * (1.0 - sg))).astype(BF)
    d_up = (d_act * silu).astype(BF)

    d_h, dh_all, d_gain_mlp, g_down = turn(
        n_fsdp, n_replica, (dot_cols(d_gate, gate_c) + dot_cols(d_up, up_c)).astype(BF), h, cotangent, gain_mlp[None],
        dot_rows(g_all, act).astype(BF))
    d_ctx = dot_cols(dh_all, w_out).astype(BF).reshape(groups, rows, heads, HEAD_WIDTH)
    d_v = jnp.einsum("ghqk,gqhd->gkd", probs_low, d_ctx, preferred_element_type=F32)
    d_p = jnp.einsum("gqhd,gkd->ghqk", d_ctx, v_win, preferred_element_type=F32)
    delta = jnp.sum(probs * d_p, axis=3, keepdims=True)
    d_s = (probs * (d_p - delta)).astype(BF)
    d_q = jnp.einsum("ghqk,gkd->gqhd", d_s, k_win, preferred_element_type=F32) * scale
    d_k = jnp.einsum("ghqk,gqhd->gkd", d_s, q_grp, preferred_element_type=F32) * scale
    d_kv = jnp.concatenate([d_k, d_v], axis=2)
    d_kv_after = lax.ppermute(d_kv[:, :halo].astype(BF), "replica", down_pairs).astype(F32)
    d_kv = d_kv[:, halo:]
    d_kv = jnp.concatenate([d_kv[:, :rows - halo], d_kv[:, rows - halo:] + d_kv_after], axis=1)
    d_k = d_kv[..., :HEAD_WIDTH].reshape(total, HEAD_WIDTH)
    d_v = d_kv[..., HEAD_WIDTH:].reshape(total, HEAD_WIDTH)
    d_q = d_q.reshape(total, heads, HEAD_WIDTH)
    dq_g = rotate(d_q, cosine[:, None], -sine[:, None])
    dk_g = rotate(d_k, cosine, -sine)
    d_gain_query = jnp.sum(dq_g * q_hat, axis=(0, 1))
    d_gain_key = jnp.sum(dk_g * k_hat, axis=0)
    dq = norm_back(dq_g * gain_query, q_hat, rq)
    dk = norm_back(dk_g * gain_key, k_hat, rk)
    d_proj = jnp.concatenate([dq.reshape(total, qw), dk, d_v], axis=1).astype(BF)
    d_heads = jnp.concatenate([d_gain_query, d_gain_key])[None]
    input_grad, output, gains, g_gate, g_up, g_qkv, g_out = end(
        n_fsdp, n_replica, dot_cols(d_proj, w_qkv_c).astype(BF), part_y, tokens, h, d_h, gain_attn[None], d_gain_mlp, d_heads,
        dot_rows(n2, d_gate).astype(BF), dot_rows(n2, d_up).astype(BF),
        dot_rows(n1, d_proj).astype(BF), dot_rows(ctx_low, dh_all).astype(BF))
    g_qkv = g_qkv.transpose(1, 0, 2).astype(F32)

    def of_key_heads(part):
        return jnp.sum(part.reshape(depth, KEY_VALUE_HEADS, shared, HEAD_WIDTH), axis=2).reshape(depth, k_w)

    g_qkv = jnp.concatenate([
        g_qkv[:, :, :qw].reshape(depth, q_w),
        of_key_heads(g_qkv[:, :, qw:qw + HEAD_WIDTH]),
        of_key_heads(g_qkv[:, :, qw + HEAD_WIDTH:])], axis=1)
    return (
        output, input_grad, g_qkv, g_out.astype(F32), g_gate.astype(F32), g_up.astype(F32), g_down.astype(F32),
        gains[0], gains[1], gains[2, :HEAD_WIDTH], gains[2, HEAD_WIDTH:2 * HEAD_WIDTH])


def solution(mesh):
    n_replica = mesh.shape["replica"]

    def program(*args):
        return per_device(n_replica, *args)

    rows = P(("fsdp", "replica"), None)
    weight = P("fsdp", None)
    return jax.shard_map(
        program,
        mesh=mesh,
        in_specs=(rows, rows) + (weight,) * 5 + (P(),) * 4 + (P("fsdp", None, None), P("fsdp", None)),
        out_specs=(rows, rows) + (weight,) * 5 + (P(),) * 4,
        check_vma=False,
    )
```

```python
import functools

import jax
import jax.numpy as jnp
import numpy as np
from jax import lax
from jax.experimental import pallas as pl
from jax.experimental.pallas import tpu as pltpu
from jax.sharding import PartitionSpec as P

QUERY_HEADS = 16
KEY_VALUE_HEADS = 8
HEAD_WIDTH = 128
LMAX = 96

EPSILON = 1e-06
ROPE_BASE = 1000000.0
NEG_FILL = -1e30
BF = jnp.bfloat16
F32 = jnp.float32


MESH = pl.DeviceIdType.MESH
ANY = pl.BlockSpec(memory_space=pl.ANY)
VMEM = pl.BlockSpec(memory_space=pltpu.VMEM)
DMA = pltpu.SemaphoreType.DMA
STRIP = 16
LAG_MID = 2
LAG_END = 6
RING = 4
LEAD = 5


class Place:
    def __init__(self, n, n_z):
        self.n, self.chips, self.n_z = n, n // 2, n_z
        self.f = lax.axis_index("fsdp")
        self.chip, self.core = self.f // 2, lax.rem(self.f, 2)
        self.sib = self.f + 1 - 2 * self.core
        self.z = lax.axis_index("replica")
        low = (self.z < n_z // 2).astype(jnp.int32)
        self.inner = self.z - 1 + 2 * low
        self.outer = self.z + 1 - 2 * low
        self.mid = (self.z == n_z // 2 - 1) | (self.z == n_z // 2)
        self.has_outer = (self.z > 0) & (self.z < n_z - 1)

    def to(self, k):
        return lax.rem(self.f + k, self.n)

    def near(self, j):
        return 2 * lax.rem(self.chip + j // 2, self.chips) + lax.rem(self.core + lax.rem(j, 2), 2)

    def near_from(self, j):
        return 2 * lax.rem(self.chip + self.chips - j // 2, self.chips) + lax.rem(self.core + lax.rem(j, 2), 2)

    def plane(self, k):
        return lax.rem(self.z + k, self.n_z)

    def chip_at(self, k):
        return lax.rem(self.chip + k, self.chips)

    def greet(self, line):
        barrier = pltpu.get_barrier_semaphore()
        for k in range(1, self.n):
            pl.semaphore_signal(barrier, inc=1, device_id={"fsdp": self.to(k)}, device_id_type=MESH)
        if line:
            for k in range(1, self.n_z):
                pl.semaphore_signal(barrier, inc=1, device_id={"replica": self.plane(k)}, device_id_type=MESH)

        pl.semaphore_wait(barrier, self.n - 1 + (self.n_z - 1 if line else 0))


def remote(src, dst, send, recv, axis, index):
    return pltpu.make_async_remote_copy(
        src_ref=src, dst_ref=dst, send_sem=send, recv_sem=recv, device_id={axis: index}, device_id_type=MESH)


def strips(rows, body):
    def step(i, carry):
        body(pl.ds(pl.multiple_of(i * STRIP, STRIP), STRIP))
        return carry

    lax.fori_loop(0, rows // STRIP, step, 0)


class Exchange:
    def __init__(self, at, pieces, send, recv):
        self.copies, self.local = [], []
        for i, (src, dst) in enumerate(pieces):
            self.local.append(pltpu.make_async_copy(src(at.f), dst(at.f), recv.at[i, 0]))
            for k in range(1, at.n):
                self.copies.append(remote(src(at.to(k)), dst(at.f), send.at[i, k], recv.at[i, k], "fsdp", at.to(k)))

    def start(self):
        for c in self.copies + self.local:
            c.start()

    def wait(self):
        for c in self.copies + self.local:
            c.wait()


class Gather:
    def __init__(self, at, own, whole, sem):
        rows = own.shape[0]

        def block(i):
            return whole.at[pl.ds(pl.multiple_of(i * rows, rows), rows)]

        self.local = pltpu.make_async_copy(own, block(at.f), sem.at[0, 0])
        self.across = [remote(own, block(at.f), sem.at[0, 1], sem.at[1, 0], "fsdp", at.sib)]
        self.far, self.on = [], []
        for k in range(1, at.chips):
            to = 2 * at.chip_at(k) + at.core
            self.far.append(remote(own, block(at.f), sem.at[2, k], sem.at[3, k], "fsdp", to))
            came = 2 * at.chip_at(at.chips - k) + at.core
            self.on.append(remote(block(came), block(came), sem.at[4, k], sem.at[5, k], "fsdp", at.sib))

    def start(self):
        for c in self.far + self.across + [self.local]:
            c.start()

    def forward(self):
        for far, on in zip(self.far, self.on):
            far.wait_recv()
            on.start()

    def wait(self):
        for c in self.far:
            c.wait_send()
        for c in self.across + self.on + [self.local]:
            c.wait()


class ScatterSum:
    def __init__(self, at, part, near, own, far, sem, made=False):
        self.made = made
        self.at, self.near, self.own, self.far = at, near, own, far
        rows = own.shape[1]
        self.rows = rows

        def block(i):
            return part.at[pl.ds(pl.multiple_of(i * rows, rows), rows)]

        self.across, self.load, self.send = [], [], []
        for k in range(at.chips):
            q = at.chip_at(k)
            other = part.at[k] if made else block(2 * q + 1 - at.core)
            self.across.append(remote(other, near.at[k], sem.at[0, k], sem.at[1, k], "fsdp", at.sib))
            if not made:
                self.load.append(pltpu.make_async_copy(block(2 * q + at.core), own.at[k], sem.at[2, k]))
            if k:
                self.send.append(
                    remote(own.at[k], far.at[k - 1], sem.at[3, k], sem.at[4, k], "fsdp", 2 * q + at.core))

    def start(self):
        for k in list(range(1, self.at.chips)) + [0]:
            self.across[k].start()
            if not self.made:
                self.load[k].start()

    def forward(self):
        for k in list(range(1, self.at.chips)) + [0]:
            self.across[k].wait()
            if not self.made:
                self.load[k].wait()

            def add(at, k=k):
                self.own[k, at] = (self.own[k, at].astype(F32) + self.near[k, at].astype(F32)).astype(BF)

            strips(self.rows, add)
            if k:
                self.send[k - 1].start()

    def wait(self):
        for c in self.send:
            c.wait()

    def total(self, at):
        out = self.own[0, at].astype(F32)
        for k in range(self.at.chips - 1):
            out += self.far[k, at].astype(F32)
        return out


class LineSum:
    def __init__(self, at, chunk, ring, arrive, send, recv, credit, out, out_sem, skip=0, feed=None):
        self.at, self.chunk, self.ring, self.arrive, self.skip = at, chunk, ring, arrive, skip
        self.send, self.recv, self.credit, self.out, self.out_sem = send, recv, credit, out, out_sem
        self.feed = feed
        self.count = chunk.shape[0]
        self.kind = at.mid.astype(jnp.int32)

    def slot(self, j):
        return lax.rem(j, RING)

    def inward(self, j):
        return remote(self.chunk.at[j], self.ring.at[self.kind, self.slot(j)], self.send.at[0, j],
                      self.recv.at[self.kind, j], "replica", self.at.inner)

    def outward(self, j, src):
        return remote(src, self.out(j), self.send.at[1, j], self.recv.at[2, j], "replica", self.at.outer)

    def keep(self, j):
        return pltpu.make_async_copy(self.chunk.at[j], self.out(j), self.out_sem.at[j])

    def take_in(self, kind, j, plane):
        here = self.ring.at[kind, self.slot(j)]
        pltpu.make_async_copy(here, here, self.recv.at[kind, j]).wait()
        self.chunk[j] = (self.chunk[j].astype(F32) + self.ring[kind, self.slot(j)].astype(F32)).astype(BF)

        @pl.when(j + RING < self.count)
        def _():
            pl.semaphore_signal(self.credit, inc=1, device_id={"replica": plane}, device_id_type=MESH)

    def up(self, j):
        if self.feed:
            @pl.when(j + LEAD < self.count)
            def _():
                self.feed(j + LEAD)

        @pl.when(j >= self.skip)
        def _():
            pltpu.make_async_copy(self.chunk.at[j], self.chunk.at[j], self.arrive.at[j]).wait()

        @pl.when(self.at.has_outer)
        def _():
            self.take_in(0, j, self.at.outer)

        @pl.when(j >= RING)
        def _():
            pl.semaphore_wait(self.credit, 1)

        self.inward(j).start()

    def meet(self, j):
        self.inward(j).wait_send()
        self.take_in(1, j, self.at.inner)

        @pl.when(self.at.has_outer)
        def _():
            self.outward(j, self.chunk.at[j]).start()

        self.keep(j).start()

    def take(self, j):
        pltpu.make_async_copy(self.out(j), self.out(j), self.recv.at[2, j]).wait()

        @pl.when(self.at.has_outer)
        def _():
            self.outward(j, self.out(j)).start()

    def settle(self):
        def step(j, carry):
            @pl.when(self.at.mid)
            def _():
                self.keep(j).wait()

            @pl.when(jnp.logical_not(self.at.mid))
            def _():
                self.inward(j).wait_send()

            @pl.when(self.at.has_outer)
            def _():
                self.outward(j, self.chunk.at[j]).wait_send()

            return carry

        lax.fori_loop(0, self.count, step, 0)


class Lines:
    def __init__(self, *lines):
        self.lines = lines
        self.order = [(i, j) for i, line in enumerate(lines) for j in range(line.count)]
        self.at = 0

    def run(self, steps=None, body=None):
        begin = self.at
        last = len(self.order) + LAG_END
        stop = last if steps is None else min(self.at + steps, len(self.order))
        while self.at < stop:
            first, size = self.at, 1
            now = self.parts(first)
            while first + size < stop and self.kinds(first + size) == self.kinds(first):
                size += 1

            def step(m, carry, now=now, first=first):
                up, mid, rest = now
                if up:
                    self.lines[up[0]].up(up[1] + m)
                if mid:
                    @pl.when(self.lines[mid[0]].at.mid)
                    def _():
                        self.lines[mid[0]].meet(mid[1] + m)
                if rest:
                    @pl.when(jnp.logical_not(self.lines[rest[0]].at.mid))
                    def _():
                        self.lines[rest[0]].take(rest[1] + m)
                if body:
                    body(first - begin + m)
                return carry

            lax.fori_loop(0, size, step, 0)
            self.at += size

    def parts(self, t):
        return [self.order[i] if 0 <= i < len(self.order) else None for i in (t, t - LAG_MID, t - LAG_END)]

    def kinds(self, t):
        return [part and part[0] for part in self.parts(t)]

    def settle(self):
        for line in self.lines:
            line.settle()


def rms_of(values):
    return lax.rsqrt(jnp.mean(values * values, axis=-1, keepdims=True) + EPSILON)


def qkv_pieces(at, w, wc, qw):
    q_w, k_w = QUERY_HEADS * HEAD_WIDTH, KEY_VALUE_HEADS * HEAD_WIDTH
    shared = at.n // KEY_VALUE_HEADS
    depth = w.shape[0]

    def cols(start, width):
        return pl.ds(pl.multiple_of(start, HEAD_WIDTH), width)

    def rows(s):
        return pl.ds(pl.multiple_of(s * depth, depth), depth)

    return [
        (lambda t: w.at[:, cols(t * qw, qw)], lambda s: wc.at[rows(s), pl.ds(0, qw)]),
        (lambda t: w.at[:, cols(q_w + t // shared * HEAD_WIDTH, HEAD_WIDTH)],
         lambda s: wc.at[rows(s), pl.ds(qw, HEAD_WIDTH)]),
        (lambda t: w.at[:, cols(q_w + k_w + t // shared * HEAD_WIDTH, HEAD_WIDTH)],
         lambda s: wc.at[rows(s), pl.ds(qw + HEAD_WIDTH, HEAD_WIDTH)]),
    ]


def col_piece(w, wc, share):
    depth = w.shape[0]
    return (lambda t: w.at[:, pl.ds(pl.multiple_of(t * share, HEAD_WIDTH), share)],
            lambda s: wc.at[pl.ds(pl.multiple_of(s * depth, depth), depth)])


def begin_kernel(n, n_z, x_ref, gain_ref, place_ref, wqkv_ref, n1_ref, wc_ref, places_ref,
                 own, s_x, r_x, s_g, s_p, r_p):
    at = Place(n, n_z)
    rows = x_ref.shape[0]
    at.greet(False)
    weights = Exchange(at, qkv_pieces(at, wqkv_ref, wc_ref, QUERY_HEADS * HEAD_WIDTH // n), s_x, r_x)
    place = Exchange(at, [(lambda t: place_ref, lambda s: places_ref.at[s])], s_p, r_p)
    place.start()
    weights.start()

    def norm(strip):
        x = x_ref[strip].astype(F32)
        own[strip] = (x * rms_of(x) * gain_ref[...]).astype(BF)

    strips(rows, norm)
    gather = Gather(at, own, n1_ref, s_g)
    gather.start()
    gather.forward()
    gather.wait()
    place.wait()
    weights.wait()


def middle_kernel(n, n_z, part_ref, x_ref, gain_ref, g_ref, gate_ref, up_ref, down_ref,
                  h_ref, n2_ref, gall_ref, gate_c, up_c, down_c,
                  near, mine, far, own, s_r, s_a, s_b, s_x, r_x, s_y, r_y):
    at = Place(n, n_z)
    share = gate_c.shape[1]
    at.greet(False)
    total = ScatterSum(at, part_ref, near, mine, far, s_r)
    total.start()
    total.forward()
    first = Exchange(at, [col_piece(gate_ref, gate_c, share), col_piece(up_ref, up_c, share)], s_x, r_x)
    second = Exchange(at, [col_piece(down_ref, down_c, share)], s_y, r_y)
    first.start()
    total.wait()

    def norm(strip):
        h = x_ref[strip].astype(F32) + total.total(strip)
        h_ref[strip] = h
        own[strip] = (h * rms_of(h) * gain_ref[...]).astype(BF)

    strips(x_ref.shape[0], norm)
    n2 = Gather(at, own, n2_ref, s_a)
    g_all = Gather(at, g_ref, gall_ref, s_b)
    n2.start()
    g_all.start()
    second.start()
    n2.forward()
    g_all.forward()
    n2.wait()
    g_all.wait()
    first.wait()
    second.wait()


def dot(left, right):
    return jnp.dot(left, right, preferred_element_type=F32)


def dot_rows(left, right):
    return lax.dot_general(left, right, (((0,), (0,)), ((), ())), preferred_element_type=F32)


def dot_cols(left, right):
    return lax.dot_general(left, right, (((1,), (1,)), ((), ())), preferred_element_type=F32)


def rope_tables(positions):
    half_size = HEAD_WIDTH // 2
    steps_up = jnp.arange(half_size, dtype=F32)
    inverse = ROPE_BASE ** (-(2.0 * steps_up) / HEAD_WIDTH)
    angles = positions.astype(F32)[:, None] * inverse[None, :]
    return jnp.cos(angles), jnp.sin(angles)


def rotate(values, cosine, sine):
    half_size = HEAD_WIDTH // 2
    first, second = values[..., :half_size], values[..., half_size:]
    return jnp.concatenate([first * cosine - second * sine, second * cosine + first * sine], axis=-1)


def norm_back(d_normed, normed, rms):
    return rms * (d_normed - normed * jnp.mean(d_normed * normed, axis=-1, keepdims=True))


class Feed:
    def __init__(self, at, grads, chunk, send, recv):
        self.at, self.grads, self.chunk, self.send, self.recv = at, grads, chunk, send, recv
        self.depth = chunk.shape[1]

    def rows(self, grad, t):
        return grad.at[pl.ds(pl.multiple_of(t * self.depth, self.depth), self.depth)]

    def copy(self, grad, c, j):
        to = self.at.near(j)
        return remote(self.rows(grad, to), self.chunk.at[c], self.send.at[c], self.recv.at[c], "fsdp", to)

    def start(self, c):
        n = self.at.n
        j = lax.rem(c, n)
        for i, grad in enumerate(self.grads):
            @pl.when((c // n == i) & (j == 0))
            def _(grad=grad):
                pltpu.make_async_copy(self.rows(grad, self.at.f), self.chunk.at[c], self.recv.at[c]).start()

            @pl.when((c // n == i) & (j > 0))
            def _(grad=grad):
                self.copy(grad, c, j).start()

    def settle(self):
        def step(c, carry):
            @pl.when(lax.rem(c, self.at.n) > 0)
            def _():
                self.copy(self.grads[0], c, lax.rem(c, self.at.n)).wait_send()

            return carry

        lax.fori_loop(0, len(self.grads) * self.at.n, step, 0)


def start_all(copies):
    for c in copies:
        c.start()


def rotate_with(values, cosine, sine):
    return values * cosine + pltpu.roll(values, HEAD_WIDTH // 2, 1) * sine


def rotation_table():
    places = HEAD_WIDTH * -(-LMAX // HEAD_WIDTH)
    inverse = ROPE_BASE ** (-(2.0 * np.arange(HEAD_WIDTH // 2)) / HEAD_WIDTH)
    angles = np.arange(places)[:, None] * inverse[None, :]
    cosine, sine = np.cos(angles), np.sin(angles)
    rest = np.concatenate([cosine, cosine, -sine, sine], axis=1).astype(np.float32)
    terms = []
    for _ in range(3):
        terms.append(rest.astype(jnp.bfloat16))
        rest = rest - terms[-1].astype(np.float32)
    return jnp.asarray(np.stack(terms))


def rotation_of(places, table):
    lane = lax.broadcasted_iota(jnp.int32, (places.shape[0], table.shape[1]), 1).astype(F32)
    pick = (lane == places.astype(F32)[:, :1]).astype(F32).astype(BF)
    both = dot(pick, table[0]) + dot(pick, table[1]) + dot(pick, table[2])
    return both[:, :HEAD_WIDTH], both[:, HEAD_WIDTH:]


def window_mask(places, rows, halo):
    i_at = lax.broadcasted_iota(jnp.int32, (rows, halo + rows), 0) + halo
    j_at = lax.broadcasted_iota(jnp.int32, (rows, halo + rows), 1)
    back = (i_at - j_at).astype(F32)
    return (back >= 0) & (back <= places.astype(F32)[:, :1])


def softmax_of(queries, keys, mask):
    scores = jnp.where(mask, dot_cols(queries, keys) * HEAD_WIDTH ** (-0.5), NEG_FILL)
    terms = jnp.exp(scores - jnp.max(scores, axis=1, keepdims=True))
    return terms / jnp.sum(terms, axis=1, keepdims=True)


def back_kernel(n, n_z, part_ref, party_ref, x_ref, h_ref, g_ref, gain1_ref, gain2_ref, gainq_ref, gaink_ref,
                down_ref, gate_ref, up_ref, wout_ref, wqkv_ref, q_ref, kv_ref, ctx_ref, proj_ref, table_ref, place_ref,
                n1_ref,
                dx_ref, y_ref, gains_ref, gmlp_ref, gqkv_ref, dhall_ref,
                near, mine, far, stage, own, dh, own_gain, plane_gain, line_gain, all_gain,
                chunk, ring, chunk2, ring2, dh_block, gout, d_kv, d_proj, halo_out, halo_in, n1_cols, qkv_send,
                s_r, s_a, s_p, r_p, s_q, r_q, s_c, r_c, s_z, r_z, s_o, s_c2, r_c2, s_z2, r_z2, s_o2, credit, done, s_d, s_n, s_h):
    at = Place(n, n_z)
    share, share_out = chunk.shape[2], chunk2.shape[2]
    rows, width = x_ref.shape
    depth = chunk.shape[1]
    outs = -(-width // share_out)
    heads = QUERY_HEADS // n
    qw = heads * HEAD_WIDTH
    halo = LMAX
    scale = HEAD_WIDTH ** (-0.5)
    at.greet(True)

    def mlp_place(j):
        s = at.near_from(lax.rem(j, n))
        return gmlp_ref.at[j // n, :, pl.ds(pl.multiple_of(s * share, HEAD_WIDTH), share)]

    def attn_place(j):
        return gqkv_ref.at[jnp.where(j < outs, j, outs + at.near_from(jnp.maximum(j - outs, 0)))]

    feed = Feed(at, (down_ref, gate_ref, up_ref), chunk, s_c, r_c)
    lines = Lines(
        LineSum(at, chunk, ring, r_c, s_z, r_z, credit.at[0], mlp_place, s_o, 0, feed.start),
        LineSum(at, chunk2, ring2, r_c2, s_z2, r_z2, credit.at[1], attn_place, s_o2, outs))
    sum_n2 = ScatterSum(at, part_ref, near, mine, far, s_r.at[0])
    for c in range(LEAD):
        feed.start(jnp.int32(c))
    sum_n2.start()
    lines.run(1)
    sum_n2.forward()
    lines.run(n - 3)
    sum_n2.wait()
    own_gain[...] = jnp.zeros_like(own_gain)

    def back_mlp(strip):
        d_n2 = sum_n2.total(strip)
        h = h_ref[strip]
        r2 = rms_of(h)
        u2 = h * r2
        own_gain[1:2] += jnp.sum(d_n2 * u2, axis=0, keepdims=True)
        d_h = g_ref[strip].astype(F32) + norm_back(d_n2 * gain2_ref[...], u2, r2)
        dh[strip] = d_h
        own[strip] = d_h.astype(BF)

    strips(rows, back_mlp)
    gather = Gather(at, own, dhall_ref, s_a)
    gather.start()
    lines.run(n // 2 + 1)
    gather.forward()
    lines.run(1)
    gather.wait()
    sum_y = ScatterSum(at, party_ref, near, mine, far, s_r.at[2])
    sum_y.start()
    lines.run(1)
    sum_y.forward()
    gout[...] = jnp.zeros_like(gout)

    def rows_of(g):
        return pl.ds(pl.multiple_of(g * rows, rows), rows)

    def block_of(g):
        return pltpu.make_async_copy(dhall_ref.at[rows_of(g)], dh_block, s_d.at[0])

    def attention(g):
        at_rows = rows_of(g)
        block_of(g).start()
        mask = window_mask(place_ref[at_rows], rows, halo)
        keys, values = kv_ref[g, :, :HEAD_WIDTH], kv_ref[g, :, HEAD_WIDTH:]
        cosine, sine = rotation_of(place_ref[at_rows], table_ref)
        block_of(g).wait()
        d_ctx = dot_cols(dh_block[...], wout_ref[...]).astype(BF)
        gout[:, :width] += dot_rows(ctx_ref[at_rows], dh_block[...])
        d_k = jnp.zeros((halo + rows, HEAD_WIDTH), F32)
        d_v = jnp.zeros((halo + rows, HEAD_WIDTH), F32)
        for head in range(heads):
            lanes = slice(head * HEAD_WIDTH, (head + 1) * HEAD_WIDTH)
            queries, d_c = q_ref[at_rows, lanes], d_ctx[:, lanes]
            probs = softmax_of(queries, keys, mask)
            d_v += dot_rows(probs.astype(BF), d_c)
            d_p = dot_cols(d_c, values)
            d_s = (probs * (d_p - jnp.sum(probs * d_p, axis=1, keepdims=True))).astype(BF)
            d_k += dot_rows(d_s, queries) * scale
            dq_g = rotate_with(dot(d_s, keys) * scale, cosine, -sine)
            raw = proj_ref[at_rows, lanes]
            rms = rms_of(raw)
            hat = raw * rms
            own_gain[2:3, :HEAD_WIDTH] += jnp.sum(dq_g * hat, axis=0, keepdims=True)
            d_proj[at_rows, lanes] = norm_back(dq_g * gainq_ref[...], hat, rms).astype(BF)
        halo_out[g, :, :HEAD_WIDTH] = d_k[:halo].astype(BF)
        halo_out[g, :, HEAD_WIDTH:] = d_v[:halo].astype(BF)
        d_kv[g, :, :HEAD_WIDTH] = d_k[halo:]
        d_kv[g, :, HEAD_WIDTH:] = d_v[halo:]

    lines.run(n, attention)

    not_first, not_last = at.z > 0, at.z < n_z - 1

    def halo_copy():
        return remote(halo_out, halo_in, s_h.at[0], s_h.at[1], "replica", jnp.maximum(at.z - 1, 0))

    @pl.when(not_first)
    def _():
        halo_copy().start()

    for i in range(outs):
        chunk2[i] = gout[:, i * share_out:(i + 1) * share_out].astype(BF)
    lines.run(1)
    sum_y.wait()

    def finish(strip):
        y_ref[strip] = (h_ref[strip] + sum_y.total(strip)).astype(BF)

    strips(rows, finish)
    for k in range(1, n):
        pl.semaphore_signal(done, inc=1, device_id={"fsdp": at.to(k)}, device_id_type=MESH)

    @pl.when(not_last)
    def _():
        pltpu.make_async_copy(halo_in, halo_in, s_h.at[1]).wait()

    @pl.when(jnp.logical_not(not_last))
    def _():
        halo_in[...] = jnp.zeros_like(halo_in)

    def keys_back(g):
        at_rows = rows_of(g)
        d_kv[g, rows - halo:] += halo_in[g].astype(F32)
        cosine, sine = rotation_of(place_ref[at_rows], table_ref)
        dk_g = rotate_with(d_kv[g, :, :HEAD_WIDTH], cosine, -sine)
        raw = proj_ref[at_rows, qw:qw + HEAD_WIDTH]
        rms = rms_of(raw)
        hat = raw * rms
        own_gain[2:3, HEAD_WIDTH:2 * HEAD_WIDTH] += jnp.sum(dk_g * hat, axis=0, keepdims=True)
        d_proj[at_rows, qw:qw + HEAD_WIDTH] = norm_back(dk_g * gaink_ref[...], hat, rms).astype(BF)
        d_proj[at_rows, qw + HEAD_WIDTH:] = d_kv[g, :, HEAD_WIDTH:].astype(BF)

    per_step = n // 2

    def keys_back_some(i):
        for m in range(per_step):
            keys_back(i * per_step + m)

    lines.run(2, keys_back_some)

    def cols_of(j):
        return pltpu.make_async_copy(
            n1_ref.at[:, pl.ds(pl.multiple_of(at.near(j) * depth, depth), depth)], n1_cols.at[lax.rem(j, 2)],
            s_n.at[lax.rem(j, 2)])

    own_qkv = pltpu.make_async_copy(qkv_send.at[0], chunk2.at[outs], r_c2.at[outs])

    def qkv_copy(j):
        return remote(qkv_send.at[j], chunk2.at[outs + j], s_c2.at[j], r_c2.at[outs + j], "fsdp", at.near(j))

    cols_of(0).start()

    def qkv_grad(j):
        @pl.when(j + 1 < n)
        def _():
            cols_of(j + 1).start()

        cols_of(j).wait()
        qkv_send[j] = dot_rows(n1_cols[lax.rem(j, 2)], d_proj[...]).astype(BF)

        @pl.when(j == 0)
        def _():
            own_qkv.start()

        @pl.when(j > 0)
        def _():
            qkv_copy(j).start()

    per_out = n // 4

    def qkv_grads(i):
        for m in range(per_out):
            qkv_grad(i * per_out + m)

    lines.run(4, qkv_grads)
    sum_n1 = ScatterSum(at, stage, near, mine, far, s_r.at[1], made=True)

    def n1_part(k):
        q = at.chip_at(k)
        stage[k] = dot_cols(d_proj[rows_of(2 * q + 1 - at.core)], wqkv_ref[...]).astype(BF)
        mine[k] = dot_cols(d_proj[rows_of(2 * q + at.core)], wqkv_ref[...]).astype(BF)

    lines.run(at.chips, n1_part)
    pl.semaphore_wait(done, n - 1)
    sum_n1.start()
    lines.run(1)
    sum_n1.forward()
    lines.run()
    sum_n1.wait()

    def back_attn(strip):
        d_n1 = sum_n1.total(strip)
        x = x_ref[strip].astype(F32)
        r1 = rms_of(x)
        u1 = x * r1
        own_gain[0:1] += jnp.sum(d_n1 * u1, axis=0, keepdims=True)
        dx_ref[strip] = (dh[strip] + norm_back(d_n1 * gain1_ref[...], u1, r1)).astype(BF)

    strips(rows, back_attn)
    gains = Exchange(at, [(lambda t: own_gain, lambda s: plane_gain.at[s])], s_p, r_p)
    gains.start()
    gains.wait()
    line_gain[...] = jnp.sum(plane_gain[...], axis=0)
    others = [
        remote(line_gain, all_gain.at[at.z], s_q.at[k], r_q.at[k], "replica", at.plane(k)) for k in range(1, n_z)]
    start_all(others)
    all_gain[at.z] = line_gain[...]
    for c in others:
        c.wait()
    gains_ref[...] = jnp.sum(all_gain[...], axis=0)
    feed.settle()
    for j in range(1, n):
        qkv_copy(j).wait_send()

    @pl.when(not_first)
    def _():
        halo_copy().wait_send()

    lines.settle()


def begin(n, n_z, x, gain, place, w_qkv):
    rows, width = x.shape
    total, wide = n * rows, (QUERY_HEADS // n + 2) * HEAD_WIDTH
    return pl.pallas_call(
        functools.partial(begin_kernel, n, n_z),
        out_shape=(
            jax.ShapeDtypeStruct((total, width), BF),
            jax.ShapeDtypeStruct((width, wide), BF),
            jax.ShapeDtypeStruct((n,) + place.shape, place.dtype),
        ),
        in_specs=[VMEM, VMEM, ANY, ANY],
        out_specs=(ANY, ANY, ANY),
        scratch_shapes=[
            pltpu.VMEM((rows, width), BF), DMA((3, n)), DMA((3, n)), DMA((6, n)), DMA((1, n)), DMA((1, n))],
        compiler_params=pltpu.CompilerParams(collective_id=0, has_side_effects=True, vmem_limit_bytes=32 << 20),
        name="begin",
    )(x, gain, place, w_qkv)


def middle(n, n_z, part, x, gain, g, gate, up, down):
    rows, width = x.shape
    total, share, chips = n * rows, gate.shape[1] // n, n // 2
    columns = jax.ShapeDtypeStruct((width, share), BF)
    return pl.pallas_call(
        functools.partial(middle_kernel, n, n_z),
        out_shape=(
            jax.ShapeDtypeStruct((rows, width), F32),
            jax.ShapeDtypeStruct((total, width), BF),
            jax.ShapeDtypeStruct((total, width), BF),
            columns, columns, columns,
        ),
        in_specs=[ANY, VMEM, VMEM, ANY, ANY, ANY, ANY],
        out_specs=(VMEM, ANY, ANY, ANY, ANY, ANY),
        scratch_shapes=[
            pltpu.VMEM((chips, rows, width), BF), pltpu.VMEM((chips, rows, width), BF),
            pltpu.VMEM((chips - 1, rows, width), BF), pltpu.VMEM((rows, width), BF),
            DMA((5, n)), DMA((6, n)), DMA((6, n)), DMA((2, n)), DMA((2, n)), DMA((1, n)), DMA((1, n))],
        compiler_params=pltpu.CompilerParams(collective_id=1, has_side_effects=True, vmem_limit_bytes=48 << 20),
        name="middle",
    )(part, x, gain, g, gate, up, down)


def back(n, n_z, part, part_y, x, h, g, gain1, gain2, gain_q, gain_k, down, gate, up, w_out, w_qkv, q, kv, ctx, proj,
         table, places, n1):
    rows, width = x.shape
    chips, share, wide, depth = n // 2, down.shape[1], w_qkv.shape[1], width // n
    outs = -(-width // wide)
    block = functools.partial(pltpu.VMEM, dtype=BF)
    gains = (8, width)
    count2 = outs + n
    return pl.pallas_call(
        functools.partial(back_kernel, n, n_z),
        out_shape=(
            jax.ShapeDtypeStruct((rows, width), BF),
            jax.ShapeDtypeStruct((rows, width), BF),
            jax.ShapeDtypeStruct(gains, F32),
            jax.ShapeDtypeStruct((3, depth, n * share), BF),
            jax.ShapeDtypeStruct((count2, depth, wide), BF),
            jax.ShapeDtypeStruct((n * rows, width), BF),
        ),
        in_specs=[ANY, ANY] + [VMEM] * 7 + [ANY] * 3 + [VMEM] * 8 + [ANY],
        out_specs=(VMEM, VMEM, VMEM, ANY, ANY, ANY),
        scratch_shapes=[
            block((chips, rows, width)), block((chips, rows, width)), block((chips - 1, rows, width)),
            block((chips, rows, width)), block((rows, width)), pltpu.VMEM((rows, width), F32),
            pltpu.VMEM(gains, F32), pltpu.VMEM((n,) + gains, F32), pltpu.VMEM(gains, F32), pltpu.VMEM((n_z,) + gains, F32),
            block((3 * n, depth, share)), block((2, RING, depth, share)),
            block((count2, depth, wide)), block((2, RING, depth, wide)),
            block((rows, width)), pltpu.VMEM((depth, outs * wide), F32),
            pltpu.VMEM((n, rows, 2 * HEAD_WIDTH), F32), block((n * rows, wide)),
            block((n, LMAX, 2 * HEAD_WIDTH)), block((n, LMAX, 2 * HEAD_WIDTH)),
            block((2, n * rows, depth)), block((n, depth, wide)),
            DMA((3, 5, n)), DMA((6, n)), DMA((1, n)), DMA((1, n)), DMA((n_z,)), DMA((n_z,)),
            DMA((3 * n,)), DMA((3 * n,)), DMA((2, 3 * n)), DMA((3, 3 * n)), DMA((3 * n,)),
            DMA((n,)), DMA((count2,)), DMA((2, count2)), DMA((3, count2)), DMA((count2,)),
            pltpu.SemaphoreType.REGULAR((2,)), pltpu.SemaphoreType.REGULAR, DMA((1,)), DMA((2,)), DMA((2,))],
        compiler_params=pltpu.CompilerParams(collective_id=2, has_side_effects=True, vmem_limit_bytes=63 << 20),
        name="back",
    )(part, part_y, x, h, g, gain1, gain2, gain_q, gain_k, down, gate, up, w_out, w_qkv, q, kv, ctx, proj, table, places, n1)


def row_positions(flat_lens, ranks, first_row, count):
    earlier = (ranks[:, None] < ranks[None, :]).astype(jnp.int32)
    starts = jnp.sum(flat_lens[:, None] * earlier, axis=0)
    rows = first_row + jnp.arange(count, dtype=jnp.int32)
    begun = jnp.where(starts[None, :] <= rows[:, None], starts[None, :], 0)
    return rows - jnp.max(begun, axis=1)


def per_device(
    n_replica, tokens, cotangent, w_qkv, w_out, w_gate, w_up, w_down_t,
    gain_attn, gain_mlp, gain_query, gain_key, dealt_lens, seq_order,
):
    rows, width = tokens.shape
    n_fsdp = width // w_qkv.shape[0]
    q_w = QUERY_HEADS * HEAD_WIDTH
    k_w = KEY_VALUE_HEADS * HEAD_WIDTH
    replica = lax.axis_index("replica")
    shared = n_fsdp // KEY_VALUE_HEADS
    heads = QUERY_HEADS // n_fsdp
    qw = heads * HEAD_WIDTH

    pos = row_positions(dealt_lens[0].reshape(-1), seq_order[0], replica * rows, rows)
    depth = w_qkv.shape[0]
    place = jnp.zeros((8, HEAD_WIDTH), jnp.int32).reshape(-1).at[:rows].set(pos).reshape(8, HEAD_WIDTH)
    n1, w_qkv_c, places = begin(n_fsdp, n_replica, tokens, gain_attn[None], place, w_qkv)
    pos_all = places.reshape(n_fsdp, -1)[:, :rows].reshape(-1)

    total = n1.shape[0]

    proj = dot(n1, w_qkv_c)
    q_rows = proj[:, :qw].reshape(total, heads, HEAD_WIDTH)
    k_rows = proj[:, qw:qw + HEAD_WIDTH]
    v_low = proj[:, qw + HEAD_WIDTH:].astype(BF)
    rq = lax.rsqrt(jnp.mean(q_rows * q_rows, axis=2, keepdims=True) + EPSILON)
    q_hat = q_rows * rq
    rk = lax.rsqrt(jnp.mean(k_rows * k_rows, axis=1, keepdims=True) + EPSILON)
    k_hat = k_rows * rk
    cosine, sine = rope_tables(pos_all)
    q_low = rotate(q_hat * gain_query, cosine[:, None], sine[:, None]).astype(BF)
    k_low = rotate(k_hat * gain_key, cosine, sine).astype(BF)

    groups = n_fsdp
    halo = LMAX
    kv = jnp.concatenate([k_low, v_low], axis=1).reshape(groups, rows, 2 * HEAD_WIDTH)
    up_pairs = [(i, i + 1) for i in range(n_replica - 1)]
    down_pairs = [(i + 1, i) for i in range(n_replica - 1)]
    kv_before = lax.ppermute(kv[:, rows - halo:], "replica", up_pairs)
    kv_window = jnp.concatenate([kv_before, kv], axis=1)
    k_win, v_win = kv_window[..., :HEAD_WIDTH], kv_window[..., HEAD_WIDTH:]
    q_grp = q_low.reshape(groups, rows, heads, HEAD_WIDTH)
    pos_grp = pos_all.reshape(groups, rows)
    i_at = halo + jnp.arange(rows, dtype=jnp.int32)
    j_at = jnp.arange(halo + rows, dtype=jnp.int32)
    mask = (j_at[None, None, :] <= i_at[None, :, None]) & (
        j_at[None, None, :] >= i_at[None, :, None] - pos_grp[:, :, None])
    mask = mask[:, None]
    scale = HEAD_WIDTH ** (-0.5)
    scores = jnp.einsum("gqhd,gkd->ghqk", q_grp, k_win, preferred_element_type=F32) * scale
    scores = jnp.where(mask, scores, NEG_FILL)
    top = jnp.max(scores, axis=3, keepdims=True)
    terms = jnp.exp(scores - top)
    probs = terms / jnp.sum(terms, axis=3, keepdims=True)
    probs_low = probs.astype(BF)
    ctx = jnp.einsum("ghqk,gkd->gqhd", probs_low, v_win, preferred_element_type=F32)
    ctx_low = ctx.reshape(total, qw).astype(BF)
    h, n2, g_all, gate_c, up_c, down_c = middle(
        n_fsdp, n_replica, dot(ctx_low, w_out).astype(BF), tokens, gain_mlp[None], cotangent, w_gate, w_up, w_down_t)

    gate = dot(n2, gate_c)
    up = dot(n2, up_c)
    sg = jax.nn.sigmoid(gate)
    silu = gate * sg
    act = (silu * up).astype(BF)
    part_y = dot_cols(act, down_c).astype(BF)

    d_act = dot(g_all, down_c)
    d_gate = (d_act * up * sg * (1.0 + gate * (1.0 - sg))).astype(BF)
    d_up = (d_act * silu).astype(BF)

    places = jnp.broadcast_to(pos_all.astype(BF)[:, None], (total, HEAD_WIDTH))
    input_grad, output, gains, g_mlp, g_attn, _ = back(
        n_fsdp, n_replica, (dot_cols(d_gate, gate_c) + dot_cols(d_up, up_c)).astype(BF), part_y, tokens, h, cotangent,
        gain_attn[None], gain_mlp[None], gain_query[None], gain_key[None],
        dot_rows(g_all, act).astype(BF), dot_rows(n2, d_gate).astype(BF), dot_rows(n2, d_up).astype(BF),
        w_out, w_qkv_c, q_low.reshape(total, qw), kv_window, ctx_low, proj[:, :qw + HEAD_WIDTH],
        rotation_table(), places, n1)
    outs = g_attn.shape[0] - n_fsdp
    g_out = g_attn[:outs].transpose(1, 0, 2).reshape(depth, -1)[:, :width]
    g_qkv = g_attn[outs:].transpose(1, 0, 2).astype(F32)

    def of_key_heads(part):
        return jnp.sum(part.reshape(depth, KEY_VALUE_HEADS, shared, HEAD_WIDTH), axis=2).reshape(depth, k_w)

    g_qkv = jnp.concatenate([
        g_qkv[:, :, :qw].reshape(depth, q_w),
        of_key_heads(g_qkv[:, :, qw:qw + HEAD_WIDTH]),
        of_key_heads(g_qkv[:, :, qw + HEAD_WIDTH:])], axis=1)
    return (
        output, input_grad, g_qkv, g_out.astype(F32), g_mlp[1].astype(F32), g_mlp[2].astype(F32), g_mlp[0].astype(F32),
        gains[0], gains[1], gains[2, :HEAD_WIDTH], gains[2, HEAD_WIDTH:2 * HEAD_WIDTH])


def solution(mesh):
    n_replica = mesh.shape["replica"]

    def program(*args):
        return per_device(n_replica, *args)

    rows = P(("fsdp", "replica"), None)
    weight = P("fsdp", None)
    return jax.shard_map(
        program,
        mesh=mesh,
        in_specs=(rows, rows) + (weight,) * 5 + (P(),) * 4 + (P("fsdp", None, None), P("fsdp", None)),
        out_specs=(rows, rows) + (weight,) * 5 + (P(),) * 4,
        check_vma=False,
    )
```

```python
import functools

import jax
import jax.numpy as jnp
import numpy as np
from jax import lax
from jax.experimental import pallas as pl
from jax.experimental.pallas import tpu as pltpu
from jax.sharding import PartitionSpec as P

QUERY_HEADS = 16
KEY_VALUE_HEADS = 8
HEAD_WIDTH = 128
LMAX = 96

EPSILON = 1e-06
ROPE_BASE = 1000000.0
NEG_FILL = -1e30
BF = jnp.bfloat16
F32 = jnp.float32


MESH = pl.DeviceIdType.MESH
ANY = pl.BlockSpec(memory_space=pl.ANY)
VMEM = pl.BlockSpec(memory_space=pltpu.VMEM)
DMA = pltpu.SemaphoreType.DMA
STRIP = 16
LAG_MID = 2
LAG_END = 6
RING = 4
LEAD = 5


def dot(left, right):
    return jnp.dot(left, right, preferred_element_type=F32)


def dot_rows(left, right):
    return lax.dot_general(left, right, (((0,), (0,)), ((), ())), preferred_element_type=F32)


def dot_cols(left, right):
    return lax.dot_general(left, right, (((1,), (1,)), ((), ())), preferred_element_type=F32)


def norm_back(d_normed, normed, rms):
    return rms * (d_normed - normed * jnp.mean(d_normed * normed, axis=-1, keepdims=True))


class Place:
    def __init__(self, n, n_z):
        self.n, self.chips, self.n_z = n, n // 2, n_z
        self.f = lax.axis_index("fsdp")
        self.chip, self.core = self.f // 2, lax.rem(self.f, 2)
        self.sib = self.f + 1 - 2 * self.core
        self.z = lax.axis_index("replica")
        low = (self.z < n_z // 2).astype(jnp.int32)
        self.inner = self.z - 1 + 2 * low
        self.outer = self.z + 1 - 2 * low
        self.mid = (self.z == n_z // 2 - 1) | (self.z == n_z // 2)
        self.has_outer = (self.z > 0) & (self.z < n_z - 1)

    def to(self, k):
        return lax.rem(self.f + k, self.n)

    def near(self, j):
        return 2 * lax.rem(self.chip + j // 2, self.chips) + lax.rem(self.core + lax.rem(j, 2), 2)

    def near_from(self, j):
        return 2 * lax.rem(self.chip + self.chips - j // 2, self.chips) + lax.rem(self.core + lax.rem(j, 2), 2)

    def plane(self, k):
        return lax.rem(self.z + k, self.n_z)

    def chip_at(self, k):
        return lax.rem(self.chip + k, self.chips)

    def greet(self, line):
        barrier = pltpu.get_barrier_semaphore()
        for k in range(1, self.n):
            pl.semaphore_signal(barrier, inc=1, device_id={"fsdp": self.to(k)}, device_id_type=MESH)
        if line:
            for k in range(1, self.n_z):
                pl.semaphore_signal(barrier, inc=1, device_id={"replica": self.plane(k)}, device_id_type=MESH)

        pl.semaphore_wait(barrier, self.n - 1 + (self.n_z - 1 if line else 0))


def remote(src, dst, send, recv, axis, index):
    return pltpu.make_async_remote_copy(
        src_ref=src, dst_ref=dst, send_sem=send, recv_sem=recv, device_id={axis: index}, device_id_type=MESH)


def strips(rows, body):
    def step(i, carry):
        body(pl.ds(pl.multiple_of(i * STRIP, STRIP), STRIP))
        return carry

    lax.fori_loop(0, rows // STRIP, step, 0)


class Exchange:
    def __init__(self, at, pieces, send, recv):
        self.copies, self.local = [], []
        for i, (src, dst) in enumerate(pieces):
            self.local.append(pltpu.make_async_copy(src(at.f), dst(at.f), recv.at[i, 0]))
            for k in range(1, at.n):
                self.copies.append(remote(src(at.to(k)), dst(at.f), send.at[i, k], recv.at[i, k], "fsdp", at.to(k)))

    def start(self):
        for c in self.copies + self.local:
            c.start()

    def wait(self):
        for c in self.copies + self.local:
            c.wait()


class Gather:
    def __init__(self, at, own, whole, sem):
        rows = own.shape[0]

        def block(i):
            return whole.at[pl.ds(pl.multiple_of(i * rows, rows), rows)]

        self.local = pltpu.make_async_copy(own, block(at.f), sem.at[0, 0])
        self.across = [remote(own, block(at.f), sem.at[0, 1], sem.at[1, 0], "fsdp", at.sib)]
        self.far, self.on = [], []
        for k in range(1, at.chips):
            to = 2 * at.chip_at(k) + at.core
            self.far.append(remote(own, block(at.f), sem.at[2, k], sem.at[3, k], "fsdp", to))
            came = 2 * at.chip_at(at.chips - k) + at.core
            self.on.append(remote(block(came), block(came), sem.at[4, k], sem.at[5, k], "fsdp", at.sib))

    def start(self):
        for c in self.far + self.across + [self.local]:
            c.start()

    def forward(self):
        for far, on in zip(self.far, self.on):
            far.wait_recv()
            on.start()

    def wait(self):
        for c in self.far:
            c.wait_send()
        for c in self.across + self.on + [self.local]:
            c.wait()


class ScatterSum:
    def __init__(self, at, part, near, own, far, sem, made=False):
        self.at, self.part, self.near, self.own, self.far, self.sem, self.made = at, part, near, own, far, sem, made
        self.rows = own.shape[1]
        self.order = list(range(1, at.chips)) + [0]

    def block(self, i):
        return self.part.at[pl.ds(pl.multiple_of(i * self.rows, self.rows), self.rows)]

    def across(self, k):
        at = self.at
        other = self.part.at[k] if self.made else self.block(2 * at.chip_at(k) + 1 - at.core)
        return remote(other, self.near.at[k], self.sem.at[0, k], self.sem.at[1, k], "fsdp", at.sib)

    def load(self, k):
        return pltpu.make_async_copy(
            self.block(2 * self.at.chip_at(k) + self.at.core), self.own.at[k], self.sem.at[2, k])

    def send(self, k):
        at = self.at
        return remote(self.own.at[k], self.far.at[k - 1], self.sem.at[3, k], self.sem.at[4, k], "fsdp",
                      2 * at.chip_at(k) + at.core)

    def start(self):
        for k in self.order:
            self.across(k).start()
            if not self.made:
                self.load(k).start()

    def pass_on(self, k):
        self.across(k).wait()
        if not self.made:
            self.load(k).wait()

        def add(at):
            self.own[k, at] = (self.own[k, at].astype(F32) + self.near[k, at].astype(F32)).astype(BF)

        strips(self.rows, add)

        @pl.when(k > 0)
        def _():
            self.send(k).start()

    def forward(self):
        def step(i, carry):
            self.pass_on(lax.rem(i + 1, self.at.chips))
            return carry

        lax.fori_loop(0, self.at.chips, step, 0)

    def wait(self):
        for k in range(1, self.at.chips):
            self.send(k).wait()

    def total(self, at):
        out = self.own[0, at].astype(F32)
        for k in range(self.at.chips - 1):
            out += self.far[k, at].astype(F32)
        return out


class LineSum:
    def __init__(self, at, chunk, ring, arrive, send, recv, credit, out, out_sem, skip=0, feed=None):
        self.at, self.chunk, self.ring, self.arrive, self.skip = at, chunk, ring, arrive, skip
        self.send, self.recv, self.credit, self.out, self.out_sem = send, recv, credit, out, out_sem
        self.feed = feed
        self.count = chunk.shape[0]
        self.kind = at.mid.astype(jnp.int32)

    def slot(self, j):
        return lax.rem(j, RING)

    def inward(self, j):
        return remote(self.chunk.at[j], self.ring.at[self.kind, self.slot(j)], self.send.at[0, j],
                      self.recv.at[self.kind, j], "replica", self.at.inner)

    def outward(self, j, src):
        return remote(src, self.out(j), self.send.at[1, j], self.recv.at[2, j], "replica", self.at.outer)

    def keep(self, j):
        return pltpu.make_async_copy(self.chunk.at[j], self.out(j), self.out_sem.at[j])

    def take_in(self, kind, j, plane):
        here = self.ring.at[kind, self.slot(j)]
        pltpu.make_async_copy(here, here, self.recv.at[kind, j]).wait()
        self.chunk[j] = (self.chunk[j].astype(F32) + self.ring[kind, self.slot(j)].astype(F32)).astype(BF)

        @pl.when(j + RING < self.count)
        def _():
            pl.semaphore_signal(self.credit, inc=1, device_id={"replica": plane}, device_id_type=MESH)

    def up(self, j):
        if self.feed:
            @pl.when(j + LEAD < self.count)
            def _():
                self.feed(j + LEAD)

        @pl.when(j >= self.skip)
        def _():
            pltpu.make_async_copy(self.chunk.at[j], self.chunk.at[j], self.arrive.at[j]).wait()

        @pl.when(self.at.has_outer)
        def _():
            self.take_in(0, j, self.at.outer)

        @pl.when(j >= RING)
        def _():
            pl.semaphore_wait(self.credit, 1)

        self.inward(j).start()

    def meet(self, j):
        self.inward(j).wait_send()
        self.take_in(1, j, self.at.inner)

        @pl.when(self.at.has_outer)
        def _():
            self.outward(j, self.chunk.at[j]).start()

        self.keep(j).start()

    def take(self, j):
        pltpu.make_async_copy(self.out(j), self.out(j), self.recv.at[2, j]).wait()

        @pl.when(self.at.has_outer)
        def _():
            self.outward(j, self.out(j)).start()

    def settle(self):
        def step(j, carry):
            @pl.when(self.at.mid)
            def _():
                self.keep(j).wait()

            @pl.when(jnp.logical_not(self.at.mid))
            def _():
                self.inward(j).wait_send()

            @pl.when(self.at.has_outer)
            def _():
                self.outward(j, self.chunk.at[j]).wait_send()

            return carry

        lax.fori_loop(0, self.count, step, 0)


class Lines:
    def __init__(self, *lines):
        self.lines = lines
        self.order = [(i, j) for i, line in enumerate(lines) for j in range(line.count)]
        self.at = 0

    def run(self, steps=None, body=None):
        begin = self.at
        last = len(self.order) + LAG_END
        stop = last if steps is None else min(self.at + steps, len(self.order))
        while self.at < stop:
            first, size = self.at, 1
            now = self.parts(first)
            while first + size < stop and self.kinds(first + size) == self.kinds(first):
                size += 1

            def step(m, carry, now=now, first=first):
                up, mid, rest = now
                if up:
                    self.lines[up[0]].up(up[1] + m)
                if mid:
                    @pl.when(self.lines[mid[0]].at.mid)
                    def _():
                        self.lines[mid[0]].meet(mid[1] + m)
                if rest:
                    @pl.when(jnp.logical_not(self.lines[rest[0]].at.mid))
                    def _():
                        self.lines[rest[0]].take(rest[1] + m)
                if body:
                    body(first - begin + m)
                return carry

            lax.fori_loop(0, size, step, 0)
            self.at += size

    def parts(self, t):
        return [self.order[i] if 0 <= i < len(self.order) else None for i in (t, t - LAG_MID, t - LAG_END)]

    def kinds(self, t):
        return [part and part[0] for part in self.parts(t)]

    def settle(self):
        for line in self.lines:
            line.settle()


def rms_of(values):
    return lax.rsqrt(jnp.mean(values * values, axis=-1, keepdims=True) + EPSILON)


def qkv_pieces(at, w, wc, qw):
    q_w, k_w = QUERY_HEADS * HEAD_WIDTH, KEY_VALUE_HEADS * HEAD_WIDTH
    shared = at.n // KEY_VALUE_HEADS
    depth = w.shape[0]

    def cols(start, width):
        return pl.ds(pl.multiple_of(start, HEAD_WIDTH), width)

    def rows(s):
        return pl.ds(pl.multiple_of(s * depth, depth), depth)

    return [
        (lambda t: w.at[:, cols(t * qw, qw)], lambda s: wc.at[rows(s), pl.ds(0, qw)]),
        (lambda t: w.at[:, cols(q_w + t // shared * HEAD_WIDTH, HEAD_WIDTH)],
         lambda s: wc.at[rows(s), pl.ds(qw, HEAD_WIDTH)]),
        (lambda t: w.at[:, cols(q_w + k_w + t // shared * HEAD_WIDTH, HEAD_WIDTH)],
         lambda s: wc.at[rows(s), pl.ds(qw + HEAD_WIDTH, HEAD_WIDTH)]),
    ]


def col_piece(w, wc, share):
    depth = w.shape[0]
    return (lambda t: w.at[:, pl.ds(pl.multiple_of(t * share, HEAD_WIDTH), share)],
            lambda s: wc.at[pl.ds(pl.multiple_of(s * depth, depth), depth)])


class Weights:
    def __init__(self, at, pairs, send, recv, z_send, z_recv):
        self.at, self.pairs, self.send, self.recv, self.z_send, self.z_recv = at, pairs, send, recv, z_send, z_recv
        self.depth, self.share = pairs[0][0].shape[0], pairs[0][1].shape[1]
        self.mine = at.core == lax.rem(at.z, 2)
        self.parity = lax.rem(at.z + at.core, 2)
        self.partner = at.z + 1 - 2 * lax.rem(at.z, 2)

    def cols(self, i, t):
        return self.pairs[i][0].at[:, pl.ds(pl.multiple_of(t * self.share, HEAD_WIDTH), self.share)]

    def rows(self, i, s):
        return self.pairs[i][1].at[pl.ds(pl.multiple_of(s * self.depth, self.depth), self.depth)]

    def local(self, i):
        return pltpu.make_async_copy(self.cols(i, self.at.f), self.rows(i, self.at.f), self.recv.at[i, 0])

    def copy(self, i, j):
        to = self.at.near(j)
        return remote(self.cols(i, to), self.rows(i, self.at.f), self.send.at[i, j], self.recv.at[i, j], "fsdp", to)

    def beside(self, i, j):
        here = self.rows(i, self.at.near_from(j))
        return remote(here, here, self.z_send.at[i, j], self.z_recv.at[i, j], "replica", self.partner)

    def start(self, i):
        self.local(i).start()
        self.copy(i, 1).start()

        @pl.when(self.mine)
        def _():
            for j in range(2, self.at.n):
                self.copy(i, j).start()

    def hand_over(self, i):
        for m in range(1, self.at.chips):
            j = 2 * m + self.parity
            here = self.rows(i, self.at.near_from(j))
            pltpu.make_async_copy(here, here, self.recv.at[i, j]).wait()
            self.beside(i, j).start()

    def wait(self, i):
        self.local(i).wait()
        self.copy(i, 1).wait()

        @pl.when(self.mine)
        def _():
            for j in range(2, self.at.n):
                self.copy(i, j).wait_send()

        for m in range(1, self.at.chips):
            self.beside(i, 2 * m + self.parity).wait_send()
            self.beside(i, 2 * m + 1 - self.parity).wait_recv()


def front_kernel(n, n_z, x_ref, gain1_ref, gain2_ref, gainq_ref, gaink_ref, place_ref, table_ref, wout_ref,
                 wqkv_ref, g_ref, gate_ref, up_ref, down_ref,
                 h_ref, q_ref, kv_ref, ctx_ref, proj_ref, places_ref,
                 n1_ref, wc_ref, n2_ref, gall_ref, gate_c, up_c, down_c,
                 near, mine, far, stage, own, n1_block, wc,
                 s_x, r_x, s_p, r_p, s_g, s_n, s_w, s_h, s_r, s_a, s_b, s_c, r_c, s_z, r_z):
    at = Place(n, n_z)
    rows = x_ref.shape[0]
    heads = QUERY_HEADS // n
    qw = heads * HEAD_WIDTH
    halo = LMAX
    at.greet(True)
    weights = Exchange(at, qkv_pieces(at, wqkv_ref, wc_ref, qw), s_x, r_x)

    def rows_of(g):
        return pl.ds(pl.multiple_of(g * rows, rows), rows)

    places = Exchange(at, [(lambda t: place_ref, lambda s: places_ref.at[rows_of(s)])], s_p, r_p)
    mlp = Weights(at, [(gate_ref, gate_c), (up_ref, up_c), (down_ref, down_c)], s_c, r_c, s_z, r_z)
    places.start()

    def norm1(strip):
        x = x_ref[strip].astype(F32)
        own[strip] = (x * rms_of(x) * gain1_ref[...]).astype(BF)

    strips(rows, norm1)
    n1 = Gather(at, own, n1_ref, s_g)
    n1.start()
    weights.start()
    n1.forward()
    n1.wait()
    places.wait()
    weights.wait()
    mlp.start(0)
    mlp.start(1)
    to_vmem = pltpu.make_async_copy(wc_ref, wc, s_w.at[0])
    to_vmem.start()

    def block_of(g):
        return pltpu.make_async_copy(n1_ref.at[rows_of(g)], n1_block.at[lax.rem(g, 2)], s_n.at[lax.rem(g, 2)])

    block_of(0).start()
    to_vmem.wait()

    def project(g, carry):
        @pl.when(g + 1 < n)
        def _():
            block_of(g + 1).start()

        at_rows = rows_of(g)
        cosine, sine = rotation_of(places_ref[at_rows], table_ref)
        block_of(g).wait()
        proj = dot(n1_block[lax.rem(g, 2)], wc[...])
        proj_ref[at_rows] = proj[:, :qw + HEAD_WIDTH]
        for head in range(heads + 1):
            lanes = slice(head * HEAD_WIDTH, (head + 1) * HEAD_WIDTH)
            raw = proj[:, lanes]
            gain = gainq_ref if head < heads else gaink_ref
            turned = rotate_with(raw * rms_of(raw) * gain[...], cosine, sine).astype(BF)
            if head < heads:
                q_ref[at_rows, lanes] = turned
            else:
                kv_ref[g, halo:, :HEAD_WIDTH] = turned
        kv_ref[g, halo:, HEAD_WIDTH:] = proj[:, qw + HEAD_WIDTH:].astype(BF)
        return carry

    lax.fori_loop(0, n, project, 0)
    not_first, not_last = at.z > 0, at.z < n_z - 1

    def halo_copy():
        return remote(kv_ref.at[:, pl.ds(rows, halo)], kv_ref.at[:, pl.ds(0, halo)], s_h.at[0], s_h.at[1], "replica",
                      jnp.minimum(at.z + 1, n_z - 1))

    @pl.when(not_last)
    def _():
        halo_copy().start()

    @pl.when(not_first)
    def _():
        here = kv_ref.at[:, pl.ds(0, halo)]
        pltpu.make_async_copy(here, here, s_h.at[1]).wait()

    @pl.when(jnp.logical_not(not_first))
    def _():
        kv_ref[:, :halo] = jnp.zeros((n, halo, 2 * HEAD_WIDTH), BF)

    sum_o = ScatterSum(at, stage, near, mine, far, s_r, made=True)

    def attend(g):
        at_rows = rows_of(g)
        mask = window_mask(places_ref[at_rows], rows, halo)
        keys, values = kv_ref[g, :, :HEAD_WIDTH], kv_ref[g, :, HEAD_WIDTH:]
        for head in range(heads):
            lanes = slice(head * HEAD_WIDTH, (head + 1) * HEAD_WIDTH)
            probs = softmax_of(q_ref[at_rows, lanes], keys, mask).astype(BF)
            ctx_ref[at_rows, lanes] = dot(probs, values).astype(BF)
        return dot(ctx_ref[at_rows], wout_ref[...]).astype(BF)

    def attend_both(i, carry):
        k = lax.rem(i + 1, at.chips)
        q = at.chip_at(k)
        stage[k] = attend(2 * q + 1 - at.core)
        sum_o.across(k).start()
        mine[k] = attend(2 * q + at.core)

        @pl.when(i > 0)
        def _():
            sum_o.pass_on(jnp.maximum(i, 1))

        return carry

    lax.fori_loop(0, at.chips, attend_both, 0)
    sum_o.pass_on(0)
    mlp.start(2)
    mlp.hand_over(0)
    sum_o.wait()

    def norm2(strip):
        h = x_ref[strip].astype(F32) + sum_o.total(strip)
        h_ref[strip] = h
        own[strip] = (h * rms_of(h) * gain2_ref[...]).astype(BF)

    strips(rows, norm2)
    n2 = Gather(at, own, n2_ref, s_a)
    g_all = Gather(at, g_ref, gall_ref, s_b)
    n2.start()
    mlp.hand_over(1)
    g_all.start()
    n2.forward()
    mlp.hand_over(2)
    g_all.forward()
    n2.wait()
    g_all.wait()

    @pl.when(not_last)
    def _():
        halo_copy().wait_send()

    for i in range(3):
        mlp.wait(i)


class Feed:
    def __init__(self, at, grads, chunk, send, recv):
        self.at, self.grads, self.chunk, self.send, self.recv = at, grads, chunk, send, recv
        self.depth = chunk.shape[1]

    def rows(self, grad, t):
        return grad.at[pl.ds(pl.multiple_of(t * self.depth, self.depth), self.depth)]

    def copy(self, grad, c, j):
        to = self.at.near(j)
        return remote(self.rows(grad, to), self.chunk.at[c], self.send.at[c], self.recv.at[c], "fsdp", to)

    def start(self, c):
        n = self.at.n
        j = lax.rem(c, n)
        for i, grad in enumerate(self.grads):
            @pl.when((c // n == i) & (j == 0))
            def _(grad=grad):
                pltpu.make_async_copy(self.rows(grad, self.at.f), self.chunk.at[c], self.recv.at[c]).start()

            @pl.when((c // n == i) & (j > 0))
            def _(grad=grad):
                self.copy(grad, c, j).start()

    def settle(self):
        def step(c, carry):
            @pl.when(lax.rem(c, self.at.n) > 0)
            def _():
                self.copy(self.grads[0], c, lax.rem(c, self.at.n)).wait_send()

            return carry

        lax.fori_loop(0, len(self.grads) * self.at.n, step, 0)


def start_all(copies):
    for c in copies:
        c.start()


def rotate_with(values, cosine, sine):
    return values * cosine + pltpu.roll(values, HEAD_WIDTH // 2, 1) * sine


def rotation_table():
    places = HEAD_WIDTH * -(-LMAX // HEAD_WIDTH)
    inverse = ROPE_BASE ** (-(2.0 * np.arange(HEAD_WIDTH // 2)) / HEAD_WIDTH)
    angles = np.arange(places)[:, None] * inverse[None, :]
    cosine, sine = np.cos(angles), np.sin(angles)
    rest = np.concatenate([cosine, cosine, -sine, sine], axis=1).astype(np.float32)
    terms = []
    for _ in range(3):
        terms.append(rest.astype(jnp.bfloat16))
        rest = rest - terms[-1].astype(np.float32)
    return jnp.asarray(np.stack(terms))


def rotation_of(places, table):
    lane = lax.broadcasted_iota(jnp.int32, (places.shape[0], table.shape[1]), 1).astype(F32)
    pick = (lane == places.astype(F32)[:, :1]).astype(F32).astype(BF)
    both = dot(pick, table[0]) + dot(pick, table[1]) + dot(pick, table[2])
    return both[:, :HEAD_WIDTH], both[:, HEAD_WIDTH:]


def window_mask(places, rows, halo):
    i_at = lax.broadcasted_iota(jnp.int32, (rows, halo + rows), 0) + halo
    j_at = lax.broadcasted_iota(jnp.int32, (rows, halo + rows), 1)
    back = (i_at - j_at).astype(F32)
    return (back >= 0) & (back <= places.astype(F32)[:, :1])


def softmax_of(queries, keys, mask):
    scores = jnp.where(mask, dot_cols(queries, keys) * HEAD_WIDTH ** (-0.5), NEG_FILL)
    terms = jnp.exp(scores - jnp.max(scores, axis=1, keepdims=True))
    return terms / jnp.sum(terms, axis=1, keepdims=True)


def back_kernel(n, n_z, part_ref, party_ref, x_ref, h_ref, g_ref, gain1_ref, gain2_ref, gainq_ref, gaink_ref,
                down_ref, gate_ref, up_ref, wout_ref, wqkv_ref, q_ref, kv_ref, ctx_ref, proj_ref, table_ref, place_ref,
                n1_ref,
                dx_ref, y_ref, gains_ref, gmlp_ref, gqkv_ref, dhall_ref,
                near, mine, far, stage, own, dh, own_gain, plane_gain, line_gain, all_gain,
                chunk, ring, chunk2, ring2, dh_block, gout, d_kv, d_proj, halo_out, halo_in, n1_cols, qkv_send,
                s_r, s_a, s_p, r_p, s_q, r_q, s_c, r_c, s_z, r_z, s_o, s_c2, r_c2, s_z2, r_z2, s_o2, credit, done, s_d, s_n, s_h):
    at = Place(n, n_z)
    share, share_out = chunk.shape[2], chunk2.shape[2]
    rows, width = x_ref.shape
    depth = chunk.shape[1]
    outs = -(-width // share_out)
    heads = QUERY_HEADS // n
    qw = heads * HEAD_WIDTH
    halo = LMAX
    scale = HEAD_WIDTH ** (-0.5)
    at.greet(True)

    def mlp_place(j):
        s = at.near_from(lax.rem(j, n))
        return gmlp_ref.at[j // n, :, pl.ds(pl.multiple_of(s * share, HEAD_WIDTH), share)]

    def attn_place(j):
        col = jnp.where(j < outs, j, outs + at.near_from(jnp.maximum(j - outs, 0)))
        return gqkv_ref.at[:, pl.ds(pl.multiple_of(col * share_out, HEAD_WIDTH), share_out)]

    feed = Feed(at, (down_ref, gate_ref, up_ref), chunk, s_c, r_c)
    lines = Lines(
        LineSum(at, chunk, ring, r_c, s_z, r_z, credit.at[0], mlp_place, s_o, 0, feed.start),
        LineSum(at, chunk2, ring2, r_c2, s_z2, r_z2, credit.at[1], attn_place, s_o2, outs))
    sum_n2 = ScatterSum(at, part_ref, near, mine, far, s_r.at[0])
    for c in range(LEAD):
        feed.start(jnp.int32(c))
    sum_n2.start()
    lines.run(1)
    sum_n2.forward()
    lines.run(n - 3)
    sum_n2.wait()
    own_gain[...] = jnp.zeros_like(own_gain)

    def back_mlp(strip):
        d_n2 = sum_n2.total(strip)
        h = h_ref[strip]
        r2 = rms_of(h)
        u2 = h * r2
        own_gain[1:2] += jnp.sum(d_n2 * u2, axis=0, keepdims=True)
        d_h = g_ref[strip].astype(F32) + norm_back(d_n2 * gain2_ref[...], u2, r2)
        dh[strip] = d_h
        own[strip] = d_h.astype(BF)

    strips(rows, back_mlp)
    gather = Gather(at, own, dhall_ref, s_a)
    gather.start()
    lines.run(n // 2 + 1)
    gather.forward()
    lines.run(1)
    gather.wait()
    sum_y = ScatterSum(at, party_ref, near, mine, far, s_r.at[2])
    sum_y.start()
    lines.run(1)
    sum_y.forward()
    gout[...] = jnp.zeros_like(gout)

    def rows_of(g):
        return pl.ds(pl.multiple_of(g * rows, rows), rows)

    def block_of(g):
        return pltpu.make_async_copy(dhall_ref.at[rows_of(g)], dh_block, s_d.at[0])

    def attention(g):
        at_rows = rows_of(g)
        block_of(g).start()
        mask = window_mask(place_ref[at_rows], rows, halo)
        keys, values = kv_ref[g, :, :HEAD_WIDTH], kv_ref[g, :, HEAD_WIDTH:]
        cosine, sine = rotation_of(place_ref[at_rows], table_ref)
        block_of(g).wait()
        d_ctx = dot_cols(dh_block[...], wout_ref[...]).astype(BF)
        gout[:, :width] += dot_rows(ctx_ref[at_rows], dh_block[...])
        d_k = jnp.zeros((halo + rows, HEAD_WIDTH), F32)
        d_v = jnp.zeros((halo + rows, HEAD_WIDTH), F32)
        for head in range(heads):
            lanes = slice(head * HEAD_WIDTH, (head + 1) * HEAD_WIDTH)
            queries, d_c = q_ref[at_rows, lanes], d_ctx[:, lanes]
            probs = softmax_of(queries, keys, mask)
            d_v += dot_rows(probs.astype(BF), d_c)
            d_p = dot_cols(d_c, values)
            d_s = (probs * (d_p - jnp.sum(probs * d_p, axis=1, keepdims=True))).astype(BF)
            d_k += dot_rows(d_s, queries) * scale
            dq_g = rotate_with(dot(d_s, keys) * scale, cosine, -sine)
            raw = proj_ref[at_rows, lanes]
            rms = rms_of(raw)
            hat = raw * rms
            own_gain[2:3, :HEAD_WIDTH] += jnp.sum(dq_g * hat, axis=0, keepdims=True)
            d_proj[at_rows, lanes] = norm_back(dq_g * gainq_ref[...], hat, rms).astype(BF)
        halo_out[g, :, :HEAD_WIDTH] = d_k[:halo].astype(BF)
        halo_out[g, :, HEAD_WIDTH:] = d_v[:halo].astype(BF)
        d_kv[g, :, :HEAD_WIDTH] = d_k[halo:]
        d_kv[g, :, HEAD_WIDTH:] = d_v[halo:]

    lines.run(n, attention)

    not_first, not_last = at.z > 0, at.z < n_z - 1

    def halo_copy():
        return remote(halo_out, halo_in, s_h.at[0], s_h.at[1], "replica", jnp.maximum(at.z - 1, 0))

    @pl.when(not_first)
    def _():
        halo_copy().start()

    for i in range(outs):
        chunk2[i] = gout[:, i * share_out:(i + 1) * share_out].astype(BF)
    lines.run(1)
    sum_y.wait()

    def finish(strip):
        y_ref[strip] = (h_ref[strip] + sum_y.total(strip)).astype(BF)

    strips(rows, finish)
    for k in range(1, n):
        pl.semaphore_signal(done, inc=1, device_id={"fsdp": at.to(k)}, device_id_type=MESH)

    @pl.when(not_last)
    def _():
        pltpu.make_async_copy(halo_in, halo_in, s_h.at[1]).wait()

    @pl.when(jnp.logical_not(not_last))
    def _():
        halo_in[...] = jnp.zeros_like(halo_in)

    def keys_back(g):
        at_rows = rows_of(g)
        d_kv[g, rows - halo:] += halo_in[g].astype(F32)
        cosine, sine = rotation_of(place_ref[at_rows], table_ref)
        dk_g = rotate_with(d_kv[g, :, :HEAD_WIDTH], cosine, -sine)
        raw = proj_ref[at_rows, qw:qw + HEAD_WIDTH]
        rms = rms_of(raw)
        hat = raw * rms
        own_gain[2:3, HEAD_WIDTH:2 * HEAD_WIDTH] += jnp.sum(dk_g * hat, axis=0, keepdims=True)
        d_proj[at_rows, qw:qw + HEAD_WIDTH] = norm_back(dk_g * gaink_ref[...], hat, rms).astype(BF)
        d_proj[at_rows, qw + HEAD_WIDTH:] = d_kv[g, :, HEAD_WIDTH:].astype(BF)

    per_step = n // 2

    def keys_back_some(i):
        for m in range(per_step):
            keys_back(i * per_step + m)

    lines.run(2, keys_back_some)

    def cols_of(j):
        return pltpu.make_async_copy(
            n1_ref.at[:, pl.ds(pl.multiple_of(at.near(j) * depth, depth), depth)], n1_cols.at[lax.rem(j, 2)],
            s_n.at[lax.rem(j, 2)])

    own_qkv = pltpu.make_async_copy(qkv_send.at[0], chunk2.at[outs], r_c2.at[outs])

    def qkv_copy(j):
        return remote(qkv_send.at[j], chunk2.at[outs + j], s_c2.at[j], r_c2.at[outs + j], "fsdp", at.near(j))

    cols_of(0).start()

    def qkv_grad(j):
        @pl.when(j + 1 < n)
        def _():
            cols_of(j + 1).start()

        cols_of(j).wait()
        qkv_send[j] = dot_rows(n1_cols[lax.rem(j, 2)], d_proj[...]).astype(BF)

        @pl.when(j == 0)
        def _():
            own_qkv.start()

        @pl.when(j > 0)
        def _():
            qkv_copy(j).start()

    per_out = n // 4

    def qkv_grads(i):
        for m in range(per_out):
            qkv_grad(i * per_out + m)

    lines.run(4, qkv_grads)
    sum_n1 = ScatterSum(at, stage, near, mine, far, s_r.at[1], made=True)

    def n1_part(k):
        q = at.chip_at(k)
        stage[k] = dot_cols(d_proj[rows_of(2 * q + 1 - at.core)], wqkv_ref[...]).astype(BF)
        mine[k] = dot_cols(d_proj[rows_of(2 * q + at.core)], wqkv_ref[...]).astype(BF)

    lines.run(at.chips, n1_part)
    pl.semaphore_wait(done, n - 1)
    sum_n1.start()
    lines.run(1)
    sum_n1.forward()
    lines.run()
    sum_n1.wait()

    def back_attn(strip):
        d_n1 = sum_n1.total(strip)
        x = x_ref[strip].astype(F32)
        r1 = rms_of(x)
        u1 = x * r1
        own_gain[0:1] += jnp.sum(d_n1 * u1, axis=0, keepdims=True)
        dx_ref[strip] = (dh[strip] + norm_back(d_n1 * gain1_ref[...], u1, r1)).astype(BF)

    strips(rows, back_attn)
    gains = Exchange(at, [(lambda t: own_gain, lambda s: plane_gain.at[s])], s_p, r_p)
    gains.start()
    gains.wait()
    line_gain[...] = jnp.sum(plane_gain[...], axis=0)
    others = [
        remote(line_gain, all_gain.at[at.z], s_q.at[k], r_q.at[k], "replica", at.plane(k)) for k in range(1, n_z)]
    start_all(others)
    all_gain[at.z] = line_gain[...]
    for c in others:
        c.wait()
    gains_ref[...] = jnp.sum(all_gain[...], axis=0)
    feed.settle()
    for j in range(1, n):
        qkv_copy(j).wait_send()

    @pl.when(not_first)
    def _():
        halo_copy().wait_send()

    lines.settle()


def front(n, n_z, x, gain1, gain2, gain_q, gain_k, place, table, w_out, w_qkv, g, gate, up, down):
    rows, width = x.shape
    chips, share, total = n // 2, gate.shape[1] // n, n * rows
    qw = QUERY_HEADS * HEAD_WIDTH // n
    wide = qw + 2 * HEAD_WIDTH
    block = functools.partial(pltpu.VMEM, dtype=BF)
    shape = jax.ShapeDtypeStruct
    return pl.pallas_call(
        functools.partial(front_kernel, n, n_z),
        out_shape=(
            shape((rows, width), F32), shape((total, qw), BF), shape((n, LMAX + rows, 2 * HEAD_WIDTH), BF),
            shape((total, qw), BF), shape((total, qw + HEAD_WIDTH), F32), shape((total, HEAD_WIDTH), BF),
            shape((total, width), BF), shape((width, wide), BF), shape((total, width), BF), shape((total, width), BF),
        ) + (shape((width, share), BF),) * 3,
        in_specs=[VMEM] * 8 + [ANY] * 5,
        out_specs=(VMEM,) * 6 + (ANY,) * 7,
        scratch_shapes=[
            block((chips, rows, width)), block((chips, rows, width)), block((chips - 1, rows, width)),
            block((chips, rows, width)), block((rows, width)), block((2, rows, width)), block((width, wide)),
            DMA((3, n)), DMA((3, n)), DMA((1, n)), DMA((1, n)), DMA((6, n)), DMA((2,)), DMA((1,)), DMA((2,)),
            DMA((5, n)), DMA((6, n)), DMA((6, n)), DMA((3, n)), DMA((3, n)), DMA((3, n)), DMA((3, n))],
        compiler_params=pltpu.CompilerParams(collective_id=0, has_side_effects=True, vmem_limit_bytes=60 << 20),
        name="front",
    )(x, gain1, gain2, gain_q, gain_k, place, table, w_out, w_qkv, g, gate, up, down)


def back(n, n_z, part, part_y, x, h, g, gain1, gain2, gain_q, gain_k, down, gate, up, w_out, w_qkv, q, kv, ctx, proj,
         table, places, n1):
    rows, width = x.shape
    chips, share, wide, depth = n // 2, down.shape[1], w_qkv.shape[1], width // n
    outs = -(-width // wide)
    block = functools.partial(pltpu.VMEM, dtype=BF)
    gains = (8, width)
    count2 = outs + n
    return pl.pallas_call(
        functools.partial(back_kernel, n, n_z),
        out_shape=(
            jax.ShapeDtypeStruct((rows, width), BF),
            jax.ShapeDtypeStruct((rows, width), BF),
            jax.ShapeDtypeStruct(gains, F32),
            jax.ShapeDtypeStruct((3, depth, n * share), BF),
            jax.ShapeDtypeStruct((depth, count2 * wide), BF),
            jax.ShapeDtypeStruct((n * rows, width), BF),
        ),
        in_specs=[ANY, ANY] + [VMEM] * 7 + [ANY] * 3 + [VMEM] * 8 + [ANY],
        out_specs=(VMEM, VMEM, VMEM, ANY, ANY, ANY),
        scratch_shapes=[
            block((chips, rows, width)), block((chips, rows, width)), block((chips - 1, rows, width)),
            block((chips, rows, width)), block((rows, width)), pltpu.VMEM((rows, width), F32),
            pltpu.VMEM(gains, F32), pltpu.VMEM((n,) + gains, F32), pltpu.VMEM(gains, F32), pltpu.VMEM((n_z,) + gains, F32),
            block((3 * n, depth, share)), block((2, RING, depth, share)),
            block((count2, depth, wide)), block((2, RING, depth, wide)),
            block((rows, width)), pltpu.VMEM((depth, outs * wide), F32),
            pltpu.VMEM((n, rows, 2 * HEAD_WIDTH), F32), block((n * rows, wide)),
            block((n, LMAX, 2 * HEAD_WIDTH)), block((n, LMAX, 2 * HEAD_WIDTH)),
            block((2, n * rows, depth)), block((n, depth, wide)),
            DMA((3, 5, n)), DMA((6, n)), DMA((1, n)), DMA((1, n)), DMA((n_z,)), DMA((n_z,)),
            DMA((3 * n,)), DMA((3 * n,)), DMA((2, 3 * n)), DMA((3, 3 * n)), DMA((3 * n,)),
            DMA((n,)), DMA((count2,)), DMA((2, count2)), DMA((3, count2)), DMA((count2,)),
            pltpu.SemaphoreType.REGULAR((2,)), pltpu.SemaphoreType.REGULAR, DMA((1,)), DMA((2,)), DMA((2,))],
        compiler_params=pltpu.CompilerParams(collective_id=2, has_side_effects=True, vmem_limit_bytes=63 << 20),
        name="back",
    )(part, part_y, x, h, g, gain1, gain2, gain_q, gain_k, down, gate, up, w_out, w_qkv, q, kv, ctx, proj, table, places, n1)


def row_positions(flat_lens, ranks, first_row, count):
    earlier = (ranks[:, None] < ranks[None, :]).astype(jnp.int32)
    starts = jnp.sum(flat_lens[:, None] * earlier, axis=0)
    rows = first_row + jnp.arange(count, dtype=jnp.int32)
    begun = jnp.where(starts[None, :] <= rows[:, None], starts[None, :], 0)
    return rows - jnp.max(begun, axis=1)


def per_device(
    n_replica, tokens, cotangent, w_qkv, w_out, w_gate, w_up, w_down_t,
    gain_attn, gain_mlp, gain_query, gain_key, dealt_lens, seq_order,
):
    rows, width = tokens.shape
    n_fsdp = width // w_qkv.shape[0]
    q_w = QUERY_HEADS * HEAD_WIDTH
    k_w = KEY_VALUE_HEADS * HEAD_WIDTH
    replica = lax.axis_index("replica")
    shared = n_fsdp // KEY_VALUE_HEADS
    heads = QUERY_HEADS // n_fsdp
    qw = heads * HEAD_WIDTH

    pos = row_positions(dealt_lens[0].reshape(-1), seq_order[0], replica * rows, rows)
    depth = w_qkv.shape[0]
    place = jnp.broadcast_to(pos.astype(BF)[:, None], (rows, HEAD_WIDTH))
    table = rotation_table()
    gains = (gain_attn[None], gain_mlp[None], gain_query[None], gain_key[None])
    h, q_low, kv_window, ctx_low, proj, places, n1, w_qkv_c, n2, g_all, gate_c, up_c, down_c = front(
        n_fsdp, n_replica, tokens, *gains, place, table, w_out, w_qkv, cotangent, w_gate, w_up, w_down_t)

    gate = dot(n2, gate_c)
    up = dot(n2, up_c)
    sg = jax.nn.sigmoid(gate)
    silu = gate * sg
    act = (silu * up).astype(BF)
    part_y = dot_cols(act, down_c).astype(BF)

    d_act = dot(g_all, down_c)
    d_gate = (d_act * up * sg * (1.0 + gate * (1.0 - sg))).astype(BF)
    d_up = (d_act * silu).astype(BF)

    input_grad, output, gain_sums, g_mlp, g_attn, _ = back(
        n_fsdp, n_replica, (dot_cols(d_gate, gate_c) + dot_cols(d_up, up_c)).astype(BF), part_y, tokens, h, cotangent, *gains,
        dot_rows(g_all, act).astype(BF), dot_rows(n2, d_gate).astype(BF), dot_rows(n2, d_up).astype(BF),
        w_out, w_qkv_c, q_low, kv_window, ctx_low, proj, table, places, n1)
    wide = qw + 2 * HEAD_WIDTH
    g_out = g_attn[:, :width]
    by_device = [g_attn[:, at:at + wide] for at in range(g_attn.shape[1] - n_fsdp * wide, g_attn.shape[1], wide)]

    def of_key_heads(first):
        parts = [part[:, first:first + HEAD_WIDTH].astype(F32) for part in by_device]
        return [sum(parts[i + 1:i + shared], parts[i]) for i in range(0, n_fsdp, shared)]

    g_qkv = jnp.concatenate(
        [part[:, :qw].astype(F32) for part in by_device] + of_key_heads(qw) + of_key_heads(qw + HEAD_WIDTH), axis=1)
    return (
        output, input_grad, g_qkv, g_out.astype(F32), g_mlp[1].astype(F32), g_mlp[2].astype(F32), g_mlp[0].astype(F32),
        gain_sums[0], gain_sums[1], gain_sums[2, :HEAD_WIDTH], gain_sums[2, HEAD_WIDTH:2 * HEAD_WIDTH])


def solution(mesh):
    n_replica = mesh.shape["replica"]

    def program(*args):
        return per_device(n_replica, *args)

    rows = P(("fsdp", "replica"), None)
    weight = P("fsdp", None)
    return jax.shard_map(
        program,
        mesh=mesh,
        in_specs=(rows, rows) + (weight,) * 5 + (P(),) * 4 + (P("fsdp", None, None), P("fsdp", None)),
        out_specs=(rows, rows) + (weight,) * 5 + (P(),) * 4,
        check_vma=False,
    )
```

```python
import functools

import jax
import jax.numpy as jnp
import numpy as np
from jax import lax
from jax.experimental import pallas as pl
from jax.experimental.pallas import tpu as pltpu
from jax.sharding import PartitionSpec as P

QUERY_HEADS = 16
KEY_VALUE_HEADS = 8
HEAD_WIDTH = 128
LMAX = 96

EPSILON = 1e-06
ROPE_BASE = 1000000.0
NEG_FILL = -1e30
BF = jnp.bfloat16
F32 = jnp.float32


MESH = pl.DeviceIdType.MESH
ANY = pl.BlockSpec(memory_space=pl.ANY)
VMEM = pl.BlockSpec(memory_space=pltpu.VMEM)
DMA = pltpu.SemaphoreType.DMA
STRIP = 16
LAG_MID = 2
LAG_END = 6
LEAD = 5


def dot(left, right):
    return jnp.dot(left, right, preferred_element_type=F32)


def dot_rows(left, right):
    return lax.dot_general(left, right, (((0,), (0,)), ((), ())), preferred_element_type=F32)


def dot_cols(left, right):
    return lax.dot_general(left, right, (((1,), (1,)), ((), ())), preferred_element_type=F32)


def norm_back(d_normed, normed, rms):
    return rms * (d_normed - normed * jnp.mean(d_normed * normed, axis=-1, keepdims=True))


class Place:
    def __init__(self, n, n_z):
        self.n, self.chips, self.n_z = n, n // 2, n_z
        self.f = lax.axis_index("fsdp")
        self.chip, self.core = self.f // 2, lax.rem(self.f, 2)
        self.sib = self.f + 1 - 2 * self.core
        self.z = lax.axis_index("replica")
        low = (self.z < n_z // 2).astype(jnp.int32)
        self.inner = self.z - 1 + 2 * low
        self.outer = self.z + 1 - 2 * low
        self.mid = (self.z == n_z // 2 - 1) | (self.z == n_z // 2)
        self.has_outer = (self.z > 0) & (self.z < n_z - 1)

    def to(self, k):
        return lax.rem(self.f + k, self.n)

    def near(self, j):
        return 2 * lax.rem(self.chip + j // 2, self.chips) + lax.rem(self.core + lax.rem(j, 2), 2)

    def near_from(self, j):
        return 2 * lax.rem(self.chip + self.chips - j // 2, self.chips) + lax.rem(self.core + lax.rem(j, 2), 2)

    def plane(self, k):
        return lax.rem(self.z + k, self.n_z)

    def chip_at(self, k):
        return lax.rem(self.chip + k, self.chips)

    def greet(self, line):
        barrier = pltpu.get_barrier_semaphore()
        for k in range(1, self.n):
            pl.semaphore_signal(barrier, inc=1, device_id={"fsdp": self.to(k)}, device_id_type=MESH)
        if line:
            for k in range(1, self.n_z):
                pl.semaphore_signal(barrier, inc=1, device_id={"replica": self.plane(k)}, device_id_type=MESH)

        pl.semaphore_wait(barrier, self.n - 1 + (self.n_z - 1 if line else 0))


def remote(src, dst, send, recv, axis, index):
    return pltpu.make_async_remote_copy(
        src_ref=src, dst_ref=dst, send_sem=send, recv_sem=recv, device_id={axis: index}, device_id_type=MESH)


def strips(rows, body):
    def step(i, carry):
        body(pl.ds(pl.multiple_of(i * STRIP, STRIP), STRIP))
        return carry

    lax.fori_loop(0, rows // STRIP, step, 0)


class Exchange:
    def __init__(self, at, pieces, send, recv):
        self.copies, self.local = [], []
        for i, (src, dst) in enumerate(pieces):
            self.local.append(pltpu.make_async_copy(src(at.f), dst(at.f), recv.at[i, 0]))
            for k in range(1, at.n):
                self.copies.append(remote(src(at.to(k)), dst(at.f), send.at[i, k], recv.at[i, k], "fsdp", at.to(k)))

    def start(self):
        for c in self.copies + self.local:
            c.start()

    def wait(self):
        for c in self.copies + self.local:
            c.wait()


class SquareGather:
    def __init__(self, at, own, whole, sem):
        rows = own.shape[0]
        half = rows // 2
        beside = (2 * (at.chip + 1 - 2 * lax.rem(at.chip, 2)) + at.core, 2 * at.chip_at(2) + at.core)

        def part(i, h):
            return whole.at[pl.ds(pl.multiple_of(i * rows + h * half, half), half)]

        def block(i):
            return whole.at[pl.ds(pl.multiple_of(i * rows, rows), rows)]

        def across(i, k):
            return remote(block(i), block(i), sem.at[0, k], sem.at[1, k], "fsdp", at.sib)

        self.local = pltpu.make_async_copy(own, block(at.f), sem.at[0, 0])
        self.out = [[remote(own.at[pl.ds(h * half, half)], part(at.f, h), sem.at[2 + w, h], sem.at[4 + w, h], "fsdp", beside[w])
                     for h in range(2)] for w in range(2)]
        self.on = [remote(part(beside[w], w), part(beside[w], w), sem.at[2 + w, 2], sem.at[4 + w, 2], "fsdp", beside[1 - w])
                   for w in range(2)]
        far = 2 * (at.chips - 1 - at.chip) + at.core
        self.across = [remote(own, block(at.f), sem.at[0, 1], sem.at[1, 1], "fsdp", at.sib)]
        self.across += [across(beside[0], 2), across(beside[1], 3), across(far, 4)]

    def start(self):
        for w in range(2):
            self.out[w][w].start()
        for w in range(2):
            self.out[w][1 - w].start()
        self.across[0].start()
        self.local.start()

    def relay(self):
        for w in range(2):
            self.out[w][w].wait_recv()
            self.on[w].start()

    def forward(self):
        for w in range(2):
            self.out[w][1 - w].wait_recv()
            self.across[1 + w].start()
        for w in range(2):
            self.on[w].wait_recv()
        self.across[3].start()

    def wait(self):
        for w in range(2):
            self.out[w][0].wait_send()
            self.out[w][1].wait_send()
            self.on[w].wait_send()
        for c in self.across + [self.local]:
            c.wait()


def gather_rows(at, own, whole, sem):
    return (SquareGather if at.chips == 4 else Gather)(at, own, whole, sem)


class Gather:
    def __init__(self, at, own, whole, sem):
        rows = own.shape[0]

        def block(i):
            return whole.at[pl.ds(pl.multiple_of(i * rows, rows), rows)]

        self.local = pltpu.make_async_copy(own, block(at.f), sem.at[0, 0])
        self.across = [remote(own, block(at.f), sem.at[0, 1], sem.at[1, 0], "fsdp", at.sib)]
        self.far, self.on = [], []
        for k in range(1, at.chips):
            to = 2 * at.chip_at(k) + at.core
            self.far.append(remote(own, block(at.f), sem.at[2, k], sem.at[3, k], "fsdp", to))
            came = 2 * at.chip_at(at.chips - k) + at.core
            self.on.append(remote(block(came), block(came), sem.at[4, k], sem.at[5, k], "fsdp", at.sib))

    def start(self):
        for c in self.far + self.across + [self.local]:
            c.start()

    def relay(self):
        pass

    def forward(self):
        for far, on in zip(self.far, self.on):
            far.wait_recv()
            on.start()

    def wait(self):
        for c in self.far:
            c.wait_send()
        for c in self.across + self.on + [self.local]:
            c.wait()


class ScatterSum:
    def __init__(self, at, part, near, own, far, sem, made=False):
        self.at, self.part, self.near, self.own, self.far, self.sem, self.made = at, part, near, own, far, sem, made
        self.rows = own.shape[1]
        self.order = list(range(1, at.chips)) + [0]

    def block(self, i):
        return self.part.at[pl.ds(pl.multiple_of(i * self.rows, self.rows), self.rows)]

    def across(self, k):
        at = self.at
        other = self.part.at[k] if self.made else self.block(2 * at.chip_at(k) + 1 - at.core)
        return remote(other, self.near.at[k], self.sem.at[0, k], self.sem.at[1, k], "fsdp", at.sib)

    def load(self, k):
        return pltpu.make_async_copy(
            self.block(2 * self.at.chip_at(k) + self.at.core), self.own.at[k], self.sem.at[2, k])

    def send(self, k):
        at = self.at
        return remote(self.own.at[k], self.far.at[k - 1], self.sem.at[3, k], self.sem.at[4, k], "fsdp",
                      2 * at.chip_at(k) + at.core)

    def start(self):
        for k in self.order:
            self.across(k).start()
            if not self.made:
                self.load(k).start()

    def pass_on(self, k):
        self.across(k).wait()
        if not self.made:
            self.load(k).wait()

        def add(at):
            self.own[k, at] = (self.own[k, at].astype(F32) + self.near[k, at].astype(F32)).astype(BF)

        strips(self.rows, add)

        @pl.when(k > 0)
        def _():
            self.send(k).start()

    def forward(self):
        def step(i, carry):
            self.pass_on(lax.rem(i + 1, self.at.chips))
            return carry

        lax.fori_loop(0, self.at.chips, step, 0)

    def wait(self):
        for k in range(1, self.at.chips):
            self.send(k).wait()

    def total(self, at):
        out = self.own[0, at].astype(F32)
        for k in range(self.at.chips - 1):
            out += self.far[k, at].astype(F32)
        return out


class LineSum:
    def __init__(self, at, chunk, ring, arrive, send, recv, credit, out, out_sem, skip=0, feed=None):
        self.at, self.chunk, self.ring, self.arrive, self.skip = at, chunk, ring, arrive, skip
        self.send, self.recv, self.credit, self.out, self.out_sem = send, recv, credit, out, out_sem
        self.feed = feed
        self.slots = ring.shape[1]
        self.count = chunk.shape[0]
        self.kind = at.mid.astype(jnp.int32)

    def slot(self, j):
        return lax.rem(j, self.slots)

    def inward(self, j):
        return remote(self.chunk.at[j], self.ring.at[self.kind, self.slot(j)], self.send.at[0, j],
                      self.recv.at[self.kind, j], "replica", self.at.inner)

    def outward(self, j, src):
        return remote(src, self.out(j), self.send.at[1, j], self.recv.at[2, j], "replica", self.at.outer)

    def keep(self, j):
        return pltpu.make_async_copy(self.chunk.at[j], self.out(j), self.out_sem.at[j])

    def take_in(self, kind, j, plane):
        here = self.ring.at[kind, self.slot(j)]
        pltpu.make_async_copy(here, here, self.recv.at[kind, j]).wait()
        self.chunk[j] = (self.chunk[j].astype(F32) + self.ring[kind, self.slot(j)].astype(F32)).astype(BF)

        @pl.when(j + self.slots < self.count)
        def _():
            pl.semaphore_signal(self.credit, inc=1, device_id={"replica": plane}, device_id_type=MESH)

    def up(self, j):
        if self.feed:
            @pl.when(j + LEAD < self.count)
            def _():
                self.feed(j + LEAD)

        @pl.when(j >= self.skip)
        def _():
            pltpu.make_async_copy(self.chunk.at[j], self.chunk.at[j], self.arrive.at[j]).wait()

        @pl.when(self.at.has_outer)
        def _():
            self.take_in(0, j, self.at.outer)

        @pl.when(j >= self.slots)
        def _():
            pl.semaphore_wait(self.credit, 1)

        self.inward(j).start()

    def meet(self, j):
        self.inward(j).wait_send()
        self.take_in(1, j, self.at.inner)

        @pl.when(self.at.has_outer)
        def _():
            self.outward(j, self.chunk.at[j]).start()

        self.keep(j).start()

    def take(self, j):
        pltpu.make_async_copy(self.out(j), self.out(j), self.recv.at[2, j]).wait()

        @pl.when(self.at.has_outer)
        def _():
            self.outward(j, self.out(j)).start()

    def settle(self):
        def step(j, carry):
            @pl.when(self.at.mid)
            def _():
                self.keep(j).wait()

            @pl.when(jnp.logical_not(self.at.mid))
            def _():
                self.inward(j).wait_send()

            @pl.when(self.at.has_outer)
            def _():
                self.outward(j, self.chunk.at[j]).wait_send()

            return carry

        lax.fori_loop(0, self.count, step, 0)


class Lines:
    def __init__(self, *lines):
        self.lines = lines
        self.order = [(i, j) for i, line in enumerate(lines) for j in range(line.count)]
        self.at = 0

    def run(self, steps=None, body=None):
        begin = self.at
        last = len(self.order) + LAG_END
        stop = last if steps is None else min(self.at + steps, len(self.order))
        while self.at < stop:
            first, size = self.at, 1
            now = self.parts(first)
            while first + size < stop and self.kinds(first + size) == self.kinds(first):
                size += 1

            def step(m, carry, now=now, first=first):
                up, mid, rest = now
                if up:
                    self.lines[up[0]].up(up[1] + m)
                if mid:
                    @pl.when(self.lines[mid[0]].at.mid)
                    def _():
                        self.lines[mid[0]].meet(mid[1] + m)
                if rest:
                    @pl.when(jnp.logical_not(self.lines[rest[0]].at.mid))
                    def _():
                        self.lines[rest[0]].take(rest[1] + m)
                if body:
                    body(first - begin + m)
                return carry

            lax.fori_loop(0, size, step, 0)
            self.at += size

    def parts(self, t):
        return [self.order[i] if 0 <= i < len(self.order) else None for i in (t, t - LAG_MID, t - LAG_END)]

    def kinds(self, t):
        return [part and part[0] for part in self.parts(t)]

    def settle(self):
        for line in self.lines:
            line.settle()


def rms_of(values):
    return lax.rsqrt(jnp.mean(values * values, axis=-1, keepdims=True) + EPSILON)


def qkv_pieces(at, w, wc, qw):
    q_w, k_w = QUERY_HEADS * HEAD_WIDTH, KEY_VALUE_HEADS * HEAD_WIDTH
    shared = at.n // KEY_VALUE_HEADS
    depth = w.shape[0]

    def cols(start, width):
        return pl.ds(pl.multiple_of(start, HEAD_WIDTH), width)

    def rows(s):
        return pl.ds(pl.multiple_of(s * depth, depth), depth)

    return [
        (lambda t: w.at[:, cols(t * qw, qw)], lambda s: wc.at[rows(s), pl.ds(0, qw)]),
        (lambda t: w.at[:, cols(q_w + t // shared * HEAD_WIDTH, HEAD_WIDTH)],
         lambda s: wc.at[rows(s), pl.ds(qw, HEAD_WIDTH)]),
        (lambda t: w.at[:, cols(q_w + k_w + t // shared * HEAD_WIDTH, HEAD_WIDTH)],
         lambda s: wc.at[rows(s), pl.ds(qw + HEAD_WIDTH, HEAD_WIDTH)]),
    ]


def col_piece(w, wc, share):
    depth = w.shape[0]
    return (lambda t: w.at[:, pl.ds(pl.multiple_of(t * share, HEAD_WIDTH), share)],
            lambda s: wc.at[pl.ds(pl.multiple_of(s * depth, depth), depth)])


class Weights:
    def __init__(self, at, pairs, send, recv, z_send, z_recv):
        self.at, self.pairs, self.send, self.recv, self.z_send, self.z_recv = at, pairs, send, recv, z_send, z_recv
        self.depth, self.share = pairs[0][0].shape[0], pairs[0][1].shape[1]
        self.mine = at.core == lax.rem(at.z, 2)
        self.parity = lax.rem(at.z + at.core, 2)
        self.partner = at.z + 1 - 2 * lax.rem(at.z, 2)

    def cols(self, i, t):
        return self.pairs[i][0].at[:, pl.ds(pl.multiple_of(t * self.share, HEAD_WIDTH), self.share)]

    def rows(self, i, s):
        return self.pairs[i][1].at[pl.ds(pl.multiple_of(s * self.depth, self.depth), self.depth)]

    def local(self, i):
        return pltpu.make_async_copy(self.cols(i, self.at.f), self.rows(i, self.at.f), self.recv.at[i, 0])

    def copy(self, i, j):
        to = self.at.near(j)
        return remote(self.cols(i, to), self.rows(i, self.at.f), self.send.at[i, j], self.recv.at[i, j], "fsdp", to)

    def beside(self, i, j):
        here = self.rows(i, self.at.near_from(j))
        return remote(here, here, self.z_send.at[i, j], self.z_recv.at[i, j], "replica", self.partner)

    def start(self, i):
        self.local(i).start()
        self.copy(i, 1).start()

        @pl.when(self.mine)
        def _():
            for j in range(2, self.at.n):
                self.copy(i, j).start()

    def hand_over(self, i):
        for m in range(1, self.at.chips):
            j = 2 * m + self.parity
            here = self.rows(i, self.at.near_from(j))
            pltpu.make_async_copy(here, here, self.recv.at[i, j]).wait()
            self.beside(i, j).start()

    def wait(self, i):
        self.local(i).wait()
        self.copy(i, 1).wait()

        @pl.when(self.mine)
        def _():
            for j in range(2, self.at.n):
                self.copy(i, j).wait_send()

        for m in range(1, self.at.chips):
            self.beside(i, 2 * m + self.parity).wait_send()
            self.beside(i, 2 * m + 1 - self.parity).wait_recv()


def front_kernel(n, n_z, x_ref, gain1_ref, gain2_ref, gainq_ref, gaink_ref, place_ref, table_ref, wout_ref,
                 wqkv_ref, g_ref, gate_ref, up_ref, down_ref,
                 h_ref, q_ref, kv_ref, ctx_ref, proj_ref, places_ref,
                 n1_ref, wc_ref, n2_ref, gall_ref, gate_c, up_c, down_c,
                 near, mine, far, stage, own, n1_block, wc,
                 s_x, r_x, s_p, r_p, s_g, s_n, s_w, s_h, s_r, s_a, s_b, s_c, r_c, s_z, r_z):
    at = Place(n, n_z)
    rows = x_ref.shape[0]
    heads = QUERY_HEADS // n
    qw = heads * HEAD_WIDTH
    halo = LMAX
    at.greet(True)
    weights = Exchange(at, qkv_pieces(at, wqkv_ref, wc_ref, qw), s_x, r_x)

    def rows_of(g):
        return pl.ds(pl.multiple_of(g * rows, rows), rows)

    places = Exchange(at, [(lambda t: place_ref, lambda s: places_ref.at[rows_of(s)])], s_p, r_p)
    mlp = Weights(at, [(gate_ref, gate_c), (up_ref, up_c), (down_ref, down_c)], s_c, r_c, s_z, r_z)
    places.start()

    def norm1(strip):
        x = x_ref[strip].astype(F32)
        own[strip] = (x * rms_of(x) * gain1_ref[...]).astype(BF)

    strips(rows, norm1)
    n1 = gather_rows(at, own, n1_ref, s_g)
    n1.start()
    weights.start()
    n1.relay()
    n1.forward()
    n1.wait()
    places.wait()
    weights.wait()
    mlp.start(0)
    mlp.start(1)
    to_vmem = pltpu.make_async_copy(wc_ref, wc, s_w.at[0])
    to_vmem.start()

    def block_of(g):
        return pltpu.make_async_copy(n1_ref.at[rows_of(g)], n1_block.at[lax.rem(g, 2)], s_n.at[lax.rem(g, 2)])

    block_of(0).start()
    to_vmem.wait()

    def project(g, carry):
        @pl.when(g + 1 < n)
        def _():
            block_of(g + 1).start()

        at_rows = rows_of(g)
        cosine, sine = rotation_of(places_ref[at_rows], table_ref)
        block_of(g).wait()
        proj = dot(n1_block[lax.rem(g, 2)], wc[...])
        proj_ref[at_rows] = proj[:, :qw + HEAD_WIDTH]
        for head in range(heads + 1):
            lanes = slice(head * HEAD_WIDTH, (head + 1) * HEAD_WIDTH)
            raw = proj[:, lanes]
            gain = gainq_ref if head < heads else gaink_ref
            turned = rotate_with(raw * rms_of(raw) * gain[...], cosine, sine).astype(BF)
            if head < heads:
                q_ref[at_rows, lanes] = turned
            else:
                kv_ref[g, halo:, :HEAD_WIDTH] = turned
        kv_ref[g, halo:, HEAD_WIDTH:] = proj[:, qw + HEAD_WIDTH:].astype(BF)
        return carry

    lax.fori_loop(0, n, project, 0)
    not_first, not_last = at.z > 0, at.z < n_z - 1

    def halo_copy():
        return remote(kv_ref.at[:, pl.ds(rows, halo)], kv_ref.at[:, pl.ds(0, halo)], s_h.at[0], s_h.at[1], "replica",
                      jnp.minimum(at.z + 1, n_z - 1))

    @pl.when(not_last)
    def _():
        halo_copy().start()

    @pl.when(not_first)
    def _():
        here = kv_ref.at[:, pl.ds(0, halo)]
        pltpu.make_async_copy(here, here, s_h.at[1]).wait()

    @pl.when(jnp.logical_not(not_first))
    def _():
        kv_ref[:, :halo] = jnp.zeros((n, halo, 2 * HEAD_WIDTH), BF)

    sum_o = ScatterSum(at, stage, near, mine, far, s_r, made=True)

    def attend(g):
        at_rows = rows_of(g)
        mask = window_mask(places_ref[at_rows], rows, halo)
        keys, values = kv_ref[g, :, :HEAD_WIDTH], kv_ref[g, :, HEAD_WIDTH:]
        for head in range(heads):
            lanes = slice(head * HEAD_WIDTH, (head + 1) * HEAD_WIDTH)
            probs = softmax_of(q_ref[at_rows, lanes], keys, mask).astype(BF)
            ctx_ref[at_rows, lanes] = dot(probs, values).astype(BF)
        return dot(ctx_ref[at_rows], wout_ref[...]).astype(BF)

    def attend_both(i, carry):
        k = lax.rem(i + 1, at.chips)
        q = at.chip_at(k)
        stage[k] = attend(2 * q + 1 - at.core)
        sum_o.across(k).start()
        mine[k] = attend(2 * q + at.core)

        @pl.when(i > 0)
        def _():
            sum_o.pass_on(jnp.maximum(i, 1))

        return carry

    lax.fori_loop(0, at.chips, attend_both, 0)
    sum_o.pass_on(0)
    mlp.start(2)
    mlp.hand_over(0)
    sum_o.wait()

    def norm2(strip):
        h = x_ref[strip].astype(F32) + sum_o.total(strip)
        h_ref[strip] = h
        own[strip] = (h * rms_of(h) * gain2_ref[...]).astype(BF)

    strips(rows, norm2)
    n2 = gather_rows(at, own, n2_ref, s_a)
    g_all = gather_rows(at, g_ref, gall_ref, s_b)
    n2.start()
    mlp.hand_over(1)
    n2.relay()
    g_all.start()
    n2.forward()
    g_all.relay()
    mlp.hand_over(2)
    g_all.forward()
    n2.wait()
    g_all.wait()

    @pl.when(not_last)
    def _():
        halo_copy().wait_send()

    for i in range(3):
        mlp.wait(i)


class Feed:
    def __init__(self, at, grads, chunk, send, recv):
        self.at, self.grads, self.chunk, self.send, self.recv = at, grads, chunk, send, recv
        self.depth = chunk.shape[1]

    def rows(self, grad, t):
        return grad.at[pl.ds(pl.multiple_of(t * self.depth, self.depth), self.depth)]

    def copy(self, grad, c, j):
        to = self.at.near(j)
        return remote(self.rows(grad, to), self.chunk.at[c], self.send.at[c], self.recv.at[c], "fsdp", to)

    def start(self, c):
        n = self.at.n
        j = lax.rem(c, n)
        for i, grad in enumerate(self.grads):
            @pl.when((c // n == i) & (j == 0))
            def _(grad=grad):
                pltpu.make_async_copy(self.rows(grad, self.at.f), self.chunk.at[c], self.recv.at[c]).start()

            @pl.when((c // n == i) & (j > 0))
            def _(grad=grad):
                self.copy(grad, c, j).start()

    def settle(self):
        def step(c, carry):
            @pl.when(lax.rem(c, self.at.n) > 0)
            def _():
                self.copy(self.grads[0], c, lax.rem(c, self.at.n)).wait_send()

            return carry

        lax.fori_loop(0, len(self.grads) * self.at.n, step, 0)


def start_all(copies):
    for c in copies:
        c.start()


def rotate_with(values, cosine, sine):
    return values * cosine + pltpu.roll(values, HEAD_WIDTH // 2, 1) * sine


def rotation_table():
    places = HEAD_WIDTH * -(-LMAX // HEAD_WIDTH)
    inverse = ROPE_BASE ** (-(2.0 * np.arange(HEAD_WIDTH // 2)) / HEAD_WIDTH)
    angles = np.arange(places)[:, None] * inverse[None, :]
    cosine, sine = np.cos(angles), np.sin(angles)
    rest = np.concatenate([cosine, cosine, -sine, sine], axis=1).astype(np.float32)
    terms = []
    for _ in range(3):
        terms.append(rest.astype(jnp.bfloat16))
        rest = rest - terms[-1].astype(np.float32)
    return jnp.asarray(np.stack(terms))


def rotation_of(places, table):
    lane = lax.broadcasted_iota(jnp.int32, (places.shape[0], table.shape[1]), 1).astype(F32)
    pick = (lane == places.astype(F32)[:, :1]).astype(F32).astype(BF)
    both = dot(pick, table[0]) + dot(pick, table[1]) + dot(pick, table[2])
    return both[:, :HEAD_WIDTH], both[:, HEAD_WIDTH:]


def window_mask(places, rows, halo):
    i_at = lax.broadcasted_iota(jnp.int32, (rows, halo + rows), 0) + halo
    j_at = lax.broadcasted_iota(jnp.int32, (rows, halo + rows), 1)
    back = (i_at - j_at).astype(F32)
    return (back >= 0) & (back <= places.astype(F32)[:, :1])


def softmax_of(queries, keys, mask):
    scores = jnp.where(mask, dot_cols(queries, keys) * HEAD_WIDTH ** (-0.5), NEG_FILL)
    terms = jnp.exp(scores - jnp.max(scores, axis=1, keepdims=True))
    return terms / jnp.sum(terms, axis=1, keepdims=True)


def back_kernel(n, n_z, part_ref, party_ref, x_ref, h_ref, g_ref, gain1_ref, gain2_ref, gainq_ref, gaink_ref,
                down_ref, n2_ref, dgate_ref, dup_ref, wout_ref, wqkv_ref, q_ref, kv_ref, ctx_ref, proj_ref, table_ref, place_ref,
                n1_ref,
                dx_ref, y_ref, gains_ref, gmlp_ref, gqkv_ref, dhall_ref, gate_ref, up_ref,
                near, mine, far, stage, dh, plane_gain, all_gain,
                chunk, ring, chunk2, ring2, dh_block, gout, d_kv, d_proj, halo_out, halo_in, n1_cols, qkv_send, d_in, tile_out,
                s_r, s_a, s_p, r_p, s_q, r_q, s_c, r_c, s_z, r_z, s_o, s_c2, r_c2, s_z2, r_z2, s_o2, credit, done, s_d, s_n, s_h, s_e, s_t):
    at = Place(n, n_z)
    share, share_out = chunk.shape[2], chunk2.shape[2]
    rows, width = x_ref.shape
    depth = chunk.shape[1]
    outs = -(-width // share_out)
    heads = QUERY_HEADS // n
    qw = heads * HEAD_WIDTH
    halo = LMAX
    scale = HEAD_WIDTH ** (-0.5)
    own = dh_block
    own_gain = all_gain.at[at.z]
    at.greet(True)

    def mlp_place(j):
        s = at.near_from(lax.rem(j, n))
        return gmlp_ref.at[j // n, :, pl.ds(pl.multiple_of(s * share, HEAD_WIDTH), share)]

    def attn_place(j):
        col = jnp.where(j < outs, j, outs + at.near_from(jnp.maximum(j - outs, 0)))
        return gqkv_ref.at[:, pl.ds(pl.multiple_of(col * share_out, HEAD_WIDTH), share_out)]

    feed = Feed(at, (down_ref, gate_ref, up_ref), chunk, s_c, r_c)
    lines = Lines(
        LineSum(at, chunk, ring, r_c, s_z, r_z, credit.at[0], mlp_place, s_o, 0, feed.start),
        LineSum(at, chunk2, ring2, r_c2, s_z2, r_z2, credit.at[1], attn_place, s_o2, outs))
    sum_n2 = ScatterSum(at, part_ref, near, mine, far, s_r.at[0])
    for c in range(LEAD):
        feed.start(jnp.int32(c))
    sum_n2.start()
    load = pltpu.make_async_copy(dgate_ref, d_in, s_e.at[0])
    load.start()
    lines.run(1)
    sum_n2.forward()

    def fetch_cols(ref, j):
        return pltpu.make_async_copy(
            ref.at[:, pl.ds(pl.multiple_of(at.near(j) * depth, depth), depth)], n1_cols.at[lax.rem(j, 2)],
            s_n.at[lax.rem(j, 2)])

    def tiles(ref, per):
        def put(j):
            return pltpu.make_async_copy(
                tile_out.at[lax.rem(j, 2)], ref.at[pl.ds(pl.multiple_of(at.near(j) * depth, depth), depth)],
                s_t.at[lax.rem(j, 2)])

        def tile(j):
            @pl.when(j + 1 < n)
            def _():
                fetch_cols(n2_ref, j + 1).start()

            fetch_cols(n2_ref, j).wait()

            @pl.when(j > 1)
            def _():
                put(j - 2).wait()

            tile_out[lax.rem(j, 2)] = dot_rows(n1_cols[lax.rem(j, 2)], d_in[...]).astype(BF)
            put(j).start()

        def body(step):
            for r in range(per):
                j = step * per + r

                @pl.when(j < n)
                def _(j=j):
                    tile(j)

        def end():
            put(n - 2).wait()
            put(n - 1).wait()

        fetch_cols(n2_ref, 0).start()
        return body, end

    per_tile = -(-n // 3)
    load.wait()
    body, end = tiles(gate_ref, per_tile)
    lines.run(3, body)
    end()
    load = pltpu.make_async_copy(dup_ref, d_in, s_e.at[0])
    load.start()
    lines.run(n - 8)
    sum_n2.wait()
    own_gain[...] = jnp.zeros_like(own_gain)

    def back_mlp(strip):
        d_n2 = sum_n2.total(strip)
        h = h_ref[strip]
        r2 = rms_of(h)
        u2 = h * r2
        own_gain[1:2] += jnp.sum(d_n2 * u2, axis=0, keepdims=True)
        d_h = g_ref[strip].astype(F32) + norm_back(d_n2 * gain2_ref[...], u2, r2)
        dh[strip] = d_h
        own[strip] = d_h.astype(BF)

    strips(rows, back_mlp)
    gather = gather_rows(at, own, dhall_ref, s_a)
    gather.start()
    load.wait()
    body, end = tiles(up_ref, per_tile)
    lines.run(3, body)
    end()
    lines.run(n // 2 - 4)
    gather.relay()
    lines.run(2)
    gather.forward()
    lines.run(1)
    gather.wait()
    sum_y = ScatterSum(at, party_ref, near, mine, far, s_r.at[2])
    sum_y.start()
    lines.run(1)
    sum_y.forward()
    gout[...] = jnp.zeros_like(gout)

    def rows_of(g):
        return pl.ds(pl.multiple_of(g * rows, rows), rows)

    def block_of(g):
        return pltpu.make_async_copy(dhall_ref.at[rows_of(g)], dh_block, s_d.at[0])

    def attention(g):
        at_rows = rows_of(g)
        block_of(g).start()
        mask = window_mask(place_ref[at_rows], rows, halo)
        keys, values = kv_ref[g, :, :HEAD_WIDTH], kv_ref[g, :, HEAD_WIDTH:]
        cosine, sine = rotation_of(place_ref[at_rows], table_ref)
        block_of(g).wait()
        d_ctx = dot_cols(dh_block[...], wout_ref[...]).astype(BF)
        gout[:, :width] += dot_rows(ctx_ref[at_rows], dh_block[...])
        d_k = jnp.zeros((halo + rows, HEAD_WIDTH), F32)
        d_v = jnp.zeros((halo + rows, HEAD_WIDTH), F32)
        for head in range(heads):
            lanes = slice(head * HEAD_WIDTH, (head + 1) * HEAD_WIDTH)
            queries, d_c = q_ref[at_rows, lanes], d_ctx[:, lanes]
            probs = softmax_of(queries, keys, mask)
            d_v += dot_rows(probs.astype(BF), d_c)
            d_p = dot_cols(d_c, values)
            d_s = (probs * (d_p - jnp.sum(probs * d_p, axis=1, keepdims=True))).astype(BF)
            d_k += dot_rows(d_s, queries) * scale
            dq_g = rotate_with(dot(d_s, keys) * scale, cosine, -sine)
            raw = proj_ref[at_rows, lanes]
            rms = rms_of(raw)
            hat = raw * rms
            own_gain[2:3, :HEAD_WIDTH] += jnp.sum(dq_g * hat, axis=0, keepdims=True)
            d_proj[at_rows, lanes] = norm_back(dq_g * gainq_ref[...], hat, rms).astype(BF)
        halo_out[g, :, :HEAD_WIDTH] = d_k[:halo].astype(BF)
        halo_out[g, :, HEAD_WIDTH:] = d_v[:halo].astype(BF)
        d_kv[g, :, :HEAD_WIDTH] = d_k[halo:]
        d_kv[g, :, HEAD_WIDTH:] = d_v[halo:]

    lines.run(n, attention)

    not_first, not_last = at.z > 0, at.z < n_z - 1

    def halo_copy():
        return remote(halo_out, halo_in, s_h.at[0], s_h.at[1], "replica", jnp.maximum(at.z - 1, 0))

    @pl.when(not_first)
    def _():
        halo_copy().start()

    for i in range(outs):
        chunk2[i] = gout[:, i * share_out:(i + 1) * share_out].astype(BF)
    lines.run(1)
    sum_y.wait()

    def finish(strip):
        y_ref[strip] = (h_ref[strip] + sum_y.total(strip)).astype(BF)

    strips(rows, finish)
    for k in range(1, n):
        pl.semaphore_signal(done, inc=1, device_id={"fsdp": at.to(k)}, device_id_type=MESH)

    @pl.when(not_last)
    def _():
        pltpu.make_async_copy(halo_in, halo_in, s_h.at[1]).wait()

    @pl.when(jnp.logical_not(not_last))
    def _():
        halo_in[...] = jnp.zeros_like(halo_in)

    def keys_back(g):
        at_rows = rows_of(g)
        d_kv[g, rows - halo:] += halo_in[g].astype(F32)
        cosine, sine = rotation_of(place_ref[at_rows], table_ref)
        dk_g = rotate_with(d_kv[g, :, :HEAD_WIDTH], cosine, -sine)
        raw = proj_ref[at_rows, qw:qw + HEAD_WIDTH]
        rms = rms_of(raw)
        hat = raw * rms
        own_gain[2:3, HEAD_WIDTH:2 * HEAD_WIDTH] += jnp.sum(dk_g * hat, axis=0, keepdims=True)
        d_proj[at_rows, qw:qw + HEAD_WIDTH] = norm_back(dk_g * gaink_ref[...], hat, rms).astype(BF)
        d_proj[at_rows, qw + HEAD_WIDTH:] = d_kv[g, :, HEAD_WIDTH:].astype(BF)

    per_step = n // 2

    def keys_back_some(i):
        for m in range(per_step):
            keys_back(i * per_step + m)

    lines.run(2, keys_back_some)

    def cols_of(j):
        return fetch_cols(n1_ref, j)

    own_qkv = pltpu.make_async_copy(qkv_send.at[0], chunk2.at[outs], r_c2.at[outs])

    def qkv_copy(j):
        return remote(qkv_send.at[j], chunk2.at[outs + j], s_c2.at[j], r_c2.at[outs + j], "fsdp", at.near(j))

    cols_of(0).start()

    def qkv_grad(j):
        @pl.when(j + 1 < n)
        def _():
            cols_of(j + 1).start()

        cols_of(j).wait()
        qkv_send[j] = dot_rows(n1_cols[lax.rem(j, 2)], d_proj[...]).astype(BF)

        @pl.when(j == 0)
        def _():
            own_qkv.start()

        @pl.when(j > 0)
        def _():
            qkv_copy(j).start()

    per_out = n // 4

    def qkv_grads(i):
        for m in range(per_out):
            qkv_grad(i * per_out + m)

    sum_n1 = ScatterSum(at, stage, near, mine, far, s_r.at[1], made=True)

    def n1_part(k):
        q = at.chip_at(k)
        stage[k] = dot_cols(d_proj[rows_of(2 * q + 1 - at.core)], wqkv_ref[...]).astype(BF)
        mine[k] = dot_cols(d_proj[rows_of(2 * q + at.core)], wqkv_ref[...]).astype(BF)

    def both(i):
        qkv_grads(i)
        for r in range(at.chips // 4):
            n1_part(i * (at.chips // 4) + r)

    lines.run(4, both)
    pl.semaphore_wait(done, n - 1)
    sum_n1.start()
    lines.run(1)
    sum_n1.forward()
    lines.run(outs + n - 4 - 1 - 2 - -2)
    sum_n1.wait()

    def back_attn(strip):
        d_n1 = sum_n1.total(strip)
        x = x_ref[strip].astype(F32)
        r1 = rms_of(x)
        u1 = x * r1
        own_gain[0:1] += jnp.sum(d_n1 * u1, axis=0, keepdims=True)
        dx_ref[strip] = (dh[strip] + norm_back(d_n1 * gain1_ref[...], u1, r1)).astype(BF)

    strips(rows, back_attn)
    gains = Exchange(at, [(lambda t: own_gain, lambda s: plane_gain.at[s])], s_p, r_p)
    gains.start()
    lines.run(1)
    gains.wait()
    own_gain[...] = jnp.sum(plane_gain[...], axis=0)
    others = [
        remote(own_gain, all_gain.at[at.z], s_q.at[k], r_q.at[k], "replica", at.plane(k)) for k in range(1, n_z)]
    start_all(others)
    lines.run()
    for c in others:
        c.wait()
    gains_ref[...] = jnp.sum(all_gain[...], axis=0)
    feed.settle()
    for j in range(1, n):
        qkv_copy(j).wait_send()

    @pl.when(not_first)
    def _():
        halo_copy().wait_send()

    lines.settle()


def front(n, n_z, x, gain1, gain2, gain_q, gain_k, place, table, w_out, w_qkv, g, gate, up, down):
    rows, width = x.shape
    chips, share, total = n // 2, gate.shape[1] // n, n * rows
    qw = QUERY_HEADS * HEAD_WIDTH // n
    wide = qw + 2 * HEAD_WIDTH
    block = functools.partial(pltpu.VMEM, dtype=BF)
    shape = jax.ShapeDtypeStruct
    return pl.pallas_call(
        functools.partial(front_kernel, n, n_z),
        out_shape=(
            shape((rows, width), F32), shape((total, qw), BF), shape((n, LMAX + rows, 2 * HEAD_WIDTH), BF),
            shape((total, qw), BF), shape((total, qw + HEAD_WIDTH), F32), shape((total, HEAD_WIDTH), BF),
            shape((total, width), BF), shape((width, wide), BF), shape((total, width), BF), shape((total, width), BF),
        ) + (shape((width, share), BF),) * 3,
        in_specs=[VMEM] * 8 + [ANY] * 5,
        out_specs=(VMEM,) * 6 + (ANY,) * 7,
        scratch_shapes=[
            block((chips, rows, width)), block((chips, rows, width)), block((chips - 1, rows, width)),
            block((chips, rows, width)), block((rows, width)), block((2, rows, width)), block((width, wide)),
            DMA((3, n)), DMA((3, n)), DMA((1, n)), DMA((1, n)), DMA((6, n)), DMA((2,)), DMA((1,)), DMA((2,)),
            DMA((5, n)), DMA((6, n)), DMA((6, n)), DMA((3, n)), DMA((3, n)), DMA((3, n)), DMA((3, n))],
        compiler_params=pltpu.CompilerParams(collective_id=0, has_side_effects=True, vmem_limit_bytes=60 << 20),
        name="front",
    )(x, gain1, gain2, gain_q, gain_k, place, table, w_out, w_qkv, g, gate, up, down)


def back(n, n_z, part, part_y, x, h, g, gain1, gain2, gain_q, gain_k, down, n2, d_gate, d_up, w_out, w_qkv, q, kv, ctx, proj,
         table, places, n1):
    rows, width = x.shape
    chips, share, wide, depth = n // 2, down.shape[1], w_qkv.shape[1], width // n
    outs = -(-width // wide)
    block = functools.partial(pltpu.VMEM, dtype=BF)
    gains = (8, width)
    count2 = outs + n
    slots = 2 + 16 // n
    return pl.pallas_call(
        functools.partial(back_kernel, n, n_z),
        out_shape=(
            jax.ShapeDtypeStruct((rows, width), BF),
            jax.ShapeDtypeStruct((rows, width), BF),
            jax.ShapeDtypeStruct(gains, F32),
            jax.ShapeDtypeStruct((3, depth, n * share), BF),
            jax.ShapeDtypeStruct((depth, count2 * wide), BF),
            jax.ShapeDtypeStruct((n * rows, width), BF),
            jax.ShapeDtypeStruct((width, share), BF),
            jax.ShapeDtypeStruct((width, share), BF),
        ),
        in_specs=[ANY, ANY] + [VMEM] * 7 + [ANY] * 4 + [VMEM] * 8 + [ANY],
        out_specs=(VMEM, VMEM, VMEM, ANY, ANY, ANY, ANY, ANY),
        scratch_shapes=[
            block((chips, rows, width)), block((chips, rows, width)), block((chips - 1, rows, width)),
            block((chips, rows, width)), pltpu.VMEM((rows, width), F32),
            pltpu.VMEM((n,) + gains, F32), pltpu.VMEM((n_z,) + gains, F32),
            block((3 * n, depth, share)), block((2, slots, depth, share)),
            block((count2, depth, wide)), block((2, slots, depth, wide)),
            block((rows, width)), pltpu.VMEM((depth, outs * wide), F32),
            pltpu.VMEM((n, rows, 2 * HEAD_WIDTH), F32), block((n * rows, wide)),
            block((n, LMAX, 2 * HEAD_WIDTH)), block((n, LMAX, 2 * HEAD_WIDTH)),
            block((2, n * rows, depth)), block((n, depth, wide)), block((n * rows, share)), block((2, depth, share)),
            DMA((3, 5, n)), DMA((6, n)), DMA((1, n)), DMA((1, n)), DMA((n_z,)), DMA((n_z,)),
            DMA((3 * n,)), DMA((3 * n,)), DMA((2, 3 * n)), DMA((3, 3 * n)), DMA((3 * n,)),
            DMA((n,)), DMA((count2,)), DMA((2, count2)), DMA((3, count2)), DMA((count2,)),
            pltpu.SemaphoreType.REGULAR((2,)), pltpu.SemaphoreType.REGULAR, DMA((1,)), DMA((2,)), DMA((2,)), DMA((1,)), DMA((2,))],
        compiler_params=pltpu.CompilerParams(collective_id=2, has_side_effects=True, vmem_limit_bytes=511 << 17),
        name="back",
    )(part, part_y, x, h, g, gain1, gain2, gain_q, gain_k, down, n2, d_gate, d_up, w_out, w_qkv, q, kv, ctx, proj, table, places, n1)


def row_positions(flat_lens, ranks, first_row, count):
    earlier = (ranks[:, None] < ranks[None, :]).astype(jnp.int32)
    starts = jnp.sum(flat_lens[:, None] * earlier, axis=0)
    rows = first_row + jnp.arange(count, dtype=jnp.int32)
    begun = jnp.where(starts[None, :] <= rows[:, None], starts[None, :], 0)
    return rows - jnp.max(begun, axis=1)


def per_device(
    n_replica, tokens, cotangent, w_qkv, w_out, w_gate, w_up, w_down_t,
    gain_attn, gain_mlp, gain_query, gain_key, dealt_lens, seq_order,
):
    rows, width = tokens.shape
    n_fsdp = width // w_qkv.shape[0]
    q_w = QUERY_HEADS * HEAD_WIDTH
    k_w = KEY_VALUE_HEADS * HEAD_WIDTH
    replica = lax.axis_index("replica")
    shared = n_fsdp // KEY_VALUE_HEADS
    heads = QUERY_HEADS // n_fsdp
    qw = heads * HEAD_WIDTH

    pos = row_positions(dealt_lens[0].reshape(-1), seq_order[0], replica * rows, rows)
    depth = w_qkv.shape[0]
    place = jnp.broadcast_to(pos.astype(BF)[:, None], (rows, HEAD_WIDTH))
    table = rotation_table()
    gains = (gain_attn[None], gain_mlp[None], gain_query[None], gain_key[None])
    h, q_low, kv_window, ctx_low, proj, places, n1, w_qkv_c, n2, g_all, gate_c, up_c, down_c = front(
        n_fsdp, n_replica, tokens, *gains, place, table, w_out, w_qkv, cotangent, w_gate, w_up, w_down_t)

    gate = dot(n2, gate_c)
    up = dot(n2, up_c)
    sg = jax.nn.sigmoid(gate)
    silu = gate * sg
    act = (silu * up).astype(BF)
    part_y = dot_cols(act, down_c).astype(BF)

    d_act = dot(g_all, down_c)
    d_gate = (d_act * up * sg * (1.0 + gate * (1.0 - sg))).astype(BF)
    d_up = (d_act * silu).astype(BF)

    input_grad, output, gain_sums, g_mlp, g_attn, _, _, _ = back(
        n_fsdp, n_replica, (dot_cols(d_gate, gate_c) + dot_cols(d_up, up_c)).astype(BF), part_y, tokens, h, cotangent, *gains,
        dot_rows(g_all, act).astype(BF), n2, d_gate, d_up,
        w_out, w_qkv_c, q_low, kv_window, ctx_low, proj, table, places, n1)
    wide = qw + 2 * HEAD_WIDTH
    g_out = g_attn[:, :width]
    by_device = [g_attn[:, at:at + wide] for at in range(g_attn.shape[1] - n_fsdp * wide, g_attn.shape[1], wide)]

    def of_key_heads(first):
        parts = [part[:, first:first + HEAD_WIDTH].astype(F32) for part in by_device]
        return [sum(parts[i + 1:i + shared], parts[i]) for i in range(0, n_fsdp, shared)]

    g_qkv = jnp.concatenate(
        [part[:, :qw].astype(F32) for part in by_device] + of_key_heads(qw) + of_key_heads(qw + HEAD_WIDTH), axis=1)
    return (
        output, input_grad, g_qkv, g_out.astype(F32), g_mlp[1].astype(F32), g_mlp[2].astype(F32), g_mlp[0].astype(F32),
        gain_sums[0], gain_sums[1], gain_sums[2, :HEAD_WIDTH], gain_sums[2, HEAD_WIDTH:2 * HEAD_WIDTH])


def solution(mesh):
    n_replica = mesh.shape["replica"]

    def program(*args):
        return per_device(n_replica, *args)

    rows = P(("fsdp", "replica"), None)
    weight = P("fsdp", None)
    return jax.shard_map(
        program,
        mesh=mesh,
        in_specs=(rows, rows) + (weight,) * 5 + (P(),) * 4 + (P("fsdp", None, None), P("fsdp", None)),
        out_specs=(rows, rows) + (weight,) * 5 + (P(),) * 4,
        check_vma=False,
    )
```

```python
import functools

import jax
import jax.numpy as jnp
import numpy as np
from jax import lax
from jax.experimental import pallas as pl
from jax.experimental.pallas import tpu as pltpu
from jax.sharding import PartitionSpec as P

QUERY_HEADS = 16
KEY_VALUE_HEADS = 8
HEAD_WIDTH = 128
LMAX = 96

EPSILON = 1e-06
ROPE_BASE = 1000000.0
NEG_FILL = -1e30
BF = jnp.bfloat16
F32 = jnp.float32


MESH = pl.DeviceIdType.MESH
ANY = pl.BlockSpec(memory_space=pl.ANY)
VMEM = pl.BlockSpec(memory_space=pltpu.VMEM)
DMA = pltpu.SemaphoreType.DMA
STRIP = 16
LAG_MID = 2
LAG_END = 6
LEAD = 5


def dot(left, right):
    return jnp.dot(left, right, preferred_element_type=F32)


def dot_rows(left, right):
    return lax.dot_general(left, right, (((0,), (0,)), ((), ())), preferred_element_type=F32)


def dot_cols(left, right):
    return lax.dot_general(left, right, (((1,), (1,)), ((), ())), preferred_element_type=F32)


def norm_back(d_normed, normed, rms):
    return rms * (d_normed - normed * jnp.mean(d_normed * normed, axis=-1, keepdims=True))


class Place:
    def __init__(self, n, n_z):
        self.n, self.chips, self.n_z = n, n // 2, n_z
        self.f = lax.axis_index("fsdp")
        self.chip, self.core = self.f // 2, lax.rem(self.f, 2)
        self.sib = self.f + 1 - 2 * self.core
        self.z = lax.axis_index("replica")
        low = (self.z < n_z // 2).astype(jnp.int32)
        self.inner = self.z - 1 + 2 * low
        self.outer = self.z + 1 - 2 * low
        self.mid = (self.z == n_z // 2 - 1) | (self.z == n_z // 2)
        self.has_outer = (self.z > 0) & (self.z < n_z - 1)

    def to(self, k):
        return lax.rem(self.f + k, self.n)

    def near(self, j):
        return 2 * lax.rem(self.chip + j // 2, self.chips) + lax.rem(self.core + lax.rem(j, 2), 2)

    def near_from(self, j):
        return 2 * lax.rem(self.chip + self.chips - j // 2, self.chips) + lax.rem(self.core + lax.rem(j, 2), 2)

    def plane(self, k):
        return lax.rem(self.z + k, self.n_z)

    def chip_at(self, k):
        return lax.rem(self.chip + k, self.chips)

    def greet(self, line):
        barrier = pltpu.get_barrier_semaphore()
        for k in range(1, self.n):
            pl.semaphore_signal(barrier, inc=1, device_id={"fsdp": self.to(k)}, device_id_type=MESH)
        if line:
            for k in range(1, self.n_z):
                pl.semaphore_signal(barrier, inc=1, device_id={"replica": self.plane(k)}, device_id_type=MESH)

        pl.semaphore_wait(barrier, self.n - 1 + (self.n_z - 1 if line else 0))


def remote(src, dst, send, recv, axis, index):
    return pltpu.make_async_remote_copy(
        src_ref=src, dst_ref=dst, send_sem=send, recv_sem=recv, device_id={axis: index}, device_id_type=MESH)


def strips(rows, body):
    def step(i, carry):
        body(pl.ds(pl.multiple_of(i * STRIP, STRIP), STRIP))
        return carry

    lax.fori_loop(0, rows // STRIP, step, 0)


class Exchange:
    def __init__(self, at, pieces, send, recv):
        self.copies, self.local = [], []
        for i, (src, dst) in enumerate(pieces):
            self.local.append(pltpu.make_async_copy(src(at.f), dst(at.f), recv.at[i, 0]))
            for k in range(1, at.n):
                self.copies.append(remote(src(at.to(k)), dst(at.f), send.at[i, k], recv.at[i, k], "fsdp", at.to(k)))

    def start(self):
        for c in self.copies + self.local:
            c.start()

    def wait(self):
        for c in self.copies + self.local:
            c.wait()


class SquareGather:
    def __init__(self, at, own, whole, sem):
        rows = own.shape[0]
        half = rows // 2
        beside = (2 * (at.chip + 1 - 2 * lax.rem(at.chip, 2)) + at.core, 2 * at.chip_at(2) + at.core)

        def part(i, h):
            return whole.at[pl.ds(pl.multiple_of(i * rows + h * half, half), half)]

        def block(i):
            return whole.at[pl.ds(pl.multiple_of(i * rows, rows), rows)]

        def across(i, k):
            return remote(block(i), block(i), sem.at[0, k], sem.at[1, k], "fsdp", at.sib)

        self.local = pltpu.make_async_copy(own, block(at.f), sem.at[0, 0])
        self.out = [[remote(own.at[pl.ds(h * half, half)], part(at.f, h), sem.at[2 + w, h], sem.at[4 + w, h], "fsdp", beside[w])
                     for h in range(2)] for w in range(2)]
        self.on = [remote(part(beside[w], w), part(beside[w], w), sem.at[2 + w, 2], sem.at[4 + w, 2], "fsdp", beside[1 - w])
                   for w in range(2)]
        far = 2 * (at.chips - 1 - at.chip) + at.core
        self.across = [remote(own, block(at.f), sem.at[0, 1], sem.at[1, 1], "fsdp", at.sib)]
        self.across += [across(beside[0], 2), across(beside[1], 3), across(far, 4)]

    def start(self):
        for w in range(2):
            self.out[w][w].start()
        for w in range(2):
            self.out[w][1 - w].start()
        self.across[0].start()
        self.local.start()

    def relay(self):
        for w in range(2):
            self.out[w][w].wait_recv()
            self.on[w].start()

    def forward(self):
        for w in range(2):
            self.out[w][1 - w].wait_recv()
            self.across[1 + w].start()
        for w in range(2):
            self.on[w].wait_recv()
        self.across[3].start()

    def wait(self):
        for w in range(2):
            self.out[w][0].wait_send()
            self.out[w][1].wait_send()
            self.on[w].wait_send()
        for c in self.across + [self.local]:
            c.wait()


def gather_rows(at, own, whole, sem):
    return (SquareGather if at.chips == 4 else Gather)(at, own, whole, sem)


class Gather:
    def __init__(self, at, own, whole, sem):
        rows = own.shape[0]

        def block(i):
            return whole.at[pl.ds(pl.multiple_of(i * rows, rows), rows)]

        self.local = pltpu.make_async_copy(own, block(at.f), sem.at[0, 0])
        self.across = [remote(own, block(at.f), sem.at[0, 1], sem.at[1, 0], "fsdp", at.sib)]
        self.far, self.on = [], []
        for k in range(1, at.chips):
            to = 2 * at.chip_at(k) + at.core
            self.far.append(remote(own, block(at.f), sem.at[2, k], sem.at[3, k], "fsdp", to))
            came = 2 * at.chip_at(at.chips - k) + at.core
            self.on.append(remote(block(came), block(came), sem.at[4, k], sem.at[5, k], "fsdp", at.sib))

    def start(self):
        for c in self.far + self.across + [self.local]:
            c.start()

    def relay(self):
        pass

    def forward(self):
        for far, on in zip(self.far, self.on):
            far.wait_recv()
            on.start()

    def wait(self):
        for c in self.far:
            c.wait_send()
        for c in self.across + self.on + [self.local]:
            c.wait()


class ScatterSum:
    def __init__(self, at, part, near, own, far, sem, made=False):
        self.at, self.part, self.near, self.own, self.far, self.sem, self.made = at, part, near, own, far, sem, made
        self.rows = own.shape[1]
        self.order = list(range(1, at.chips)) + [0]

    def block(self, i):
        return self.part.at[pl.ds(pl.multiple_of(i * self.rows, self.rows), self.rows)]

    def across(self, k):
        at = self.at
        other = self.part.at[k] if self.made else self.block(2 * at.chip_at(k) + 1 - at.core)
        return remote(other, self.near.at[k], self.sem.at[0, k], self.sem.at[1, k], "fsdp", at.sib)

    def load(self, k):
        return pltpu.make_async_copy(
            self.block(2 * self.at.chip_at(k) + self.at.core), self.own.at[k], self.sem.at[2, k])

    def send(self, k):
        at = self.at
        return remote(self.own.at[k], self.far.at[k - 1], self.sem.at[3, k], self.sem.at[4, k], "fsdp",
                      2 * at.chip_at(k) + at.core)

    def start(self):
        for k in self.order:
            self.across(k).start()
            if not self.made:
                self.load(k).start()

    def pass_on(self, k):
        self.across(k).wait()
        if not self.made:
            self.load(k).wait()

        def add(at):
            self.own[k, at] = (self.own[k, at].astype(F32) + self.near[k, at].astype(F32)).astype(BF)

        strips(self.rows, add)

        @pl.when(k > 0)
        def _():
            self.send(k).start()

    def forward(self):
        def step(i, carry):
            self.pass_on(lax.rem(i + 1, self.at.chips))
            return carry

        lax.fori_loop(0, self.at.chips, step, 0)

    def wait(self):
        for k in range(1, self.at.chips):
            self.send(k).wait()

    def total(self, at):
        out = self.own[0, at].astype(F32)
        for k in range(self.at.chips - 1):
            out += self.far[k, at].astype(F32)
        return out


class LineSum:
    def __init__(self, at, chunk, ring, arrive, send, recv, credit, out, out_sem, skip=0, feed=None):
        self.at, self.chunk, self.ring, self.arrive, self.skip = at, chunk, ring, arrive, skip
        self.send, self.recv, self.credit, self.out, self.out_sem = send, recv, credit, out, out_sem
        self.feed = feed
        self.slots = ring.shape[1]
        self.count = chunk.shape[0]
        self.kind = at.mid.astype(jnp.int32)

    def slot(self, j):
        return lax.rem(j, self.slots)

    def inward(self, j):
        return remote(self.chunk.at[j], self.ring.at[self.kind, self.slot(j)], self.send.at[0, j],
                      self.recv.at[self.kind, j], "replica", self.at.inner)

    def outward(self, j, src):
        return remote(src, self.out(j), self.send.at[1, j], self.recv.at[2, j], "replica", self.at.outer)

    def keep(self, j):
        return pltpu.make_async_copy(self.chunk.at[j], self.out(j), self.out_sem.at[j])

    def take_in(self, kind, j, plane):
        here = self.ring.at[kind, self.slot(j)]
        pltpu.make_async_copy(here, here, self.recv.at[kind, j]).wait()
        self.chunk[j] = (self.chunk[j].astype(F32) + self.ring[kind, self.slot(j)].astype(F32)).astype(BF)

        @pl.when(j + self.slots < self.count)
        def _():
            pl.semaphore_signal(self.credit, inc=1, device_id={"replica": plane}, device_id_type=MESH)

    def up(self, j):
        if self.feed:
            @pl.when(j + LEAD < self.count)
            def _():
                self.feed(j + LEAD)

        @pl.when(j >= self.skip)
        def _():
            pltpu.make_async_copy(self.chunk.at[j], self.chunk.at[j], self.arrive.at[j]).wait()

        @pl.when(self.at.has_outer)
        def _():
            self.take_in(0, j, self.at.outer)

        @pl.when(j >= self.slots)
        def _():
            pl.semaphore_wait(self.credit, 1)

        self.inward(j).start()

    def meet(self, j):
        self.inward(j).wait_send()
        self.take_in(1, j, self.at.inner)

        @pl.when(self.at.has_outer)
        def _():
            self.outward(j, self.chunk.at[j]).start()

        self.keep(j).start()

    def take(self, j):
        pltpu.make_async_copy(self.out(j), self.out(j), self.recv.at[2, j]).wait()

        @pl.when(self.at.has_outer)
        def _():
            self.outward(j, self.out(j)).start()

    def settle(self):
        def step(j, carry):
            @pl.when(self.at.mid)
            def _():
                self.keep(j).wait()

            @pl.when(jnp.logical_not(self.at.mid))
            def _():
                self.inward(j).wait_send()

            @pl.when(self.at.has_outer)
            def _():
                self.outward(j, self.chunk.at[j]).wait_send()

            return carry

        lax.fori_loop(0, self.count, step, 0)


class Lines:
    def __init__(self, *lines):
        self.lines = lines
        self.order = [(i, j) for i, line in enumerate(lines) for j in range(line.count)]
        self.at = 0

    def run(self, steps=None, body=None):
        begin = self.at
        last = len(self.order) + LAG_END
        stop = last if steps is None else min(self.at + steps, len(self.order))
        while self.at < stop:
            first, size = self.at, 1
            now = self.parts(first)
            while first + size < stop and self.kinds(first + size) == self.kinds(first):
                size += 1

            def step(m, carry, now=now, first=first):
                up, mid, rest = now
                if up:
                    self.lines[up[0]].up(up[1] + m)
                if mid:
                    @pl.when(self.lines[mid[0]].at.mid)
                    def _():
                        self.lines[mid[0]].meet(mid[1] + m)
                if rest:
                    @pl.when(jnp.logical_not(self.lines[rest[0]].at.mid))
                    def _():
                        self.lines[rest[0]].take(rest[1] + m)
                if body:
                    body(first - begin + m)
                return carry

            lax.fori_loop(0, size, step, 0)
            self.at += size

    def parts(self, t):
        return [self.order[i] if 0 <= i < len(self.order) else None for i in (t, t - LAG_MID, t - LAG_END)]

    def kinds(self, t):
        return [part and part[0] for part in self.parts(t)]

    def settle(self):
        for line in self.lines:
            line.settle()


def rms_of(values):
    return lax.rsqrt(jnp.mean(values * values, axis=-1, keepdims=True) + EPSILON)


def qkv_pieces(at, w, wc, qw):
    q_w, k_w = QUERY_HEADS * HEAD_WIDTH, KEY_VALUE_HEADS * HEAD_WIDTH
    shared = at.n // KEY_VALUE_HEADS
    depth = w.shape[0]

    def cols(start, width):
        return pl.ds(pl.multiple_of(start, HEAD_WIDTH), width)

    def rows(s):
        return pl.ds(pl.multiple_of(s * depth, depth), depth)

    return [
        (lambda t: w.at[:, cols(t * qw, qw)], lambda s: wc.at[rows(s), pl.ds(0, qw)]),
        (lambda t: w.at[:, cols(q_w + t // shared * HEAD_WIDTH, HEAD_WIDTH)],
         lambda s: wc.at[rows(s), pl.ds(qw, HEAD_WIDTH)]),
        (lambda t: w.at[:, cols(q_w + k_w + t // shared * HEAD_WIDTH, HEAD_WIDTH)],
         lambda s: wc.at[rows(s), pl.ds(qw + HEAD_WIDTH, HEAD_WIDTH)]),
    ]


def col_piece(w, wc, share):
    depth = w.shape[0]
    return (lambda t: w.at[:, pl.ds(pl.multiple_of(t * share, HEAD_WIDTH), share)],
            lambda s: wc.at[pl.ds(pl.multiple_of(s * depth, depth), depth)])


class Weights:
    def __init__(self, at, pieces, send, recv, z_send, z_recv):
        self.at, self.pieces, self.send, self.recv, self.z_send, self.z_recv = at, pieces, send, recv, z_send, z_recv
        self.mine = at.core == lax.rem(at.z, 2)
        self.parity = lax.rem(at.z + at.core, 2)
        self.partner = at.z + 1 - 2 * lax.rem(at.z, 2)

    def cols(self, i, t):
        return self.pieces[i][0](t)

    def rows(self, i, s):
        return self.pieces[i][1](s)

    def local(self, i):
        return pltpu.make_async_copy(self.cols(i, self.at.f), self.rows(i, self.at.f), self.recv.at[i, 0])

    def copy(self, i, j):
        to = self.at.near(j)
        return remote(self.cols(i, to), self.rows(i, self.at.f), self.send.at[i, j], self.recv.at[i, j], "fsdp", to)

    def beside(self, i, j):
        here = self.rows(i, self.at.near_from(j))
        return remote(here, here, self.z_send.at[i, j], self.z_recv.at[i, j], "replica", self.partner)

    def start(self, i):
        self.local(i).start()
        self.copy(i, 1).start()

        @pl.when(self.mine)
        def _():
            for j in range(2, self.at.n):
                self.copy(i, j).start()

    def hand_over(self, i):
        for m in range(1, self.at.chips):
            j = 2 * m + self.parity
            here = self.rows(i, self.at.near_from(j))
            pltpu.make_async_copy(here, here, self.recv.at[i, j]).wait()
            self.beside(i, j).start()

    def wait(self, i):
        self.local(i).wait()
        self.copy(i, 1).wait()

        @pl.when(self.mine)
        def _():
            for j in range(2, self.at.n):
                self.copy(i, j).wait_send()

        for m in range(1, self.at.chips):
            self.beside(i, 2 * m + self.parity).wait_send()
            self.beside(i, 2 * m + 1 - self.parity).wait_recv()


def front_kernel(n, n_z, x_ref, gain1_ref, gain2_ref, gainq_ref, gaink_ref, place_ref, table_ref, wout_ref,
                 wqkv_ref, g_ref, gate_ref, up_ref, down_ref,
                 h_ref, q_ref, kv_ref, ctx_ref, proj_ref, places_ref,
                 n1_ref, wc_ref, n2_ref, gall_ref, gate_c, up_c, down_c,
                 near, mine, far, stage, own, n1_block, wc,
                 s_x, r_x, s_p, r_p, s_g, s_n, s_w, s_h, s_r, s_a, s_b, s_c, r_c, s_z, r_z, s_xz, r_xz):
    at = Place(n, n_z)
    rows = x_ref.shape[0]
    heads = QUERY_HEADS // n
    qw = heads * HEAD_WIDTH
    halo = LMAX
    at.greet(True)
    weights = Weights(at, qkv_pieces(at, wqkv_ref, wc_ref, qw), s_x, r_x, s_xz, r_xz)
    for i in range(3):
        weights.start(i)

    def rows_of(g):
        return pl.ds(pl.multiple_of(g * rows, rows), rows)

    places = Exchange(at, [(lambda t: place_ref, lambda s: places_ref.at[rows_of(s)])], s_p, r_p)
    share = gate_c.shape[1]
    mlp = Weights(
        at, [col_piece(gate_ref, gate_c, share), col_piece(up_ref, up_c, share), col_piece(down_ref, down_c, share)],
        s_c, r_c, s_z, r_z)
    places.start()

    def norm1(strip):
        x = x_ref[strip].astype(F32)
        own[strip] = (x * rms_of(x) * gain1_ref[...]).astype(BF)

    strips(rows, norm1)
    n1 = gather_rows(at, own, n1_ref, s_g)
    n1.start()
    n1.relay()
    for i in range(3):
        weights.hand_over(i)
    n1.forward()
    n1.wait()
    places.wait()
    for i in range(3):
        weights.wait(i)
    mlp.start(0)
    mlp.start(1)
    to_vmem = pltpu.make_async_copy(wc_ref, wc, s_w.at[0])
    to_vmem.start()

    def block_of(g):
        return pltpu.make_async_copy(n1_ref.at[rows_of(g)], n1_block.at[lax.rem(g, 2)], s_n.at[lax.rem(g, 2)])

    block_of(0).start()
    to_vmem.wait()

    def project(g, carry):
        @pl.when(g + 1 < n)
        def _():
            block_of(g + 1).start()

        at_rows = rows_of(g)
        cosine, sine = rotation_of(places_ref[at_rows], table_ref)
        block_of(g).wait()
        proj = dot(n1_block[lax.rem(g, 2)], wc[...])
        proj_ref[at_rows] = proj[:, :qw + HEAD_WIDTH]
        for head in range(heads + 1):
            lanes = slice(head * HEAD_WIDTH, (head + 1) * HEAD_WIDTH)
            raw = proj[:, lanes]
            gain = gainq_ref if head < heads else gaink_ref
            turned = rotate_with(raw * rms_of(raw) * gain[...], cosine, sine).astype(BF)
            if head < heads:
                q_ref[at_rows, lanes] = turned
            else:
                kv_ref[g, halo:, :HEAD_WIDTH] = turned
        kv_ref[g, halo:, HEAD_WIDTH:] = proj[:, qw + HEAD_WIDTH:].astype(BF)
        return carry

    lax.fori_loop(0, n, project, 0)
    not_first, not_last = at.z > 0, at.z < n_z - 1

    def halo_copy():
        return remote(kv_ref.at[:, pl.ds(rows, halo)], kv_ref.at[:, pl.ds(0, halo)], s_h.at[0], s_h.at[1], "replica",
                      jnp.minimum(at.z + 1, n_z - 1))

    @pl.when(not_last)
    def _():
        halo_copy().start()

    @pl.when(not_first)
    def _():
        here = kv_ref.at[:, pl.ds(0, halo)]
        pltpu.make_async_copy(here, here, s_h.at[1]).wait()

    @pl.when(jnp.logical_not(not_first))
    def _():
        kv_ref[:, :halo] = jnp.zeros((n, halo, 2 * HEAD_WIDTH), BF)

    sum_o = ScatterSum(at, stage, near, mine, far, s_r, made=True)

    def attend(g):
        at_rows = rows_of(g)
        mask = window_mask(places_ref[at_rows], rows, halo)
        keys, values = kv_ref[g, :, :HEAD_WIDTH], kv_ref[g, :, HEAD_WIDTH:]
        for head in range(heads):
            lanes = slice(head * HEAD_WIDTH, (head + 1) * HEAD_WIDTH)
            probs = softmax_of(q_ref[at_rows, lanes], keys, mask).astype(BF)
            ctx_ref[at_rows, lanes] = dot(probs, values).astype(BF)
        return dot(ctx_ref[at_rows], wout_ref[...]).astype(BF)

    def attend_both(i, carry):
        k = lax.rem(i + 1, at.chips)
        q = at.chip_at(k)
        stage[k] = attend(2 * q + 1 - at.core)
        sum_o.across(k).start()
        mine[k] = attend(2 * q + at.core)

        @pl.when(i > 0)
        def _():
            sum_o.pass_on(jnp.maximum(i, 1))

        return carry

    lax.fori_loop(0, at.chips, attend_both, 0)
    sum_o.pass_on(0)
    mlp.start(2)
    mlp.hand_over(0)
    sum_o.wait()

    def norm2(strip):
        h = x_ref[strip].astype(F32) + sum_o.total(strip)
        h_ref[strip] = h
        own[strip] = (h * rms_of(h) * gain2_ref[...]).astype(BF)

    strips(rows, norm2)
    n2 = gather_rows(at, own, n2_ref, s_a)
    g_all = gather_rows(at, g_ref, gall_ref, s_b)
    n2.start()
    mlp.hand_over(1)
    n2.relay()
    g_all.start()
    n2.forward()
    g_all.relay()
    mlp.hand_over(2)
    g_all.forward()
    n2.wait()
    g_all.wait()

    @pl.when(not_last)
    def _():
        halo_copy().wait_send()

    for i in range(3):
        mlp.wait(i)


class Feed:
    def __init__(self, at, grads, chunk, send, recv):
        self.at, self.grads, self.chunk, self.send, self.recv = at, grads, chunk, send, recv
        self.depth = chunk.shape[1]

    def rows(self, grad, t):
        return grad.at[pl.ds(pl.multiple_of(t * self.depth, self.depth), self.depth)]

    def copy(self, grad, c, j):
        to = self.at.near(j)
        return remote(self.rows(grad, to), self.chunk.at[c], self.send.at[c], self.recv.at[c], "fsdp", to)

    def start(self, c):
        n = self.at.n
        j = lax.rem(c, n)
        for i, grad in enumerate(self.grads):
            @pl.when((c // n == i) & (j == 0))
            def _(grad=grad):
                pltpu.make_async_copy(self.rows(grad, self.at.f), self.chunk.at[c], self.recv.at[c]).start()

            @pl.when((c // n == i) & (j > 0))
            def _(grad=grad):
                self.copy(grad, c, j).start()

    def settle(self):
        def step(c, carry):
            @pl.when(lax.rem(c, self.at.n) > 0)
            def _():
                self.copy(self.grads[0], c, lax.rem(c, self.at.n)).wait_send()

            return carry

        lax.fori_loop(0, len(self.grads) * self.at.n, step, 0)


def start_all(copies):
    for c in copies:
        c.start()


def rotate_with(values, cosine, sine):
    return values * cosine + pltpu.roll(values, HEAD_WIDTH // 2, 1) * sine


def rotation_table():
    places = HEAD_WIDTH * -(-LMAX // HEAD_WIDTH)
    inverse = ROPE_BASE ** (-(2.0 * np.arange(HEAD_WIDTH // 2)) / HEAD_WIDTH)
    angles = np.arange(places)[:, None] * inverse[None, :]
    cosine, sine = np.cos(angles), np.sin(angles)
    rest = np.concatenate([cosine, cosine, -sine, sine], axis=1).astype(np.float32)
    terms = []
    for _ in range(3):
        terms.append(rest.astype(jnp.bfloat16))
        rest = rest - terms[-1].astype(np.float32)
    return jnp.asarray(np.stack(terms))


def rotation_of(places, table):
    lane = lax.broadcasted_iota(jnp.int32, (places.shape[0], table.shape[1]), 1).astype(F32)
    pick = (lane == places.astype(F32)[:, :1]).astype(F32).astype(BF)
    both = dot(pick, table[0]) + dot(pick, table[1]) + dot(pick, table[2])
    return both[:, :HEAD_WIDTH], both[:, HEAD_WIDTH:]


def window_mask(places, rows, halo):
    i_at = lax.broadcasted_iota(jnp.int32, (rows, halo + rows), 0) + halo
    j_at = lax.broadcasted_iota(jnp.int32, (rows, halo + rows), 1)
    back = (i_at - j_at).astype(F32)
    return (back >= 0) & (back <= places.astype(F32)[:, :1])


def softmax_of(queries, keys, mask):
    scores = jnp.where(mask, dot_cols(queries, keys) * HEAD_WIDTH ** (-0.5), NEG_FILL)
    terms = jnp.exp(scores - jnp.max(scores, axis=1, keepdims=True))
    return terms / jnp.sum(terms, axis=1, keepdims=True)


def back_kernel(n, n_z, part_ref, party_ref, x_ref, h_ref, g_ref, gain1_ref, gain2_ref, gainq_ref, gaink_ref,
                down_ref, n2_ref, dgate_ref, dup_ref, wout_ref, wqkv_ref, q_ref, kv_ref, ctx_ref, proj_ref, table_ref, place_ref,
                n1_ref,
                dx_ref, y_ref, gains_ref, gmlp_ref, gqkv_ref, dhall_ref, gate_ref, up_ref,
                near, mine, far, stage, dh, plane_gain, all_gain,
                chunk, ring, chunk2, ring2, dh_block, gout, d_kv, d_proj, halo_out, halo_in, n1_cols, qkv_send, d_in, tile_out,
                s_r, s_a, s_p, r_p, s_q, r_q, s_c, r_c, s_z, r_z, s_o, s_c2, r_c2, s_z2, r_z2, s_o2, credit, done, s_d, s_n, s_h, s_e, s_t):
    at = Place(n, n_z)
    share, share_out = chunk.shape[2], chunk2.shape[2]
    rows, width = x_ref.shape
    depth = chunk.shape[1]
    outs = -(-width // share_out)
    heads = QUERY_HEADS // n
    qw = heads * HEAD_WIDTH
    halo = LMAX
    scale = HEAD_WIDTH ** (-0.5)
    own = dh_block
    own_gain = all_gain.at[at.z]
    at.greet(True)

    def mlp_place(j):
        s = at.near_from(lax.rem(j, n))
        return gmlp_ref.at[j // n, :, pl.ds(pl.multiple_of(s * share, HEAD_WIDTH), share)]

    def attn_place(j):
        col = jnp.where(j < outs, j, outs + at.near_from(jnp.maximum(j - outs, 0)))
        return gqkv_ref.at[:, pl.ds(pl.multiple_of(col * share_out, HEAD_WIDTH), share_out)]

    feed = Feed(at, (down_ref, gate_ref, up_ref), chunk, s_c, r_c)
    lines = Lines(
        LineSum(at, chunk, ring, r_c, s_z, r_z, credit.at[0], mlp_place, s_o, 0, feed.start),
        LineSum(at, chunk2, ring2, r_c2, s_z2, r_z2, credit.at[1], attn_place, s_o2, outs))
    sum_n2 = ScatterSum(at, part_ref, near, mine, far, s_r.at[0])
    for c in range(LEAD):
        feed.start(jnp.int32(c))
    sum_n2.start()
    load = pltpu.make_async_copy(dgate_ref, d_in, s_e.at[0])
    load.start()
    lines.run(1)
    sum_n2.forward()

    def fetch_cols(ref, j):
        return pltpu.make_async_copy(
            ref.at[:, pl.ds(pl.multiple_of(at.near(j) * depth, depth), depth)], n1_cols.at[lax.rem(j, 2)],
            s_n.at[lax.rem(j, 2)])

    def tiles(ref, per):
        def put(j):
            return pltpu.make_async_copy(
                tile_out.at[lax.rem(j, 2)], ref.at[pl.ds(pl.multiple_of(at.near(j) * depth, depth), depth)],
                s_t.at[lax.rem(j, 2)])

        def tile(j):
            @pl.when(j + 1 < n)
            def _():
                fetch_cols(n2_ref, j + 1).start()

            fetch_cols(n2_ref, j).wait()

            @pl.when(j > 1)
            def _():
                put(j - 2).wait()

            tile_out[lax.rem(j, 2)] = dot_rows(n1_cols[lax.rem(j, 2)], d_in[...]).astype(BF)
            put(j).start()

        def body(step):
            for r in range(per):
                j = step * per + r

                @pl.when(j < n)
                def _(j=j):
                    tile(j)

        def end():
            put(n - 2).wait()
            put(n - 1).wait()

        fetch_cols(n2_ref, 0).start()
        return body, end

    per_tile = -(-n // 3)
    load.wait()
    body, end = tiles(gate_ref, per_tile)
    lines.run(3, body)
    end()
    load = pltpu.make_async_copy(dup_ref, d_in, s_e.at[0])
    load.start()
    lines.run(n - 8)
    sum_n2.wait()
    own_gain[...] = jnp.zeros_like(own_gain)

    def back_mlp(strip):
        d_n2 = sum_n2.total(strip)
        h = h_ref[strip]
        r2 = rms_of(h)
        u2 = h * r2
        own_gain[1:2] += jnp.sum(d_n2 * u2, axis=0, keepdims=True)
        d_h = g_ref[strip].astype(F32) + norm_back(d_n2 * gain2_ref[...], u2, r2)
        dh[strip] = d_h
        own[strip] = d_h.astype(BF)

    strips(rows, back_mlp)
    gather = gather_rows(at, own, dhall_ref, s_a)
    gather.start()
    load.wait()
    body, end = tiles(up_ref, per_tile)
    lines.run(3, body)
    end()
    lines.run(n // 2 - 4)
    gather.relay()
    lines.run(2)
    gather.forward()
    lines.run(1)
    gather.wait()
    sum_y = ScatterSum(at, party_ref, near, mine, far, s_r.at[2])
    sum_y.start()
    lines.run(1)
    sum_y.forward()
    gout[...] = jnp.zeros_like(gout)

    def rows_of(g):
        return pl.ds(pl.multiple_of(g * rows, rows), rows)

    def block_of(g):
        return pltpu.make_async_copy(dhall_ref.at[rows_of(g)], dh_block, s_d.at[0])

    def attention(g):
        at_rows = rows_of(g)
        block_of(g).start()
        mask = window_mask(place_ref[at_rows], rows, halo)
        keys, values = kv_ref[g, :, :HEAD_WIDTH], kv_ref[g, :, HEAD_WIDTH:]
        cosine, sine = rotation_of(place_ref[at_rows], table_ref)
        block_of(g).wait()
        d_ctx = dot_cols(dh_block[...], wout_ref[...]).astype(BF)
        gout[:, :width] += dot_rows(ctx_ref[at_rows], dh_block[...])
        d_k = jnp.zeros((halo + rows, HEAD_WIDTH), F32)
        d_v = jnp.zeros((halo + rows, HEAD_WIDTH), F32)
        for head in range(heads):
            lanes = slice(head * HEAD_WIDTH, (head + 1) * HEAD_WIDTH)
            queries, d_c = q_ref[at_rows, lanes], d_ctx[:, lanes]
            probs = softmax_of(queries, keys, mask)
            d_v += dot_rows(probs.astype(BF), d_c)
            d_p = dot_cols(d_c, values)
            d_s = (probs * (d_p - jnp.sum(probs * d_p, axis=1, keepdims=True))).astype(BF)
            d_k += dot_rows(d_s, queries) * scale
            dq_g = rotate_with(dot(d_s, keys) * scale, cosine, -sine)
            raw = proj_ref[at_rows, lanes]
            rms = rms_of(raw)
            hat = raw * rms
            own_gain[2:3, :HEAD_WIDTH] += jnp.sum(dq_g * hat, axis=0, keepdims=True)
            d_proj[at_rows, lanes] = norm_back(dq_g * gainq_ref[...], hat, rms).astype(BF)
        halo_out[g, :, :HEAD_WIDTH] = d_k[:halo].astype(BF)
        halo_out[g, :, HEAD_WIDTH:] = d_v[:halo].astype(BF)
        d_kv[g, :, :HEAD_WIDTH] = d_k[halo:]
        d_kv[g, :, HEAD_WIDTH:] = d_v[halo:]

    lines.run(n, attention)

    not_first, not_last = at.z > 0, at.z < n_z - 1

    def halo_copy():
        return remote(halo_out, halo_in, s_h.at[0], s_h.at[1], "replica", jnp.maximum(at.z - 1, 0))

    @pl.when(not_first)
    def _():
        halo_copy().start()

    for i in range(outs):
        chunk2[i] = gout[:, i * share_out:(i + 1) * share_out].astype(BF)
    lines.run(1)
    sum_y.wait()

    def finish(strip):
        y_ref[strip] = (h_ref[strip] + sum_y.total(strip)).astype(BF)

    strips(rows, finish)
    for k in range(1, n):
        pl.semaphore_signal(done, inc=1, device_id={"fsdp": at.to(k)}, device_id_type=MESH)

    @pl.when(not_last)
    def _():
        pltpu.make_async_copy(halo_in, halo_in, s_h.at[1]).wait()

    @pl.when(jnp.logical_not(not_last))
    def _():
        halo_in[...] = jnp.zeros_like(halo_in)

    def keys_back(g):
        at_rows = rows_of(g)
        d_kv[g, rows - halo:] += halo_in[g].astype(F32)
        cosine, sine = rotation_of(place_ref[at_rows], table_ref)
        dk_g = rotate_with(d_kv[g, :, :HEAD_WIDTH], cosine, -sine)
        raw = proj_ref[at_rows, qw:qw + HEAD_WIDTH]
        rms = rms_of(raw)
        hat = raw * rms
        own_gain[2:3, HEAD_WIDTH:2 * HEAD_WIDTH] += jnp.sum(dk_g * hat, axis=0, keepdims=True)
        d_proj[at_rows, qw:qw + HEAD_WIDTH] = norm_back(dk_g * gaink_ref[...], hat, rms).astype(BF)
        d_proj[at_rows, qw + HEAD_WIDTH:] = d_kv[g, :, HEAD_WIDTH:].astype(BF)

    per_step = n // 2

    def keys_back_some(i):
        for m in range(per_step):
            keys_back(i * per_step + m)

    lines.run(2, keys_back_some)

    def cols_of(j):
        return fetch_cols(n1_ref, j)

    own_qkv = pltpu.make_async_copy(qkv_send.at[0], chunk2.at[outs], r_c2.at[outs])

    def qkv_copy(j):
        return remote(qkv_send.at[j], chunk2.at[outs + j], s_c2.at[j], r_c2.at[outs + j], "fsdp", at.near(j))

    cols_of(0).start()

    def qkv_grad(j):
        @pl.when(j + 1 < n)
        def _():
            cols_of(j + 1).start()

        cols_of(j).wait()
        qkv_send[j] = dot_rows(n1_cols[lax.rem(j, 2)], d_proj[...]).astype(BF)

        @pl.when(j == 0)
        def _():
            own_qkv.start()

        @pl.when(j > 0)
        def _():
            qkv_copy(j).start()

    per_out = n // 4

    def qkv_grads(i):
        for m in range(per_out):
            qkv_grad(i * per_out + m)

    sum_n1 = ScatterSum(at, stage, near, mine, far, s_r.at[1], made=True)

    def n1_part(k):
        q = at.chip_at(k)
        stage[k] = dot_cols(d_proj[rows_of(2 * q + 1 - at.core)], wqkv_ref[...]).astype(BF)
        mine[k] = dot_cols(d_proj[rows_of(2 * q + at.core)], wqkv_ref[...]).astype(BF)

    def both(i):
        qkv_grads(i)
        for r in range(at.chips // 4):
            n1_part(i * (at.chips // 4) + r)

    lines.run(4, both)
    pl.semaphore_wait(done, n - 1)
    sum_n1.start()
    lines.run(1)
    sum_n1.forward()
    lines.run(outs + n - 4 - 1 - 2 - -2)
    sum_n1.wait()

    def back_attn(strip):
        d_n1 = sum_n1.total(strip)
        x = x_ref[strip].astype(F32)
        r1 = rms_of(x)
        u1 = x * r1
        own_gain[0:1] += jnp.sum(d_n1 * u1, axis=0, keepdims=True)
        dx_ref[strip] = (dh[strip] + norm_back(d_n1 * gain1_ref[...], u1, r1)).astype(BF)

    strips(rows, back_attn)
    gains = Exchange(at, [(lambda t: own_gain, lambda s: plane_gain.at[s])], s_p, r_p)
    gains.start()
    lines.run(1)
    gains.wait()
    own_gain[...] = jnp.sum(plane_gain[...], axis=0)
    others = [
        remote(own_gain, all_gain.at[at.z], s_q.at[k], r_q.at[k], "replica", at.plane(k)) for k in range(1, n_z)]
    start_all(others)
    lines.run()
    for c in others:
        c.wait()
    gains_ref[...] = jnp.sum(all_gain[...], axis=0)
    feed.settle()
    for j in range(1, n):
        qkv_copy(j).wait_send()

    @pl.when(not_first)
    def _():
        halo_copy().wait_send()

    lines.settle()


def front(n, n_z, x, gain1, gain2, gain_q, gain_k, place, table, w_out, w_qkv, g, gate, up, down):
    rows, width = x.shape
    chips, share, total = n // 2, gate.shape[1] // n, n * rows
    qw = QUERY_HEADS * HEAD_WIDTH // n
    wide = qw + 2 * HEAD_WIDTH
    block = functools.partial(pltpu.VMEM, dtype=BF)
    shape = jax.ShapeDtypeStruct
    return pl.pallas_call(
        functools.partial(front_kernel, n, n_z),
        out_shape=(
            shape((rows, width), F32), shape((total, qw), BF), shape((n, LMAX + rows, 2 * HEAD_WIDTH), BF),
            shape((total, qw), BF), shape((total, qw + HEAD_WIDTH), F32), shape((total, HEAD_WIDTH), BF),
            shape((total, width), BF), shape((width, wide), BF), shape((total, width), BF), shape((total, width), BF),
        ) + (shape((width, share), BF),) * 3,
        in_specs=[VMEM] * 8 + [ANY] * 5,
        out_specs=(VMEM,) * 6 + (ANY,) * 7,
        scratch_shapes=[
            block((chips, rows, width)), block((chips, rows, width)), block((chips - 1, rows, width)),
            block((chips, rows, width)), block((rows, width)), block((2, rows, width)), block((width, wide)),
            DMA((3, n)), DMA((3, n)), DMA((1, n)), DMA((1, n)), DMA((6, n)), DMA((2,)), DMA((1,)), DMA((2,)),
            DMA((5, n)), DMA((6, n)), DMA((6, n)), DMA((3, n)), DMA((3, n)), DMA((3, n)), DMA((3, n)),
            DMA((3, n)), DMA((3, n))],
        compiler_params=pltpu.CompilerParams(collective_id=0, has_side_effects=True, vmem_limit_bytes=60 << 20),
        name="front",
    )(x, gain1, gain2, gain_q, gain_k, place, table, w_out, w_qkv, g, gate, up, down)


def back(n, n_z, part, part_y, x, h, g, gain1, gain2, gain_q, gain_k, down, n2, d_gate, d_up, w_out, w_qkv, q, kv, ctx, proj,
         table, places, n1):
    rows, width = x.shape
    chips, share, wide, depth = n // 2, down.shape[1], w_qkv.shape[1], width // n
    outs = -(-width // wide)
    block = functools.partial(pltpu.VMEM, dtype=BF)
    gains = (8, width)
    count2 = outs + n
    slots = 2 + 16 // n
    return pl.pallas_call(
        functools.partial(back_kernel, n, n_z),
        out_shape=(
            jax.ShapeDtypeStruct((rows, width), BF),
            jax.ShapeDtypeStruct((rows, width), BF),
            jax.ShapeDtypeStruct(gains, F32),
            jax.ShapeDtypeStruct((3, depth, n * share), BF),
            jax.ShapeDtypeStruct((depth, count2 * wide), BF),
            jax.ShapeDtypeStruct((n * rows, width), BF),
            jax.ShapeDtypeStruct((width, share), BF),
            jax.ShapeDtypeStruct((width, share), BF),
        ),
        in_specs=[ANY, ANY] + [VMEM] * 7 + [ANY] * 4 + [VMEM] * 8 + [ANY],
        out_specs=(VMEM, VMEM, VMEM, ANY, ANY, ANY, ANY, ANY),
        scratch_shapes=[
            block((chips, rows, width)), block((chips, rows, width)), block((chips - 1, rows, width)),
            block((chips, rows, width)), pltpu.VMEM((rows, width), F32),
            pltpu.VMEM((n,) + gains, F32), pltpu.VMEM((n_z,) + gains, F32),
            block((3 * n, depth, share)), block((2, slots, depth, share)),
            block((count2, depth, wide)), block((2, slots, depth, wide)),
            block((rows, width)), pltpu.VMEM((depth, outs * wide), F32),
            pltpu.VMEM((n, rows, 2 * HEAD_WIDTH), F32), block((n * rows, wide)),
            block((n, LMAX, 2 * HEAD_WIDTH)), block((n, LMAX, 2 * HEAD_WIDTH)),
            block((2, n * rows, depth)), block((n, depth, wide)), block((n * rows, share)), block((2, depth, share)),
            DMA((3, 5, n)), DMA((6, n)), DMA((1, n)), DMA((1, n)), DMA((n_z,)), DMA((n_z,)),
            DMA((3 * n,)), DMA((3 * n,)), DMA((2, 3 * n)), DMA((3, 3 * n)), DMA((3 * n,)),
            DMA((n,)), DMA((count2,)), DMA((2, count2)), DMA((3, count2)), DMA((count2,)),
            pltpu.SemaphoreType.REGULAR((2,)), pltpu.SemaphoreType.REGULAR, DMA((1,)), DMA((2,)), DMA((2,)), DMA((1,)), DMA((2,))],
        compiler_params=pltpu.CompilerParams(collective_id=2, has_side_effects=True, vmem_limit_bytes=511 << 17),
        name="back",
    )(part, part_y, x, h, g, gain1, gain2, gain_q, gain_k, down, n2, d_gate, d_up, w_out, w_qkv, q, kv, ctx, proj, table, places, n1)


def row_positions(flat_lens, ranks, first_row, count):
    earlier = (ranks[:, None] < ranks[None, :]).astype(jnp.int32)
    starts = jnp.sum(flat_lens[:, None] * earlier, axis=0)
    rows = first_row + jnp.arange(count, dtype=jnp.int32)
    begun = jnp.where(starts[None, :] <= rows[:, None], starts[None, :], 0)
    return rows - jnp.max(begun, axis=1)


def per_device(
    n_replica, tokens, cotangent, w_qkv, w_out, w_gate, w_up, w_down_t,
    gain_attn, gain_mlp, gain_query, gain_key, dealt_lens, seq_order,
):
    rows, width = tokens.shape
    n_fsdp = width // w_qkv.shape[0]
    q_w = QUERY_HEADS * HEAD_WIDTH
    k_w = KEY_VALUE_HEADS * HEAD_WIDTH
    replica = lax.axis_index("replica")
    shared = n_fsdp // KEY_VALUE_HEADS
    heads = QUERY_HEADS // n_fsdp
    qw = heads * HEAD_WIDTH

    pos = row_positions(dealt_lens[0].reshape(-1), seq_order[0], replica * rows, rows)
    depth = w_qkv.shape[0]
    place = jnp.broadcast_to(pos.astype(BF)[:, None], (rows, HEAD_WIDTH))
    table = rotation_table()
    gains = (gain_attn[None], gain_mlp[None], gain_query[None], gain_key[None])
    h, q_low, kv_window, ctx_low, proj, places, n1, w_qkv_c, n2, g_all, gate_c, up_c, down_c = front(
        n_fsdp, n_replica, tokens, *gains, place, table, w_out, w_qkv, cotangent, w_gate, w_up, w_down_t)

    gate = dot(n2, gate_c)
    up = dot(n2, up_c)
    sg = jax.nn.sigmoid(gate)
    silu = gate * sg
    act = (silu * up).astype(BF)
    part_y = dot_cols(act, down_c).astype(BF)

    d_act = dot(g_all, down_c)
    d_gate = (d_act * up * sg * (1.0 + gate * (1.0 - sg))).astype(BF)
    d_up = (d_act * silu).astype(BF)

    input_grad, output, gain_sums, g_mlp, g_attn, _, _, _ = back(
        n_fsdp, n_replica, (dot_cols(d_gate, gate_c) + dot_cols(d_up, up_c)).astype(BF), part_y, tokens, h, cotangent, *gains,
        dot_rows(g_all, act).astype(BF), n2, d_gate, d_up,
        w_out, w_qkv_c, q_low, kv_window, ctx_low, proj, table, places, n1)
    wide = qw + 2 * HEAD_WIDTH
    g_out = g_attn[:, :width]
    by_device = [g_attn[:, at:at + wide] for at in range(g_attn.shape[1] - n_fsdp * wide, g_attn.shape[1], wide)]

    def of_key_heads(first):
        parts = [part[:, first:first + HEAD_WIDTH].astype(F32) for part in by_device]
        return [sum(parts[i + 1:i + shared], parts[i]) for i in range(0, n_fsdp, shared)]

    g_qkv = jnp.concatenate(
        [part[:, :qw].astype(F32) for part in by_device] + of_key_heads(qw) + of_key_heads(qw + HEAD_WIDTH), axis=1)
    return (
        output, input_grad, g_qkv, g_out.astype(F32), g_mlp[1].astype(F32), g_mlp[2].astype(F32), g_mlp[0].astype(F32),
        gain_sums[0], gain_sums[1], gain_sums[2, :HEAD_WIDTH], gain_sums[2, HEAD_WIDTH:2 * HEAD_WIDTH])


def solution(mesh):
    n_replica = mesh.shape["replica"]

    def program(*args):
        return per_device(n_replica, *args)

    rows = P(("fsdp", "replica"), None)
    weight = P("fsdp", None)
    return jax.shard_map(
        program,
        mesh=mesh,
        in_specs=(rows, rows) + (weight,) * 5 + (P(),) * 4 + (P("fsdp", None, None), P("fsdp", None)),
        out_specs=(rows, rows) + (weight,) * 5 + (P(),) * 4,
        check_vma=False,
    )
```

```python
import functools

import jax
import jax.numpy as jnp
import numpy as np
from jax import lax
from jax.experimental import pallas as pl
from jax.experimental.pallas import tpu as pltpu
from jax.sharding import PartitionSpec as P

QUERY_HEADS = 16
KEY_VALUE_HEADS = 8
HEAD_WIDTH = 128
LMAX = 96

EPSILON = 1e-06
ROPE_BASE = 1000000.0
NEG_FILL = -1e30
BF = jnp.bfloat16
F32 = jnp.float32


MESH = pl.DeviceIdType.MESH
ANY = pl.BlockSpec(memory_space=pl.ANY)
VMEM = pl.BlockSpec(memory_space=pltpu.VMEM)
DMA = pltpu.SemaphoreType.DMA
STRIP = 16
LAG_MID = 2
LAG_END = 6
LEAD = 5


def dot(left, right):
    return jnp.dot(left, right, preferred_element_type=F32)


def dot_rows(left, right):
    return lax.dot_general(left, right, (((0,), (0,)), ((), ())), preferred_element_type=F32)


def dot_cols(left, right):
    return lax.dot_general(left, right, (((1,), (1,)), ((), ())), preferred_element_type=F32)


def norm_back(d_normed, normed, rms):
    return rms * (d_normed - normed * jnp.mean(d_normed * normed, axis=-1, keepdims=True))


class Place:
    def __init__(self, n, n_z):
        self.n, self.chips, self.n_z = n, n // 2, n_z
        self.f = lax.axis_index("fsdp")
        self.chip, self.core = self.f // 2, lax.rem(self.f, 2)
        self.sib = self.f + 1 - 2 * self.core
        self.z = lax.axis_index("replica")
        low = (self.z < n_z // 2).astype(jnp.int32)
        self.inner = self.z - 1 + 2 * low
        self.outer = self.z + 1 - 2 * low
        self.mid = (self.z == n_z // 2 - 1) | (self.z == n_z // 2)
        self.has_outer = (self.z > 0) & (self.z < n_z - 1)

    def to(self, k):
        return lax.rem(self.f + k, self.n)

    def near(self, j):
        return 2 * lax.rem(self.chip + j // 2, self.chips) + lax.rem(self.core + lax.rem(j, 2), 2)

    def near_from(self, j):
        return 2 * lax.rem(self.chip + self.chips - j // 2, self.chips) + lax.rem(self.core + lax.rem(j, 2), 2)

    def plane(self, k):
        return lax.rem(self.z + k, self.n_z)

    def chip_at(self, k):
        return lax.rem(self.chip + k, self.chips)

    def greet(self, line):
        barrier = pltpu.get_barrier_semaphore()
        for k in range(1, self.n):
            pl.semaphore_signal(barrier, inc=1, device_id={"fsdp": self.to(k)}, device_id_type=MESH)
        if line:
            for k in range(1, self.n_z):
                pl.semaphore_signal(barrier, inc=1, device_id={"replica": self.plane(k)}, device_id_type=MESH)

        pl.semaphore_wait(barrier, self.n - 1 + (self.n_z - 1 if line else 0))


def remote(src, dst, send, recv, axis, index):
    return pltpu.make_async_remote_copy(
        src_ref=src, dst_ref=dst, send_sem=send, recv_sem=recv, device_id={axis: index}, device_id_type=MESH)


def strips(rows, body):
    def step(i, carry):
        body(pl.ds(pl.multiple_of(i * STRIP, STRIP), STRIP))
        return carry

    lax.fori_loop(0, rows // STRIP, step, 0)


class Exchange:
    def __init__(self, at, pieces, send, recv):
        self.copies, self.local = [], []
        for i, (src, dst) in enumerate(pieces):
            self.local.append(pltpu.make_async_copy(src(at.f), dst(at.f), recv.at[i, 0]))
            for k in range(1, at.n):
                self.copies.append(remote(src(at.to(k)), dst(at.f), send.at[i, k], recv.at[i, k], "fsdp", at.to(k)))

    def start(self):
        for c in self.copies + self.local:
            c.start()

    def wait(self):
        for c in self.copies + self.local:
            c.wait()


class SquareGather:
    def __init__(self, at, own, whole, sem):
        rows = own.shape[0]
        half = rows // 2
        beside = (2 * (at.chip + 1 - 2 * lax.rem(at.chip, 2)) + at.core, 2 * at.chip_at(2) + at.core)

        def part(i, h):
            return whole.at[pl.ds(pl.multiple_of(i * rows + h * half, half), half)]

        def block(i):
            return whole.at[pl.ds(pl.multiple_of(i * rows, rows), rows)]

        def across(i, k):
            return remote(block(i), block(i), sem.at[0, k], sem.at[1, k], "fsdp", at.sib)

        self.local = pltpu.make_async_copy(own, block(at.f), sem.at[0, 0])
        self.out = [[remote(own.at[pl.ds(h * half, half)], part(at.f, h), sem.at[2 + w, h], sem.at[4 + w, h], "fsdp", beside[w])
                     for h in range(2)] for w in range(2)]
        self.on = [remote(part(beside[w], w), part(beside[w], w), sem.at[2 + w, 2], sem.at[4 + w, 2], "fsdp", beside[1 - w])
                   for w in range(2)]
        far = 2 * (at.chips - 1 - at.chip) + at.core
        self.across = [remote(own, block(at.f), sem.at[0, 1], sem.at[1, 1], "fsdp", at.sib)]
        self.across += [across(beside[0], 2), across(beside[1], 3), across(far, 4)]

    def start(self):
        for w in range(2):
            self.out[w][w].start()
        for w in range(2):
            self.out[w][1 - w].start()
        self.across[0].start()
        self.local.start()

    def relay(self):
        for w in range(2):
            self.out[w][w].wait_recv()
            self.on[w].start()

    def forward(self):
        for w in range(2):
            self.out[w][1 - w].wait_recv()
            self.across[1 + w].start()
        for w in range(2):
            self.on[w].wait_recv()
        self.across[3].start()

    def wait(self):
        for w in range(2):
            self.out[w][0].wait_send()
            self.out[w][1].wait_send()
            self.on[w].wait_send()
        for c in self.across + [self.local]:
            c.wait()


def gather_rows(at, own, whole, sem):
    return (SquareGather if at.chips == 4 else Gather)(at, own, whole, sem)


class Gather:
    def __init__(self, at, own, whole, sem):
        rows = own.shape[0]

        def block(i):
            return whole.at[pl.ds(pl.multiple_of(i * rows, rows), rows)]

        self.local = pltpu.make_async_copy(own, block(at.f), sem.at[0, 0])
        self.across = [remote(own, block(at.f), sem.at[0, 1], sem.at[1, 0], "fsdp", at.sib)]
        self.far, self.on = [], []
        for k in range(1, at.chips):
            to = 2 * at.chip_at(k) + at.core
            self.far.append(remote(own, block(at.f), sem.at[2, k], sem.at[3, k], "fsdp", to))
            came = 2 * at.chip_at(at.chips - k) + at.core
            self.on.append(remote(block(came), block(came), sem.at[4, k], sem.at[5, k], "fsdp", at.sib))

    def start(self):
        for c in self.far + self.across + [self.local]:
            c.start()

    def relay(self):
        pass

    def forward(self):
        for far, on in zip(self.far, self.on):
            far.wait_recv()
            on.start()

    def wait(self):
        for c in self.far:
            c.wait_send()
        for c in self.across + self.on + [self.local]:
            c.wait()


class ScatterSum:
    def __init__(self, at, part, near, own, far, sem, made=False):
        self.at, self.part, self.near, self.own, self.far, self.sem, self.made = at, part, near, own, far, sem, made
        self.rows = own.shape[1]
        self.order = list(range(1, at.chips)) + [0]

    def block(self, i):
        return self.part.at[pl.ds(pl.multiple_of(i * self.rows, self.rows), self.rows)]

    def across(self, k):
        at = self.at
        other = self.part.at[k] if self.made else self.block(2 * at.chip_at(k) + 1 - at.core)
        return remote(other, self.near.at[k], self.sem.at[0, k], self.sem.at[1, k], "fsdp", at.sib)

    def load(self, k):
        return pltpu.make_async_copy(
            self.block(2 * self.at.chip_at(k) + self.at.core), self.own.at[k], self.sem.at[2, k])

    def send(self, k):
        at = self.at
        return remote(self.own.at[k], self.far.at[k - 1], self.sem.at[3, k], self.sem.at[4, k], "fsdp",
                      2 * at.chip_at(k) + at.core)

    def start(self):
        for k in self.order:
            self.across(k).start()
            if not self.made:
                self.load(k).start()

    def pass_on(self, k):
        self.across(k).wait()
        if not self.made:
            self.load(k).wait()

        def add(at):
            self.own[k, at] = (self.own[k, at].astype(F32) + self.near[k, at].astype(F32)).astype(BF)

        strips(self.rows, add)

        @pl.when(k > 0)
        def _():
            self.send(k).start()

    def forward(self):
        def step(i, carry):
            self.pass_on(lax.rem(i + 1, self.at.chips))
            return carry

        lax.fori_loop(0, self.at.chips, step, 0)

    def wait(self):
        for k in range(1, self.at.chips):
            self.send(k).wait()

    def total(self, at):
        out = self.own[0, at].astype(F32)
        for k in range(self.at.chips - 1):
            out += self.far[k, at].astype(F32)
        return out


class LineSum:
    def __init__(self, at, chunk, ring, arrive, send, recv, credit, out, out_sem, skip=0, feed=None):
        self.at, self.chunk, self.ring, self.arrive, self.skip = at, chunk, ring, arrive, skip
        self.send, self.recv, self.credit, self.out, self.out_sem = send, recv, credit, out, out_sem
        self.feed = feed
        self.slots = ring.shape[1]
        self.count = chunk.shape[0]
        self.kind = at.mid.astype(jnp.int32)

    def slot(self, j):
        return lax.rem(j, self.slots)

    def inward(self, j):
        return remote(self.chunk.at[j], self.ring.at[self.kind, self.slot(j)], self.send.at[0, j],
                      self.recv.at[self.kind, j], "replica", self.at.inner)

    def outward(self, j, src):
        return remote(src, self.out(j), self.send.at[1, j], self.recv.at[2, j], "replica", self.at.outer)

    def keep(self, j):
        return pltpu.make_async_copy(self.chunk.at[j], self.out(j), self.out_sem.at[j])

    def take_in(self, kind, j, plane):
        here = self.ring.at[kind, self.slot(j)]
        pltpu.make_async_copy(here, here, self.recv.at[kind, j]).wait()
        self.chunk[j] = (self.chunk[j].astype(F32) + self.ring[kind, self.slot(j)].astype(F32)).astype(BF)

        @pl.when(j + self.slots < self.count)
        def _():
            pl.semaphore_signal(self.credit, inc=1, device_id={"replica": plane}, device_id_type=MESH)

    def up(self, j):
        if self.feed:
            @pl.when(j + LEAD < self.count)
            def _():
                self.feed(j + LEAD)

        @pl.when(j >= self.skip)
        def _():
            pltpu.make_async_copy(self.chunk.at[j], self.chunk.at[j], self.arrive.at[j]).wait()

        @pl.when(self.at.has_outer)
        def _():
            self.take_in(0, j, self.at.outer)

        @pl.when(j >= self.slots)
        def _():
            pl.semaphore_wait(self.credit, 1)

        self.inward(j).start()

    def meet(self, j):
        self.inward(j).wait_send()
        self.take_in(1, j, self.at.inner)

        @pl.when(self.at.has_outer)
        def _():
            self.outward(j, self.chunk.at[j]).start()

        self.keep(j).start()

    def take(self, j):
        pltpu.make_async_copy(self.out(j), self.out(j), self.recv.at[2, j]).wait()

        @pl.when(self.at.has_outer)
        def _():
            self.outward(j, self.out(j)).start()

    def settle(self):
        def step(j, carry):
            @pl.when(self.at.mid)
            def _():
                self.keep(j).wait()

            @pl.when(jnp.logical_not(self.at.mid))
            def _():
                self.inward(j).wait_send()

            @pl.when(self.at.has_outer)
            def _():
                self.outward(j, self.chunk.at[j]).wait_send()

            return carry

        lax.fori_loop(0, self.count, step, 0)


class Lines:
    def __init__(self, *lines):
        self.lines = lines
        self.order = [(i, j) for i, line in enumerate(lines) for j in range(line.count)]
        self.at = 0

    def run(self, steps=None, body=None):
        begin = self.at
        last = len(self.order) + LAG_END
        stop = last if steps is None else min(self.at + steps, len(self.order))
        while self.at < stop:
            first, size = self.at, 1
            now = self.parts(first)
            while first + size < stop and self.kinds(first + size) == self.kinds(first):
                size += 1

            def step(m, carry, now=now, first=first):
                up, mid, rest = now
                if up:
                    self.lines[up[0]].up(up[1] + m)
                if mid:
                    @pl.when(self.lines[mid[0]].at.mid)
                    def _():
                        self.lines[mid[0]].meet(mid[1] + m)
                if rest:
                    @pl.when(jnp.logical_not(self.lines[rest[0]].at.mid))
                    def _():
                        self.lines[rest[0]].take(rest[1] + m)
                if body:
                    body(first - begin + m)
                return carry

            lax.fori_loop(0, size, step, 0)
            self.at += size

    def parts(self, t):
        return [self.order[i] if 0 <= i < len(self.order) else None for i in (t, t - LAG_MID, t - LAG_END)]

    def kinds(self, t):
        return [part and part[0] for part in self.parts(t)]

    def settle(self):
        for line in self.lines:
            line.settle()


def rms_of(values):
    return lax.rsqrt(jnp.mean(values * values, axis=-1, keepdims=True) + EPSILON)


def qkv_pieces(at, w, wc, qw):
    q_w, k_w = QUERY_HEADS * HEAD_WIDTH, KEY_VALUE_HEADS * HEAD_WIDTH
    shared = at.n // KEY_VALUE_HEADS
    depth = w.shape[0]

    def cols(start, width):
        return pl.ds(pl.multiple_of(start, HEAD_WIDTH), width)

    def rows(s):
        return pl.ds(pl.multiple_of(s * depth, depth), depth)

    return [
        (lambda t: w.at[:, cols(t * qw, qw)], lambda s: wc.at[rows(s), pl.ds(0, qw)]),
        (lambda t: w.at[:, cols(q_w + t // shared * HEAD_WIDTH, HEAD_WIDTH)],
         lambda s: wc.at[rows(s), pl.ds(qw, HEAD_WIDTH)]),
        (lambda t: w.at[:, cols(q_w + k_w + t // shared * HEAD_WIDTH, HEAD_WIDTH)],
         lambda s: wc.at[rows(s), pl.ds(qw + HEAD_WIDTH, HEAD_WIDTH)]),
    ]


def col_piece(w, wc, share, first=0):
    depth = w.shape[0]
    return (lambda t: w.at[:, pl.ds(pl.multiple_of(t * share, HEAD_WIDTH), share)],
            lambda s: wc.at[pl.ds(pl.multiple_of(s * depth, depth), depth), pl.ds(first, share)])


class Weights:
    def __init__(self, at, pieces, send, recv, z_send, z_recv):
        self.at, self.pieces, self.send, self.recv, self.z_send, self.z_recv = at, pieces, send, recv, z_send, z_recv
        self.mine = at.core == lax.rem(at.z, 2)
        self.parity = lax.rem(at.z + at.core, 2)
        self.partner = at.z + 1 - 2 * lax.rem(at.z, 2)

    def cols(self, i, t):
        return self.pieces[i][0](t)

    def rows(self, i, s):
        return self.pieces[i][1](s)

    def local(self, i):
        return pltpu.make_async_copy(self.cols(i, self.at.f), self.rows(i, self.at.f), self.recv.at[i, 0])

    def copy(self, i, j):
        to = self.at.near(j)
        return remote(self.cols(i, to), self.rows(i, self.at.f), self.send.at[i, j], self.recv.at[i, j], "fsdp", to)

    def beside(self, i, j):
        here = self.rows(i, self.at.near_from(j))
        return remote(here, here, self.z_send.at[i, j], self.z_recv.at[i, j], "replica", self.partner)

    def start(self, i):
        self.local(i).start()
        self.copy(i, 1).start()

        @pl.when(self.mine)
        def _():
            for j in range(2, self.at.n):
                self.copy(i, j).start()

    def hand_over(self, i):
        for m in range(1, self.at.chips):
            j = 2 * m + self.parity
            here = self.rows(i, self.at.near_from(j))
            pltpu.make_async_copy(here, here, self.recv.at[i, j]).wait()
            self.beside(i, j).start()

    def wait(self, i):
        self.local(i).wait()
        self.copy(i, 1).wait()

        @pl.when(self.mine)
        def _():
            for j in range(2, self.at.n):
                self.copy(i, j).wait_send()

        for m in range(1, self.at.chips):
            self.beside(i, 2 * m + self.parity).wait_send()
            self.beside(i, 2 * m + 1 - self.parity).wait_recv()


def front_kernel(n, n_z, x_ref, gain1_ref, gain2_ref, gainq_ref, gaink_ref, place_ref, table_ref, wout_ref,
                 wqkv_ref, g_ref, gate_ref, up_ref, down_ref,
                 h_ref, q_ref, kv_ref, ctx_ref, proj_ref, places_ref,
                 n1_ref, wc_ref, n2_ref, gall_ref, pair_c, down_c,
                 near, mine, far, stage, own, n1_block, wc,
                 s_x, r_x, s_p, r_p, s_g, s_n, s_w, s_h, s_r, s_a, s_b, s_c, r_c, s_z, r_z, s_xz, r_xz):
    at = Place(n, n_z)
    rows = x_ref.shape[0]
    heads = QUERY_HEADS // n
    qw = heads * HEAD_WIDTH
    halo = LMAX
    at.greet(True)
    weights = Weights(at, qkv_pieces(at, wqkv_ref, wc_ref, qw), s_x, r_x, s_xz, r_xz)
    for i in range(3):
        weights.start(i)

    def rows_of(g):
        return pl.ds(pl.multiple_of(g * rows, rows), rows)

    places = Exchange(at, [(lambda t: place_ref, lambda s: places_ref.at[rows_of(s)])], s_p, r_p)
    share = down_c.shape[1]
    mlp = Weights(
        at, [col_piece(gate_ref, pair_c, share), col_piece(up_ref, pair_c, share, share), col_piece(down_ref, down_c, share)],
        s_c, r_c, s_z, r_z)
    places.start()

    def norm1(strip):
        x = x_ref[strip].astype(F32)
        own[strip] = (x * rms_of(x) * gain1_ref[...]).astype(BF)

    strips(rows, norm1)
    n1 = gather_rows(at, own, n1_ref, s_g)
    n1.start()
    n1.relay()
    for i in range(3):
        weights.hand_over(i)
    n1.forward()
    n1.wait()
    places.wait()
    for i in range(3):
        weights.wait(i)
    mlp.start(0)
    mlp.start(1)
    to_vmem = pltpu.make_async_copy(wc_ref, wc, s_w.at[0])
    to_vmem.start()

    def block_of(g):
        return pltpu.make_async_copy(n1_ref.at[rows_of(g)], n1_block.at[lax.rem(g, 2)], s_n.at[lax.rem(g, 2)])

    block_of(0).start()
    to_vmem.wait()

    def project(g, carry):
        @pl.when(g + 1 < n)
        def _():
            block_of(g + 1).start()

        at_rows = rows_of(g)
        cosine, sine = rotation_of(places_ref[at_rows], table_ref)
        block_of(g).wait()
        proj = dot(n1_block[lax.rem(g, 2)], wc[...])
        proj_ref[at_rows] = proj[:, :qw + HEAD_WIDTH]
        for head in range(heads + 1):
            lanes = slice(head * HEAD_WIDTH, (head + 1) * HEAD_WIDTH)
            raw = proj[:, lanes]
            gain = gainq_ref if head < heads else gaink_ref
            turned = rotate_with(raw * rms_of(raw) * gain[...], cosine, sine).astype(BF)
            if head < heads:
                q_ref[at_rows, lanes] = turned
            else:
                kv_ref[g, halo:, :HEAD_WIDTH] = turned
        kv_ref[g, halo:, HEAD_WIDTH:] = proj[:, qw + HEAD_WIDTH:].astype(BF)
        return carry

    lax.fori_loop(0, n, project, 0)
    not_first, not_last = at.z > 0, at.z < n_z - 1

    def halo_copy():
        return remote(kv_ref.at[:, pl.ds(rows, halo)], kv_ref.at[:, pl.ds(0, halo)], s_h.at[0], s_h.at[1], "replica",
                      jnp.minimum(at.z + 1, n_z - 1))

    @pl.when(not_last)
    def _():
        halo_copy().start()

    @pl.when(not_first)
    def _():
        here = kv_ref.at[:, pl.ds(0, halo)]
        pltpu.make_async_copy(here, here, s_h.at[1]).wait()

    @pl.when(jnp.logical_not(not_first))
    def _():
        kv_ref[:, :halo] = jnp.zeros((n, halo, 2 * HEAD_WIDTH), BF)

    sum_o = ScatterSum(at, stage, near, mine, far, s_r, made=True)

    def attend(g):
        at_rows = rows_of(g)
        mask = window_mask(places_ref[at_rows], rows, halo)
        keys, values = kv_ref[g, :, :HEAD_WIDTH], kv_ref[g, :, HEAD_WIDTH:]
        for head in range(heads):
            lanes = slice(head * HEAD_WIDTH, (head + 1) * HEAD_WIDTH)
            probs = softmax_of(q_ref[at_rows, lanes], keys, mask).astype(BF)
            ctx_ref[at_rows, lanes] = dot(probs, values).astype(BF)
        return dot(ctx_ref[at_rows], wout_ref[...]).astype(BF)

    def attend_both(i, carry):
        k = lax.rem(i + 1, at.chips)
        q = at.chip_at(k)
        stage[k] = attend(2 * q + 1 - at.core)
        sum_o.across(k).start()
        mine[k] = attend(2 * q + at.core)

        @pl.when(i > 0)
        def _():
            sum_o.pass_on(jnp.maximum(i, 1))

        return carry

    lax.fori_loop(0, at.chips, attend_both, 0)
    sum_o.pass_on(0)
    mlp.start(2)
    mlp.hand_over(0)
    sum_o.wait()

    def norm2(strip):
        h = x_ref[strip].astype(F32) + sum_o.total(strip)
        h_ref[strip] = h
        own[strip] = (h * rms_of(h) * gain2_ref[...]).astype(BF)

    strips(rows, norm2)
    n2 = gather_rows(at, own, n2_ref, s_a)
    g_all = gather_rows(at, g_ref, gall_ref, s_b)
    n2.start()
    mlp.hand_over(1)
    n2.relay()
    g_all.start()
    n2.forward()
    g_all.relay()
    mlp.hand_over(2)
    g_all.forward()
    n2.wait()
    g_all.wait()

    @pl.when(not_last)
    def _():
        halo_copy().wait_send()

    for i in range(3):
        mlp.wait(i)


class Feed:
    def __init__(self, at, grads, chunk, send, recv):
        self.at, self.grads, self.chunk, self.send, self.recv = at, grads, chunk, send, recv
        self.depth = chunk.shape[1]

    def rows(self, grad, t):
        return grad.at[pl.ds(pl.multiple_of(t * self.depth, self.depth), self.depth)]

    def copy(self, grad, c, j):
        to = self.at.near(j)
        return remote(self.rows(grad, to), self.chunk.at[c], self.send.at[c], self.recv.at[c], "fsdp", to)

    def start(self, c):
        n = self.at.n
        j = lax.rem(c, n)
        for i, grad in enumerate(self.grads):
            @pl.when((c // n == i) & (j == 0))
            def _(grad=grad):
                pltpu.make_async_copy(self.rows(grad, self.at.f), self.chunk.at[c], self.recv.at[c]).start()

            @pl.when((c // n == i) & (j > 0))
            def _(grad=grad):
                self.copy(grad, c, j).start()

    def settle(self):
        def step(c, carry):
            @pl.when(lax.rem(c, self.at.n) > 0)
            def _():
                self.copy(self.grads[0], c, lax.rem(c, self.at.n)).wait_send()

            return carry

        lax.fori_loop(0, len(self.grads) * self.at.n, step, 0)


def start_all(copies):
    for c in copies:
        c.start()


def rotate_with(values, cosine, sine):
    return values * cosine + pltpu.roll(values, HEAD_WIDTH // 2, 1) * sine


def rotation_table():
    places = HEAD_WIDTH * -(-LMAX // HEAD_WIDTH)
    inverse = ROPE_BASE ** (-(2.0 * np.arange(HEAD_WIDTH // 2)) / HEAD_WIDTH)
    angles = np.arange(places)[:, None] * inverse[None, :]
    cosine, sine = np.cos(angles), np.sin(angles)
    rest = np.concatenate([cosine, cosine, -sine, sine], axis=1).astype(np.float32)
    terms = []
    for _ in range(3):
        terms.append(rest.astype(jnp.bfloat16))
        rest = rest - terms[-1].astype(np.float32)
    return jnp.asarray(np.stack(terms))


def rotation_of(places, table):
    lane = lax.broadcasted_iota(jnp.int32, (places.shape[0], table.shape[1]), 1).astype(F32)
    pick = (lane == places.astype(F32)[:, :1]).astype(F32).astype(BF)
    both = dot(pick, table[0]) + dot(pick, table[1]) + dot(pick, table[2])
    return both[:, :HEAD_WIDTH], both[:, HEAD_WIDTH:]


def window_mask(places, rows, halo):
    i_at = lax.broadcasted_iota(jnp.int32, (rows, halo + rows), 0) + halo
    j_at = lax.broadcasted_iota(jnp.int32, (rows, halo + rows), 1)
    back = (i_at - j_at).astype(F32)
    return (back >= 0) & (back <= places.astype(F32)[:, :1])


def softmax_of(queries, keys, mask):
    scores = jnp.where(mask, dot_cols(queries, keys) * HEAD_WIDTH ** (-0.5), NEG_FILL)
    terms = jnp.exp(scores - jnp.max(scores, axis=1, keepdims=True))
    return terms / jnp.sum(terms, axis=1, keepdims=True)


def back_kernel(n, n_z, part_ref, party_ref, x_ref, h_ref, g_ref, gain1_ref, gain2_ref, gainq_ref, gaink_ref,
                down_ref, n2_ref, dpair_ref, wout_ref, wqkv_ref, q_ref, kv_ref, ctx_ref, proj_ref, table_ref, place_ref,
                n1_ref,
                dx_ref, y_ref, gains_ref, gmlp_ref, gqkv_ref, dhall_ref, gate_ref, up_ref,
                near, mine, far, stage, dh, plane_gain, all_gain,
                chunk, ring, chunk2, ring2, dh_block, gout, d_kv, d_proj, halo_out, halo_in, n1_cols, qkv_send, d_in, tile_out,
                s_r, s_a, s_p, r_p, s_q, r_q, s_c, r_c, s_z, r_z, s_o, s_c2, r_c2, s_z2, r_z2, s_o2, credit, done, s_d, s_n, s_h, s_e, s_t):
    at = Place(n, n_z)
    share, share_out = chunk.shape[2], chunk2.shape[2]
    rows, width = x_ref.shape
    depth = chunk.shape[1]
    outs = -(-width // share_out)
    heads = QUERY_HEADS // n
    qw = heads * HEAD_WIDTH
    halo = LMAX
    scale = HEAD_WIDTH ** (-0.5)
    own = dh_block
    own_gain = all_gain.at[at.z]
    at.greet(True)

    def mlp_place(j):
        s = at.near_from(lax.rem(j, n))
        return gmlp_ref.at[j // n, :, pl.ds(pl.multiple_of(s * share, HEAD_WIDTH), share)]

    def attn_place(j):
        col = jnp.where(j < outs, j, outs + at.near_from(jnp.maximum(j - outs, 0)))
        return gqkv_ref.at[:, pl.ds(pl.multiple_of(col * share_out, HEAD_WIDTH), share_out)]

    feed = Feed(at, (down_ref, gate_ref, up_ref), chunk, s_c, r_c)
    lines = Lines(
        LineSum(at, chunk, ring, r_c, s_z, r_z, credit.at[0], mlp_place, s_o, 0, feed.start),
        LineSum(at, chunk2, ring2, r_c2, s_z2, r_z2, credit.at[1], attn_place, s_o2, outs))
    sum_n2 = ScatterSum(at, part_ref, near, mine, far, s_r.at[0])
    for c in range(LEAD):
        feed.start(jnp.int32(c))
    sum_n2.start()
    load = pltpu.make_async_copy(dpair_ref.at[:, pl.ds(0, share)], d_in, s_e.at[0])
    load.start()
    lines.run(1)
    sum_n2.forward()

    def fetch_cols(ref, j):
        return pltpu.make_async_copy(
            ref.at[:, pl.ds(pl.multiple_of(at.near(j) * depth, depth), depth)], n1_cols.at[lax.rem(j, 2)],
            s_n.at[lax.rem(j, 2)])

    def tiles(ref, per):
        def put(j):
            return pltpu.make_async_copy(
                tile_out.at[lax.rem(j, 2)], ref.at[pl.ds(pl.multiple_of(at.near(j) * depth, depth), depth)],
                s_t.at[lax.rem(j, 2)])

        def tile(j):
            @pl.when(j + 1 < n)
            def _():
                fetch_cols(n2_ref, j + 1).start()

            fetch_cols(n2_ref, j).wait()

            @pl.when(j > 1)
            def _():
                put(j - 2).wait()

            tile_out[lax.rem(j, 2)] = dot_rows(n1_cols[lax.rem(j, 2)], d_in[...]).astype(BF)
            put(j).start()

        def body(step):
            for r in range(per):
                j = step * per + r

                @pl.when(j < n)
                def _(j=j):
                    tile(j)

        def end():
            put(n - 2).wait()
            put(n - 1).wait()

        fetch_cols(n2_ref, 0).start()
        return body, end

    per_tile = -(-n // 3)
    load.wait()
    body, end = tiles(gate_ref, per_tile)
    lines.run(3, body)
    end()
    load = pltpu.make_async_copy(dpair_ref.at[:, pl.ds(share, share)], d_in, s_e.at[0])
    load.start()
    lines.run(n - 8)
    sum_n2.wait()
    own_gain[...] = jnp.zeros_like(own_gain)

    def back_mlp(strip):
        d_n2 = sum_n2.total(strip)
        h = h_ref[strip]
        r2 = rms_of(h)
        u2 = h * r2
        own_gain[1:2] += jnp.sum(d_n2 * u2, axis=0, keepdims=True)
        d_h = g_ref[strip].astype(F32) + norm_back(d_n2 * gain2_ref[...], u2, r2)
        dh[strip] = d_h
        own[strip] = d_h.astype(BF)

    strips(rows, back_mlp)
    gather = gather_rows(at, own, dhall_ref, s_a)
    gather.start()
    load.wait()
    body, end = tiles(up_ref, per_tile)
    lines.run(3, body)
    end()
    lines.run(n // 2 - 4)
    gather.relay()
    lines.run(2)
    gather.forward()
    lines.run(1)
    gather.wait()
    sum_y = ScatterSum(at, party_ref, near, mine, far, s_r.at[2])
    sum_y.start()
    lines.run(1)
    sum_y.forward()
    gout[...] = jnp.zeros_like(gout)

    def rows_of(g):
        return pl.ds(pl.multiple_of(g * rows, rows), rows)

    def block_of(g):
        return pltpu.make_async_copy(dhall_ref.at[rows_of(g)], dh_block, s_d.at[0])

    def attention(g):
        at_rows = rows_of(g)
        block_of(g).start()
        mask = window_mask(place_ref[at_rows], rows, halo)
        keys, values = kv_ref[g, :, :HEAD_WIDTH], kv_ref[g, :, HEAD_WIDTH:]
        cosine, sine = rotation_of(place_ref[at_rows], table_ref)
        block_of(g).wait()
        d_ctx = dot_cols(dh_block[...], wout_ref[...]).astype(BF)
        gout[:, :width] += dot_rows(ctx_ref[at_rows], dh_block[...])
        d_k = jnp.zeros((halo + rows, HEAD_WIDTH), F32)
        d_v = jnp.zeros((halo + rows, HEAD_WIDTH), F32)
        for head in range(heads):
            lanes = slice(head * HEAD_WIDTH, (head + 1) * HEAD_WIDTH)
            queries, d_c = q_ref[at_rows, lanes], d_ctx[:, lanes]
            probs = softmax_of(queries, keys, mask)
            d_v += dot_rows(probs.astype(BF), d_c)
            d_p = dot_cols(d_c, values)
            d_s = (probs * (d_p - jnp.sum(probs * d_p, axis=1, keepdims=True))).astype(BF)
            d_k += dot_rows(d_s, queries) * scale
            dq_g = rotate_with(dot(d_s, keys) * scale, cosine, -sine)
            raw = proj_ref[at_rows, lanes]
            rms = rms_of(raw)
            hat = raw * rms
            own_gain[2:3, :HEAD_WIDTH] += jnp.sum(dq_g * hat, axis=0, keepdims=True)
            d_proj[at_rows, lanes] = norm_back(dq_g * gainq_ref[...], hat, rms).astype(BF)
        halo_out[g, :, :HEAD_WIDTH] = d_k[:halo].astype(BF)
        halo_out[g, :, HEAD_WIDTH:] = d_v[:halo].astype(BF)
        d_kv[g, :, :HEAD_WIDTH] = d_k[halo:]
        d_kv[g, :, HEAD_WIDTH:] = d_v[halo:]

    lines.run(n, attention)

    not_first, not_last = at.z > 0, at.z < n_z - 1

    def halo_copy():
        return remote(halo_out, halo_in, s_h.at[0], s_h.at[1], "replica", jnp.maximum(at.z - 1, 0))

    @pl.when(not_first)
    def _():
        halo_copy().start()

    for i in range(outs):
        chunk2[i] = gout[:, i * share_out:(i + 1) * share_out].astype(BF)
    lines.run(1)
    sum_y.wait()

    def finish(strip):
        y_ref[strip] = (h_ref[strip] + sum_y.total(strip)).astype(BF)

    strips(rows, finish)
    for k in range(1, n):
        pl.semaphore_signal(done, inc=1, device_id={"fsdp": at.to(k)}, device_id_type=MESH)

    @pl.when(not_last)
    def _():
        pltpu.make_async_copy(halo_in, halo_in, s_h.at[1]).wait()

    @pl.when(jnp.logical_not(not_last))
    def _():
        halo_in[...] = jnp.zeros_like(halo_in)

    def keys_back(g):
        at_rows = rows_of(g)
        d_kv[g, rows - halo:] += halo_in[g].astype(F32)
        cosine, sine = rotation_of(place_ref[at_rows], table_ref)
        dk_g = rotate_with(d_kv[g, :, :HEAD_WIDTH], cosine, -sine)
        raw = proj_ref[at_rows, qw:qw + HEAD_WIDTH]
        rms = rms_of(raw)
        hat = raw * rms
        own_gain[2:3, HEAD_WIDTH:2 * HEAD_WIDTH] += jnp.sum(dk_g * hat, axis=0, keepdims=True)
        d_proj[at_rows, qw:qw + HEAD_WIDTH] = norm_back(dk_g * gaink_ref[...], hat, rms).astype(BF)
        d_proj[at_rows, qw + HEAD_WIDTH:] = d_kv[g, :, HEAD_WIDTH:].astype(BF)

    per_step = n // 2

    def keys_back_some(i):
        for m in range(per_step):
            keys_back(i * per_step + m)

    lines.run(2, keys_back_some)

    def cols_of(j):
        return fetch_cols(n1_ref, j)

    own_qkv = pltpu.make_async_copy(qkv_send.at[0], chunk2.at[outs], r_c2.at[outs])

    def qkv_copy(j):
        return remote(qkv_send.at[j], chunk2.at[outs + j], s_c2.at[j], r_c2.at[outs + j], "fsdp", at.near(j))

    cols_of(0).start()

    def qkv_grad(j):
        @pl.when(j + 1 < n)
        def _():
            cols_of(j + 1).start()

        cols_of(j).wait()
        qkv_send[j] = dot_rows(n1_cols[lax.rem(j, 2)], d_proj[...]).astype(BF)

        @pl.when(j == 0)
        def _():
            own_qkv.start()

        @pl.when(j > 0)
        def _():
            qkv_copy(j).start()

    per_out = n // 4

    def qkv_grads(i):
        for m in range(per_out):
            qkv_grad(i * per_out + m)

    sum_n1 = ScatterSum(at, stage, near, mine, far, s_r.at[1], made=True)

    def n1_part(k):
        q = at.chip_at(k)
        stage[k] = dot_cols(d_proj[rows_of(2 * q + 1 - at.core)], wqkv_ref[...]).astype(BF)
        mine[k] = dot_cols(d_proj[rows_of(2 * q + at.core)], wqkv_ref[...]).astype(BF)

    def both(i):
        qkv_grads(i)
        for r in range(at.chips // 4):
            n1_part(i * (at.chips // 4) + r)

    lines.run(4, both)
    pl.semaphore_wait(done, n - 1)
    sum_n1.start()
    lines.run(1)
    sum_n1.forward()
    lines.run(outs + n - 4 - 1 - 2 - -2)
    sum_n1.wait()

    def back_attn(strip):
        d_n1 = sum_n1.total(strip)
        x = x_ref[strip].astype(F32)
        r1 = rms_of(x)
        u1 = x * r1
        own_gain[0:1] += jnp.sum(d_n1 * u1, axis=0, keepdims=True)
        dx_ref[strip] = (dh[strip] + norm_back(d_n1 * gain1_ref[...], u1, r1)).astype(BF)

    strips(rows, back_attn)
    gains = Exchange(at, [(lambda t: own_gain, lambda s: plane_gain.at[s])], s_p, r_p)
    gains.start()
    lines.run(1)
    gains.wait()
    own_gain[...] = jnp.sum(plane_gain[...], axis=0)
    others = [
        remote(own_gain, all_gain.at[at.z], s_q.at[k], r_q.at[k], "replica", at.plane(k)) for k in range(1, n_z)]
    start_all(others)
    lines.run()
    for c in others:
        c.wait()
    gains_ref[...] = jnp.sum(all_gain[...], axis=0)
    feed.settle()
    for j in range(1, n):
        qkv_copy(j).wait_send()

    @pl.when(not_first)
    def _():
        halo_copy().wait_send()

    lines.settle()


def front(n, n_z, x, gain1, gain2, gain_q, gain_k, place, table, w_out, w_qkv, g, gate, up, down):
    rows, width = x.shape
    chips, share, total = n // 2, gate.shape[1] // n, n * rows
    qw = QUERY_HEADS * HEAD_WIDTH // n
    wide = qw + 2 * HEAD_WIDTH
    block = functools.partial(pltpu.VMEM, dtype=BF)
    shape = jax.ShapeDtypeStruct
    return pl.pallas_call(
        functools.partial(front_kernel, n, n_z),
        out_shape=(
            shape((rows, width), F32), shape((total, qw), BF), shape((n, LMAX + rows, 2 * HEAD_WIDTH), BF),
            shape((total, qw), BF), shape((total, qw + HEAD_WIDTH), F32), shape((total, HEAD_WIDTH), BF),
            shape((total, width), BF), shape((width, wide), BF), shape((total, width), BF), shape((total, width), BF),
        ) + (shape((width, 2 * share), BF), shape((width, share), BF)),
        in_specs=[VMEM] * 8 + [ANY] * 5,
        out_specs=(VMEM,) * 6 + (ANY,) * 6,
        scratch_shapes=[
            block((chips, rows, width)), block((chips, rows, width)), block((chips - 1, rows, width)),
            block((chips, rows, width)), block((rows, width)), block((2, rows, width)), block((width, wide)),
            DMA((3, n)), DMA((3, n)), DMA((1, n)), DMA((1, n)), DMA((6, n)), DMA((2,)), DMA((1,)), DMA((2,)),
            DMA((5, n)), DMA((6, n)), DMA((6, n)), DMA((3, n)), DMA((3, n)), DMA((3, n)), DMA((3, n)),
            DMA((3, n)), DMA((3, n))],
        compiler_params=pltpu.CompilerParams(collective_id=0, has_side_effects=True, vmem_limit_bytes=60 << 20),
        name="front",
    )(x, gain1, gain2, gain_q, gain_k, place, table, w_out, w_qkv, g, gate, up, down)


def back(n, n_z, part, part_y, x, h, g, gain1, gain2, gain_q, gain_k, down, n2, d_pair, w_out, w_qkv, q, kv, ctx, proj,
         table, places, n1):
    rows, width = x.shape
    chips, share, wide, depth = n // 2, down.shape[1], w_qkv.shape[1], width // n
    outs = -(-width // wide)
    block = functools.partial(pltpu.VMEM, dtype=BF)
    gains = (8, width)
    count2 = outs + n
    slots = 2 + 16 // n
    return pl.pallas_call(
        functools.partial(back_kernel, n, n_z),
        out_shape=(
            jax.ShapeDtypeStruct((rows, width), BF),
            jax.ShapeDtypeStruct((rows, width), BF),
            jax.ShapeDtypeStruct(gains, F32),
            jax.ShapeDtypeStruct((3, depth, n * share), BF),
            jax.ShapeDtypeStruct((depth, count2 * wide), BF),
            jax.ShapeDtypeStruct((n * rows, width), BF),
            jax.ShapeDtypeStruct((width, share), BF),
            jax.ShapeDtypeStruct((width, share), BF),
        ),
        in_specs=[ANY, ANY] + [VMEM] * 7 + [ANY] * 3 + [VMEM] * 8 + [ANY],
        out_specs=(VMEM, VMEM, VMEM, ANY, ANY, ANY, ANY, ANY),
        scratch_shapes=[
            block((chips, rows, width)), block((chips, rows, width)), block((chips - 1, rows, width)),
            block((chips, rows, width)), pltpu.VMEM((rows, width), F32),
            pltpu.VMEM((n,) + gains, F32), pltpu.VMEM((n_z,) + gains, F32),
            block((3 * n, depth, share)), block((2, slots, depth, share)),
            block((count2, depth, wide)), block((2, slots, depth, wide)),
            block((rows, width)), pltpu.VMEM((depth, outs * wide), F32),
            pltpu.VMEM((n, rows, 2 * HEAD_WIDTH), F32), block((n * rows, wide)),
            block((n, LMAX, 2 * HEAD_WIDTH)), block((n, LMAX, 2 * HEAD_WIDTH)),
            block((2, n * rows, depth)), block((n, depth, wide)), block((n * rows, share)), block((2, depth, share)),
            DMA((3, 5, n)), DMA((6, n)), DMA((1, n)), DMA((1, n)), DMA((n_z,)), DMA((n_z,)),
            DMA((3 * n,)), DMA((3 * n,)), DMA((2, 3 * n)), DMA((3, 3 * n)), DMA((3 * n,)),
            DMA((n,)), DMA((count2,)), DMA((2, count2)), DMA((3, count2)), DMA((count2,)),
            pltpu.SemaphoreType.REGULAR((2,)), pltpu.SemaphoreType.REGULAR, DMA((1,)), DMA((2,)), DMA((2,)), DMA((1,)), DMA((2,))],
        compiler_params=pltpu.CompilerParams(collective_id=2, has_side_effects=True, vmem_limit_bytes=511 << 17),
        name="back",
    )(part, part_y, x, h, g, gain1, gain2, gain_q, gain_k, down, n2, d_pair, w_out, w_qkv, q, kv, ctx, proj, table, places, n1)


def row_positions(flat_lens, ranks, first_row, count):
    earlier = (ranks[:, None] < ranks[None, :]).astype(jnp.int32)
    starts = jnp.sum(flat_lens[:, None] * earlier, axis=0)
    rows = first_row + jnp.arange(count, dtype=jnp.int32)
    begun = jnp.where(starts[None, :] <= rows[:, None], starts[None, :], 0)
    return rows - jnp.max(begun, axis=1)


def per_device(
    n_replica, tokens, cotangent, w_qkv, w_out, w_gate, w_up, w_down_t,
    gain_attn, gain_mlp, gain_query, gain_key, dealt_lens, seq_order,
):
    rows, width = tokens.shape
    n_fsdp = width // w_qkv.shape[0]
    q_w = QUERY_HEADS * HEAD_WIDTH
    k_w = KEY_VALUE_HEADS * HEAD_WIDTH
    replica = lax.axis_index("replica")
    shared = n_fsdp // KEY_VALUE_HEADS
    heads = QUERY_HEADS // n_fsdp
    qw = heads * HEAD_WIDTH

    pos = row_positions(dealt_lens[0].reshape(-1), seq_order[0], replica * rows, rows)
    depth = w_qkv.shape[0]
    place = jnp.broadcast_to(pos.astype(BF)[:, None], (rows, HEAD_WIDTH))
    table = rotation_table()
    gains = (gain_attn[None], gain_mlp[None], gain_query[None], gain_key[None])
    h, q_low, kv_window, ctx_low, proj, places, n1, w_qkv_c, n2, g_all, pair_c, down_c = front(
        n_fsdp, n_replica, tokens, *gains, place, table, w_out, w_qkv, cotangent, w_gate, w_up, w_down_t)

    both = dot(n2, pair_c)
    share = down_c.shape[1]
    gate, up = both[:, :share], both[:, share:]
    sg = jax.nn.sigmoid(gate)
    silu = gate * sg
    act = (silu * up).astype(BF)
    part_y = dot_cols(act, down_c).astype(BF)

    d_act = dot(g_all, down_c)
    d_pair = jnp.concatenate([d_act * up * sg * (1.0 + gate * (1.0 - sg)), d_act * silu], axis=1).astype(BF)

    input_grad, output, gain_sums, g_mlp, g_attn, _, _, _ = back(
        n_fsdp, n_replica, dot_cols(d_pair, pair_c).astype(BF), part_y, tokens, h, cotangent, *gains,
        dot_rows(g_all, act).astype(BF), n2, d_pair,
        w_out, w_qkv_c, q_low, kv_window, ctx_low, proj, table, places, n1)
    wide = qw + 2 * HEAD_WIDTH
    g_out = g_attn[:, :width]
    by_device = [g_attn[:, at:at + wide] for at in range(g_attn.shape[1] - n_fsdp * wide, g_attn.shape[1], wide)]

    def of_key_heads(first):
        parts = [part[:, first:first + HEAD_WIDTH].astype(F32) for part in by_device]
        return [sum(parts[i + 1:i + shared], parts[i]) for i in range(0, n_fsdp, shared)]

    g_qkv = jnp.concatenate(
        [part[:, :qw].astype(F32) for part in by_device] + of_key_heads(qw) + of_key_heads(qw + HEAD_WIDTH), axis=1)
    return (
        output, input_grad, g_qkv, g_out.astype(F32), g_mlp[1].astype(F32), g_mlp[2].astype(F32), g_mlp[0].astype(F32),
        gain_sums[0], gain_sums[1], gain_sums[2, :HEAD_WIDTH], gain_sums[2, HEAD_WIDTH:2 * HEAD_WIDTH])


def solution(mesh):
    n_replica = mesh.shape["replica"]

    def program(*args):
        return per_device(n_replica, *args)

    rows = P(("fsdp", "replica"), None)
    weight = P("fsdp", None)
    return jax.shard_map(
        program,
        mesh=mesh,
        in_specs=(rows, rows) + (weight,) * 5 + (P(),) * 4 + (P("fsdp", None, None), P("fsdp", None)),
        out_specs=(rows, rows) + (weight,) * 5 + (P(),) * 4,
        check_vma=False,
    )
```

```python
import functools

import jax
import jax.numpy as jnp
import numpy as np
from jax import lax
from jax.experimental import pallas as pl
from jax.experimental.pallas import tpu as pltpu
from jax.sharding import PartitionSpec as P

QUERY_HEADS = 16
KEY_VALUE_HEADS = 8
HEAD_WIDTH = 128
LMAX = 96

EPSILON = 1e-06
ROPE_BASE = 1000000.0
NEG_FILL = -1e30
BF = jnp.bfloat16
F32 = jnp.float32


MESH = pl.DeviceIdType.MESH
ANY = pl.BlockSpec(memory_space=pl.ANY)
VMEM = pl.BlockSpec(memory_space=pltpu.VMEM)
DMA = pltpu.SemaphoreType.DMA
STRIP = 16
LAG_MID = 2
LAG_END = 6
LEAD = 5


def dot(left, right):
    return jnp.dot(left, right, preferred_element_type=F32)


def dot_rows(left, right):
    return lax.dot_general(left, right, (((0,), (0,)), ((), ())), preferred_element_type=F32)


def dot_cols(left, right):
    return lax.dot_general(left, right, (((1,), (1,)), ((), ())), preferred_element_type=F32)


def norm_back(d_normed, normed, rms):
    return rms * (d_normed - normed * jnp.mean(d_normed * normed, axis=-1, keepdims=True))


class Place:
    def __init__(self, n, n_z):
        self.n, self.chips, self.n_z = n, n // 2, n_z
        self.f = lax.axis_index("fsdp")
        self.chip, self.core = self.f // 2, lax.rem(self.f, 2)
        self.sib = self.f + 1 - 2 * self.core
        self.z = lax.axis_index("replica")
        low = (self.z < n_z // 2).astype(jnp.int32)
        self.inner = self.z - 1 + 2 * low
        self.outer = self.z + 1 - 2 * low
        self.mid = (self.z == n_z // 2 - 1) | (self.z == n_z // 2)
        self.has_outer = (self.z > 0) & (self.z < n_z - 1)

    def to(self, k):
        return lax.rem(self.f + k, self.n)

    def near(self, j):
        return 2 * lax.rem(self.chip + j // 2, self.chips) + lax.rem(self.core + lax.rem(j, 2), 2)

    def near_from(self, j):
        return 2 * lax.rem(self.chip + self.chips - j // 2, self.chips) + lax.rem(self.core + lax.rem(j, 2), 2)

    def plane(self, k):
        return lax.rem(self.z + k, self.n_z)

    def chip_at(self, k):
        return lax.rem(self.chip + k, self.chips)

    def greet(self, line):
        barrier = pltpu.get_barrier_semaphore()
        for k in range(1, self.n):
            pl.semaphore_signal(barrier, inc=1, device_id={"fsdp": self.to(k)}, device_id_type=MESH)
        if line:
            for k in range(1, self.n_z):
                pl.semaphore_signal(barrier, inc=1, device_id={"replica": self.plane(k)}, device_id_type=MESH)

        pl.semaphore_wait(barrier, self.n - 1 + (self.n_z - 1 if line else 0))


def remote(src, dst, send, recv, axis, index):
    return pltpu.make_async_remote_copy(
        src_ref=src, dst_ref=dst, send_sem=send, recv_sem=recv, device_id={axis: index}, device_id_type=MESH)


def strips(rows, body):
    def step(i, carry):
        body(pl.ds(pl.multiple_of(i * STRIP, STRIP), STRIP))
        return carry

    lax.fori_loop(0, rows // STRIP, step, 0)


class Exchange:
    def __init__(self, at, pieces, send, recv):
        self.copies, self.local = [], []
        for i, (src, dst) in enumerate(pieces):
            self.local.append(pltpu.make_async_copy(src(at.f), dst(at.f), recv.at[i, 0]))
            for k in range(1, at.n):
                self.copies.append(remote(src(at.to(k)), dst(at.f), send.at[i, k], recv.at[i, k], "fsdp", at.to(k)))

    def start(self):
        for c in self.copies + self.local:
            c.start()

    def wait(self):
        for c in self.copies + self.local:
            c.wait()


class SquareGather:
    def __init__(self, at, own, whole, sem):
        rows = own.shape[0]
        half = rows // 2
        beside = (2 * (at.chip + 1 - 2 * lax.rem(at.chip, 2)) + at.core, 2 * at.chip_at(2) + at.core)

        def part(i, h):
            return whole.at[pl.ds(pl.multiple_of(i * rows + h * half, half), half)]

        def block(i):
            return whole.at[pl.ds(pl.multiple_of(i * rows, rows), rows)]

        def across(i, k):
            return remote(block(i), block(i), sem.at[0, k], sem.at[1, k], "fsdp", at.sib)

        self.local = pltpu.make_async_copy(own, block(at.f), sem.at[0, 0])
        self.out = [[remote(own.at[pl.ds(h * half, half)], part(at.f, h), sem.at[2 + w, h], sem.at[4 + w, h], "fsdp", beside[w])
                     for h in range(2)] for w in range(2)]
        self.on = [remote(part(beside[w], w), part(beside[w], w), sem.at[2 + w, 2], sem.at[4 + w, 2], "fsdp", beside[1 - w])
                   for w in range(2)]
        far = 2 * (at.chips - 1 - at.chip) + at.core
        self.across = [remote(own, block(at.f), sem.at[0, 1], sem.at[1, 1], "fsdp", at.sib)]
        self.across += [across(beside[0], 2), across(beside[1], 3), across(far, 4)]

    def start(self):
        for w in range(2):
            self.out[w][w].start()
        for w in range(2):
            self.out[w][1 - w].start()
        self.across[0].start()
        self.local.start()

    def relay(self):
        for w in range(2):
            self.out[w][w].wait_recv()
            self.on[w].start()

    def forward(self):
        for w in range(2):
            self.out[w][1 - w].wait_recv()
            self.across[1 + w].start()
        for w in range(2):
            self.on[w].wait_recv()
        self.across[3].start()

    def wait(self):
        for w in range(2):
            self.out[w][0].wait_send()
            self.out[w][1].wait_send()
            self.on[w].wait_send()
        for c in self.across + [self.local]:
            c.wait()


def gather_rows(at, own, whole, sem):
    return (SquareGather if at.chips == 4 else Gather)(at, own, whole, sem)


class Gather:
    def __init__(self, at, own, whole, sem):
        rows = own.shape[0]

        def block(i):
            return whole.at[pl.ds(pl.multiple_of(i * rows, rows), rows)]

        self.local = pltpu.make_async_copy(own, block(at.f), sem.at[0, 0])
        self.across = [remote(own, block(at.f), sem.at[0, 1], sem.at[1, 0], "fsdp", at.sib)]
        self.far, self.on = [], []
        for k in range(1, at.chips):
            to = 2 * at.chip_at(k) + at.core
            self.far.append(remote(own, block(at.f), sem.at[2, k], sem.at[3, k], "fsdp", to))
            came = 2 * at.chip_at(at.chips - k) + at.core
            self.on.append(remote(block(came), block(came), sem.at[4, k], sem.at[5, k], "fsdp", at.sib))

    def start(self):
        for c in self.far + self.across + [self.local]:
            c.start()

    def relay(self):
        pass

    def forward(self):
        for far, on in zip(self.far, self.on):
            far.wait_recv()
            on.start()

    def wait(self):
        for c in self.far:
            c.wait_send()
        for c in self.across + self.on + [self.local]:
            c.wait()


class ScatterSum:
    def __init__(self, at, part, near, own, far, sem, made=False):
        self.at, self.part, self.near, self.own, self.far, self.sem, self.made = at, part, near, own, far, sem, made
        self.rows = own.shape[1]
        self.order = list(range(1, at.chips)) + [0]

    def block(self, i):
        return self.part.at[pl.ds(pl.multiple_of(i * self.rows, self.rows), self.rows)]

    def across(self, k):
        at = self.at
        other = self.part.at[k] if self.made else self.block(2 * at.chip_at(k) + 1 - at.core)
        return remote(other, self.near.at[k], self.sem.at[0, k], self.sem.at[1, k], "fsdp", at.sib)

    def load(self, k):
        return pltpu.make_async_copy(
            self.block(2 * self.at.chip_at(k) + self.at.core), self.own.at[k], self.sem.at[2, k])

    def send(self, k):
        at = self.at
        return remote(self.own.at[k], self.far.at[k - 1], self.sem.at[3, k], self.sem.at[4, k], "fsdp",
                      2 * at.chip_at(k) + at.core)

    def start(self):
        for k in self.order:
            self.across(k).start()
            if not self.made:
                self.load(k).start()

    def pass_on(self, k):
        self.across(k).wait()
        if not self.made:
            self.load(k).wait()

        def add(at):
            self.own[k, at] = (self.own[k, at].astype(F32) + self.near[k, at].astype(F32)).astype(BF)

        strips(self.rows, add)

        @pl.when(k > 0)
        def _():
            self.send(k).start()

    def forward(self):
        def step(i, carry):
            self.pass_on(lax.rem(i + 1, self.at.chips))
            return carry

        lax.fori_loop(0, self.at.chips, step, 0)

    def wait(self):
        for k in range(1, self.at.chips):
            self.send(k).wait()

    def total(self, at):
        out = self.own[0, at].astype(F32)
        for k in range(self.at.chips - 1):
            out += self.far[k, at].astype(F32)
        return out


class LineSum:
    def __init__(self, at, chunk, ring, arrive, send, recv, credit, out, out_sem, skip=0, feed=None):
        self.at, self.chunk, self.ring, self.arrive, self.skip = at, chunk, ring, arrive, skip
        self.send, self.recv, self.credit, self.out, self.out_sem = send, recv, credit, out, out_sem
        self.feed = feed
        self.slots = ring.shape[1]
        self.count = chunk.shape[0]
        self.kind = at.mid.astype(jnp.int32)

    def slot(self, j):
        return lax.rem(j, self.slots)

    def inward(self, j):
        return remote(self.chunk.at[j], self.ring.at[self.kind, self.slot(j)], self.send.at[0, j],
                      self.recv.at[self.kind, j], "replica", self.at.inner)

    def outward(self, j, src):
        return remote(src, self.out(j), self.send.at[1, j], self.recv.at[2, j], "replica", self.at.outer)

    def keep(self, j):
        return pltpu.make_async_copy(self.chunk.at[j], self.out(j), self.out_sem.at[j])

    def take_in(self, kind, j, plane):
        here = self.ring.at[kind, self.slot(j)]
        pltpu.make_async_copy(here, here, self.recv.at[kind, j]).wait()
        self.chunk[j] = (self.chunk[j].astype(F32) + self.ring[kind, self.slot(j)].astype(F32)).astype(BF)

        @pl.when(j + self.slots < self.count)
        def _():
            pl.semaphore_signal(self.credit, inc=1, device_id={"replica": plane}, device_id_type=MESH)

    def up(self, j):
        if self.feed:
            @pl.when(j + LEAD < self.count)
            def _():
                self.feed(j + LEAD)

        @pl.when(j >= self.skip)
        def _():
            pltpu.make_async_copy(self.chunk.at[j], self.chunk.at[j], self.arrive.at[j]).wait()

        @pl.when(self.at.has_outer)
        def _():
            self.take_in(0, j, self.at.outer)

        @pl.when(j >= self.slots)
        def _():
            pl.semaphore_wait(self.credit, 1)

        self.inward(j).start()

    def meet(self, j):
        self.inward(j).wait_send()
        self.take_in(1, j, self.at.inner)

        @pl.when(self.at.has_outer)
        def _():
            self.outward(j, self.chunk.at[j]).start()

        self.keep(j).start()

    def take(self, j):
        pltpu.make_async_copy(self.out(j), self.out(j), self.recv.at[2, j]).wait()

        @pl.when(self.at.has_outer)
        def _():
            self.outward(j, self.out(j)).start()

    def settle(self):
        def step(j, carry):
            @pl.when(self.at.mid)
            def _():
                self.keep(j).wait()

            @pl.when(jnp.logical_not(self.at.mid))
            def _():
                self.inward(j).wait_send()

            @pl.when(self.at.has_outer)
            def _():
                self.outward(j, self.chunk.at[j]).wait_send()

            return carry

        lax.fori_loop(0, self.count, step, 0)


class Lines:
    def __init__(self, *lines):
        self.lines = lines
        self.order = [(i, j) for i, line in enumerate(lines) for j in range(line.count)]
        self.at = 0

    def run(self, steps=None, body=None):
        begin = self.at
        last = len(self.order) + LAG_END
        stop = last if steps is None else min(self.at + steps, len(self.order))
        while self.at < stop:
            first, size = self.at, 1
            now = self.parts(first)
            while first + size < stop and self.kinds(first + size) == self.kinds(first):
                size += 1

            def step(m, carry, now=now, first=first):
                up, mid, rest = now
                if up:
                    self.lines[up[0]].up(up[1] + m)
                if mid:
                    @pl.when(self.lines[mid[0]].at.mid)
                    def _():
                        self.lines[mid[0]].meet(mid[1] + m)
                if rest:
                    @pl.when(jnp.logical_not(self.lines[rest[0]].at.mid))
                    def _():
                        self.lines[rest[0]].take(rest[1] + m)
                if body:
                    body(first - begin + m)
                return carry

            lax.fori_loop(0, size, step, 0)
            self.at += size

    def parts(self, t):
        return [self.order[i] if 0 <= i < len(self.order) else None for i in (t, t - LAG_MID, t - LAG_END)]

    def kinds(self, t):
        return [part and part[0] for part in self.parts(t)]

    def settle(self):
        for line in self.lines:
            line.settle()


def rms_of(values):
    return lax.rsqrt(jnp.mean(values * values, axis=-1, keepdims=True) + EPSILON)


def qkv_pieces(at, w, wc, qw):
    q_w, k_w = QUERY_HEADS * HEAD_WIDTH, KEY_VALUE_HEADS * HEAD_WIDTH
    shared = at.n // KEY_VALUE_HEADS
    depth = w.shape[0]

    def cols(start, width):
        return pl.ds(pl.multiple_of(start, HEAD_WIDTH), width)

    def rows(s):
        return pl.ds(pl.multiple_of(s * depth, depth), depth)

    return [
        (lambda t: w.at[:, cols(t * qw, qw)], lambda s: wc.at[rows(s), pl.ds(0, qw)]),
        (lambda t: w.at[:, cols(q_w + t // shared * HEAD_WIDTH, HEAD_WIDTH)],
         lambda s: wc.at[rows(s), pl.ds(qw, HEAD_WIDTH)]),
        (lambda t: w.at[:, cols(q_w + k_w + t // shared * HEAD_WIDTH, HEAD_WIDTH)],
         lambda s: wc.at[rows(s), pl.ds(qw + HEAD_WIDTH, HEAD_WIDTH)]),
    ]


def col_piece(w, wc, share, first=0):
    depth = w.shape[0]
    return (lambda t: w.at[:, pl.ds(pl.multiple_of(t * share, HEAD_WIDTH), share)],
            lambda s: wc.at[pl.ds(pl.multiple_of(s * depth, depth), depth), pl.ds(first, share)])


class Weights:
    def __init__(self, at, pieces, send, recv, z_send, z_recv):
        self.at, self.pieces, self.send, self.recv, self.z_send, self.z_recv = at, pieces, send, recv, z_send, z_recv
        self.mine = at.core == lax.rem(at.z, 2)
        self.parity = lax.rem(at.z + at.core, 2)
        self.partner = at.z + 1 - 2 * lax.rem(at.z, 2)

    def cols(self, i, t):
        return self.pieces[i][0](t)

    def rows(self, i, s):
        return self.pieces[i][1](s)

    def local(self, i):
        return pltpu.make_async_copy(self.cols(i, self.at.f), self.rows(i, self.at.f), self.recv.at[i, 0])

    def copy(self, i, j):
        to = self.at.near(j)
        return remote(self.cols(i, to), self.rows(i, self.at.f), self.send.at[i, j], self.recv.at[i, j], "fsdp", to)

    def beside(self, i, j):
        here = self.rows(i, self.at.near_from(j))
        return remote(here, here, self.z_send.at[i, j], self.z_recv.at[i, j], "replica", self.partner)

    def start(self, i):
        self.local(i).start()
        self.copy(i, 1).start()

        @pl.when(self.mine)
        def _():
            for j in range(2, self.at.n):
                self.copy(i, j).start()

    def hand_over(self, i):
        for m in range(1, self.at.chips):
            j = 2 * m + self.parity
            here = self.rows(i, self.at.near_from(j))
            pltpu.make_async_copy(here, here, self.recv.at[i, j]).wait()
            self.beside(i, j).start()

    def wait(self, i):
        self.local(i).wait()
        self.copy(i, 1).wait()

        @pl.when(self.mine)
        def _():
            for j in range(2, self.at.n):
                self.copy(i, j).wait_send()

        for m in range(1, self.at.chips):
            self.beside(i, 2 * m + self.parity).wait_send()
            self.beside(i, 2 * m + 1 - self.parity).wait_recv()


def front_kernel(n, n_z, x_ref, gain1_ref, gain2_ref, gainq_ref, gaink_ref, place_ref, table_ref, wout_ref,
                 wqkv_ref, g_ref, gate_ref, up_ref, down_ref,
                 h_ref, q_ref, kv_ref, ctx_ref, proj_ref, places_ref,
                 n1_ref, wc_ref, n2_ref, gall_ref, pair_c, down_c,
                 near, mine, far, stage, own, n1_block, wc,
                 s_x, r_x, s_p, r_p, s_g, s_n, s_w, s_h, s_r, s_a, s_b, s_c, r_c, s_z, r_z, s_xz, r_xz):
    at = Place(n, n_z)
    rows = x_ref.shape[0]
    heads = QUERY_HEADS // n
    qw = heads * HEAD_WIDTH
    halo = LMAX
    at.greet(True)
    weights = Weights(at, qkv_pieces(at, wqkv_ref, wc_ref, qw), s_x, r_x, s_xz, r_xz)
    for i in range(3):
        weights.start(i)

    def rows_of(g):
        return pl.ds(pl.multiple_of(g * rows, rows), rows)

    places = Exchange(at, [(lambda t: place_ref, lambda s: places_ref.at[rows_of(s)])], s_p, r_p)
    share = down_c.shape[1]
    mlp = Weights(
        at, [col_piece(gate_ref, pair_c, share), col_piece(up_ref, pair_c, share, share), col_piece(down_ref, down_c, share)],
        s_c, r_c, s_z, r_z)
    places.start()

    def norm1(strip):
        x = x_ref[strip].astype(F32)
        own[strip] = (x * rms_of(x) * gain1_ref[...]).astype(BF)

    strips(rows, norm1)
    n1 = gather_rows(at, own, n1_ref, s_g)
    n1.start()
    n1.relay()
    for i in range(3):
        weights.hand_over(i)
    n1.forward()
    n1.wait()
    places.wait()
    for i in range(3):
        weights.wait(i)
    mlp.start(0)
    mlp.start(1)
    to_vmem = pltpu.make_async_copy(wc_ref, wc, s_w.at[0])
    to_vmem.start()

    def block_of(g):
        return pltpu.make_async_copy(n1_ref.at[rows_of(g)], n1_block.at[lax.rem(g, 2)], s_n.at[lax.rem(g, 2)])

    block_of(0).start()
    to_vmem.wait()

    def project(g, carry):
        @pl.when(g + 1 < n)
        def _():
            block_of(g + 1).start()

        at_rows = rows_of(g)
        cosine, sine = rotation_of(places_ref[at_rows], table_ref)
        block_of(g).wait()
        proj = dot(n1_block[lax.rem(g, 2)], wc[...])
        proj_ref[at_rows] = proj[:, :qw + HEAD_WIDTH]
        for head in range(heads + 1):
            lanes = slice(head * HEAD_WIDTH, (head + 1) * HEAD_WIDTH)
            raw = proj[:, lanes]
            gain = gainq_ref if head < heads else gaink_ref
            turned = rotate_with(raw * rms_of(raw) * gain[...], cosine, sine).astype(BF)
            if head < heads:
                q_ref[at_rows, lanes] = turned
            else:
                kv_ref[g, halo:, :HEAD_WIDTH] = turned
        kv_ref[g, halo:, HEAD_WIDTH:] = proj[:, qw + HEAD_WIDTH:].astype(BF)
        return carry

    lax.fori_loop(0, n, project, 0)
    not_first, not_last = at.z > 0, at.z < n_z - 1

    def halo_copy():
        return remote(kv_ref.at[:, pl.ds(rows, halo)], kv_ref.at[:, pl.ds(0, halo)], s_h.at[0], s_h.at[1], "replica",
                      jnp.minimum(at.z + 1, n_z - 1))

    @pl.when(not_last)
    def _():
        halo_copy().start()

    @pl.when(not_first)
    def _():
        here = kv_ref.at[:, pl.ds(0, halo)]
        pltpu.make_async_copy(here, here, s_h.at[1]).wait()

    @pl.when(jnp.logical_not(not_first))
    def _():
        kv_ref[:, :halo] = jnp.zeros((n, halo, 2 * HEAD_WIDTH), BF)

    sum_o = ScatterSum(at, stage, near, mine, far, s_r, made=True)

    def attend(g):
        at_rows = rows_of(g)
        mask = window_mask(places_ref[at_rows], rows, halo)
        keys, values = kv_ref[g, :, :HEAD_WIDTH], kv_ref[g, :, HEAD_WIDTH:]
        for head in range(heads):
            lanes = slice(head * HEAD_WIDTH, (head + 1) * HEAD_WIDTH)
            probs = softmax_of(q_ref[at_rows, lanes], keys, mask).astype(BF)
            ctx_ref[at_rows, lanes] = dot(probs, values).astype(BF)
        return dot(ctx_ref[at_rows], wout_ref[...]).astype(BF)

    def attend_both(i, carry):
        k = lax.rem(i + 1, at.chips)
        q = at.chip_at(k)
        stage[k] = attend(2 * q + 1 - at.core)
        sum_o.across(k).start()
        mine[k] = attend(2 * q + at.core)

        @pl.when(i > 0)
        def _():
            sum_o.pass_on(jnp.maximum(i, 1))

        return carry

    lax.fori_loop(0, at.chips, attend_both, 0)
    sum_o.pass_on(0)
    mlp.start(2)
    mlp.hand_over(0)
    sum_o.wait()

    def norm2(strip):
        h = x_ref[strip].astype(F32) + sum_o.total(strip)
        h_ref[strip] = h
        own[strip] = (h * rms_of(h) * gain2_ref[...]).astype(BF)

    strips(rows, norm2)
    n2 = gather_rows(at, own, n2_ref, s_a)
    g_all = gather_rows(at, g_ref, gall_ref, s_b)
    n2.start()
    mlp.hand_over(1)
    n2.relay()
    g_all.start()
    n2.forward()
    g_all.relay()
    mlp.hand_over(2)
    g_all.forward()
    n2.wait()
    g_all.wait()

    @pl.when(not_last)
    def _():
        halo_copy().wait_send()

    for i in range(3):
        mlp.wait(i)


class Feed:
    def __init__(self, at, grads, chunk, send, recv):
        self.at, self.grads, self.chunk, self.send, self.recv = at, grads, chunk, send, recv
        self.depth = chunk.shape[1]

    def rows(self, grad, t):
        return grad.at[pl.ds(pl.multiple_of(t * self.depth, self.depth), self.depth)]

    def copy(self, grad, c, j):
        to = self.at.near(j)
        return remote(self.rows(grad, to), self.chunk.at[c], self.send.at[c], self.recv.at[c], "fsdp", to)

    def start(self, c):
        n = self.at.n
        j = lax.rem(c, n)
        for i, grad in enumerate(self.grads):
            @pl.when((c // n == i) & (j == 0))
            def _(grad=grad):
                pltpu.make_async_copy(self.rows(grad, self.at.f), self.chunk.at[c], self.recv.at[c]).start()

            @pl.when((c // n == i) & (j > 0))
            def _(grad=grad):
                self.copy(grad, c, j).start()

    def settle(self):
        def step(c, carry):
            @pl.when(lax.rem(c, self.at.n) > 0)
            def _():
                self.copy(self.grads[0], c, lax.rem(c, self.at.n)).wait_send()

            return carry

        lax.fori_loop(0, len(self.grads) * self.at.n, step, 0)


def start_all(copies):
    for c in copies:
        c.start()


def rotate_with(values, cosine, sine):
    return values * cosine + pltpu.roll(values, HEAD_WIDTH // 2, 1) * sine


def rotation_table():
    places = HEAD_WIDTH * -(-LMAX // HEAD_WIDTH)
    inverse = ROPE_BASE ** (-(2.0 * np.arange(HEAD_WIDTH // 2)) / HEAD_WIDTH)
    angles = np.arange(places)[:, None] * inverse[None, :]
    cosine, sine = np.cos(angles), np.sin(angles)
    rest = np.concatenate([cosine, cosine, -sine, sine], axis=1).astype(np.float32)
    terms = []
    for _ in range(3):
        terms.append(rest.astype(jnp.bfloat16))
        rest = rest - terms[-1].astype(np.float32)
    return jnp.asarray(np.stack(terms))


def rotation_of(places, table):
    lane = lax.broadcasted_iota(jnp.int32, (places.shape[0], table.shape[1]), 1).astype(F32)
    pick = (lane == places.astype(F32)[:, :1]).astype(F32).astype(BF)
    both = dot(pick, table[0]) + dot(pick, table[1]) + dot(pick, table[2])
    return both[:, :HEAD_WIDTH], both[:, HEAD_WIDTH:]


def window_mask(places, rows, halo):
    i_at = lax.broadcasted_iota(jnp.int32, (rows, halo + rows), 0) + halo
    j_at = lax.broadcasted_iota(jnp.int32, (rows, halo + rows), 1)
    back = (i_at - j_at).astype(F32)
    return (back >= 0) & (back <= places.astype(F32)[:, :1])


def softmax_of(queries, keys, mask):
    scores = jnp.where(mask, dot_cols(queries, keys) * HEAD_WIDTH ** (-0.5), NEG_FILL)
    terms = jnp.exp(scores - jnp.max(scores, axis=1, keepdims=True))
    return terms / jnp.sum(terms, axis=1, keepdims=True)


def back_kernel(n, n_z, part_ref, party_ref, x_ref, h_ref, g_ref, gain1_ref, gain2_ref, gainq_ref, gaink_ref,
                down_ref, n2_ref, dgate_ref, dup_ref, wout_ref, wqkv_ref, q_ref, kv_ref, ctx_ref, proj_ref, table_ref, place_ref,
                n1_ref,
                dx_ref, y_ref, gains_ref, gmlp_ref, gqkv_ref, dhall_ref, gate_ref, up_ref,
                near, mine, far, stage, dh, plane_gain, all_gain,
                chunk, ring, chunk2, ring2, dh_block, gout, d_kv, d_proj, halo_out, halo_in, n1_cols, qkv_send, d_in, tile_out,
                s_r, s_a, s_p, r_p, s_q, r_q, s_c, r_c, s_z, r_z, s_o, s_c2, r_c2, s_z2, r_z2, s_o2, credit, done, s_d, s_n, s_h, s_e, s_t):
    at = Place(n, n_z)
    share, share_out = chunk.shape[2], chunk2.shape[2]
    rows, width = x_ref.shape
    depth = chunk.shape[1]
    outs = -(-width // share_out)
    heads = QUERY_HEADS // n
    qw = heads * HEAD_WIDTH
    halo = LMAX
    scale = HEAD_WIDTH ** (-0.5)
    own = dh_block
    own_gain = all_gain.at[at.z]
    at.greet(True)

    def mlp_place(j):
        s = at.near_from(lax.rem(j, n))
        return gmlp_ref.at[j // n, :, pl.ds(pl.multiple_of(s * share, HEAD_WIDTH), share)]

    def attn_place(j):
        col = jnp.where(j < outs, j, outs + at.near_from(jnp.maximum(j - outs, 0)))
        return gqkv_ref.at[:, pl.ds(pl.multiple_of(col * share_out, HEAD_WIDTH), share_out)]

    feed = Feed(at, (down_ref, gate_ref, up_ref), chunk, s_c, r_c)
    lines = Lines(
        LineSum(at, chunk, ring, r_c, s_z, r_z, credit.at[0], mlp_place, s_o, 0, feed.start),
        LineSum(at, chunk2, ring2, r_c2, s_z2, r_z2, credit.at[1], attn_place, s_o2, outs))
    sum_n2 = ScatterSum(at, part_ref, near, mine, far, s_r.at[0])
    sum_n2.start()
    for c in range(LEAD):
        feed.start(jnp.int32(c))
    load = pltpu.make_async_copy(dgate_ref, d_in, s_e.at[0])
    load.start()
    lines.run(1)
    sum_n2.forward()

    def fetch_cols(ref, j):
        return pltpu.make_async_copy(
            ref.at[:, pl.ds(pl.multiple_of(at.near(j) * depth, depth), depth)], n1_cols.at[lax.rem(j, 2)],
            s_n.at[lax.rem(j, 2)])

    def tiles(ref, per):
        def put(j):
            return pltpu.make_async_copy(
                tile_out.at[lax.rem(j, 2)], ref.at[pl.ds(pl.multiple_of(at.near(j) * depth, depth), depth)],
                s_t.at[lax.rem(j, 2)])

        def tile(j):
            @pl.when(j + 1 < n)
            def _():
                fetch_cols(n2_ref, j + 1).start()

            fetch_cols(n2_ref, j).wait()

            @pl.when(j > 1)
            def _():
                put(j - 2).wait()

            tile_out[lax.rem(j, 2)] = dot_rows(n1_cols[lax.rem(j, 2)], d_in[...]).astype(BF)
            put(j).start()

        def body(step):
            for r in range(per):
                j = step * per + r

                @pl.when(j < n)
                def _(j=j):
                    tile(j)

        def end():
            put(n - 2).wait()
            put(n - 1).wait()

        fetch_cols(n2_ref, 0).start()
        return body, end

    per_tile = -(-n // 3)
    load.wait()
    body, end = tiles(gate_ref, per_tile)
    lines.run(3, body)
    end()
    load = pltpu.make_async_copy(dup_ref, d_in, s_e.at[0])
    load.start()
    lines.run(n - 8)
    sum_n2.wait()
    own_gain[...] = jnp.zeros_like(own_gain)

    def back_mlp(strip):
        d_n2 = sum_n2.total(strip)
        h = h_ref[strip]
        r2 = rms_of(h)
        u2 = h * r2
        own_gain[1:2] += jnp.sum(d_n2 * u2, axis=0, keepdims=True)
        d_h = g_ref[strip].astype(F32) + norm_back(d_n2 * gain2_ref[...], u2, r2)
        dh[strip] = d_h
        own[strip] = d_h.astype(BF)

    strips(rows, back_mlp)
    gather = gather_rows(at, own, dhall_ref, s_a)
    gather.start()
    load.wait()
    body, end = tiles(up_ref, per_tile)
    lines.run(3, body)
    end()
    lines.run(n // 2 - 4)
    gather.relay()
    lines.run(2)
    gather.forward()
    lines.run(1)
    gather.wait()
    sum_y = ScatterSum(at, party_ref, near, mine, far, s_r.at[2])
    sum_y.start()
    lines.run(1)
    sum_y.forward()
    gout[...] = jnp.zeros_like(gout)

    def rows_of(g):
        return pl.ds(pl.multiple_of(g * rows, rows), rows)

    def block_of(g):
        return pltpu.make_async_copy(dhall_ref.at[rows_of(g)], dh_block, s_d.at[0])

    def attention(g):
        at_rows = rows_of(g)
        block_of(g).start()
        mask = window_mask(place_ref[at_rows], rows, halo)
        keys, values = kv_ref[g, :, :HEAD_WIDTH], kv_ref[g, :, HEAD_WIDTH:]
        cosine, sine = rotation_of(place_ref[at_rows], table_ref)
        block_of(g).wait()
        d_ctx = dot_cols(dh_block[...], wout_ref[...]).astype(BF)
        gout[:, :width] += dot_rows(ctx_ref[at_rows], dh_block[...])
        d_k = jnp.zeros((halo + rows, HEAD_WIDTH), F32)
        d_v = jnp.zeros((halo + rows, HEAD_WIDTH), F32)
        for head in range(heads):
            lanes = slice(head * HEAD_WIDTH, (head + 1) * HEAD_WIDTH)
            queries, d_c = q_ref[at_rows, lanes], d_ctx[:, lanes]
            probs = softmax_of(queries, keys, mask)
            d_v += dot_rows(probs.astype(BF), d_c)
            d_p = dot_cols(d_c, values)
            d_s = (probs * (d_p - jnp.sum(probs * d_p, axis=1, keepdims=True))).astype(BF)
            d_k += dot_rows(d_s, queries) * scale
            dq_g = rotate_with(dot(d_s, keys) * scale, cosine, -sine)
            raw = proj_ref[at_rows, lanes]
            rms = rms_of(raw)
            hat = raw * rms
            own_gain[2:3, :HEAD_WIDTH] += jnp.sum(dq_g * hat, axis=0, keepdims=True)
            d_proj[at_rows, lanes] = norm_back(dq_g * gainq_ref[...], hat, rms).astype(BF)
        halo_out[g, :, :HEAD_WIDTH] = d_k[:halo].astype(BF)
        halo_out[g, :, HEAD_WIDTH:] = d_v[:halo].astype(BF)
        d_kv[g, :, :HEAD_WIDTH] = d_k[halo:]
        d_kv[g, :, HEAD_WIDTH:] = d_v[halo:]

    lines.run(n, attention)

    not_first, not_last = at.z > 0, at.z < n_z - 1

    def halo_copy():
        return remote(halo_out, halo_in, s_h.at[0], s_h.at[1], "replica", jnp.maximum(at.z - 1, 0))

    @pl.when(not_first)
    def _():
        halo_copy().start()

    for i in range(outs):
        chunk2[i] = gout[:, i * share_out:(i + 1) * share_out].astype(BF)
    lines.run(1)
    sum_y.wait()

    def finish(strip):
        y_ref[strip] = (h_ref[strip] + sum_y.total(strip)).astype(BF)

    strips(rows, finish)
    for k in range(1, n):
        pl.semaphore_signal(done, inc=1, device_id={"fsdp": at.to(k)}, device_id_type=MESH)

    @pl.when(not_last)
    def _():
        pltpu.make_async_copy(halo_in, halo_in, s_h.at[1]).wait()

    @pl.when(jnp.logical_not(not_last))
    def _():
        halo_in[...] = jnp.zeros_like(halo_in)

    def keys_back(g):
        at_rows = rows_of(g)
        d_kv[g, rows - halo:] += halo_in[g].astype(F32)
        cosine, sine = rotation_of(place_ref[at_rows], table_ref)
        dk_g = rotate_with(d_kv[g, :, :HEAD_WIDTH], cosine, -sine)
        raw = proj_ref[at_rows, qw:qw + HEAD_WIDTH]
        rms = rms_of(raw)
        hat = raw * rms
        own_gain[2:3, HEAD_WIDTH:2 * HEAD_WIDTH] += jnp.sum(dk_g * hat, axis=0, keepdims=True)
        d_proj[at_rows, qw:qw + HEAD_WIDTH] = norm_back(dk_g * gaink_ref[...], hat, rms).astype(BF)
        d_proj[at_rows, qw + HEAD_WIDTH:] = d_kv[g, :, HEAD_WIDTH:].astype(BF)

    per_step = n // 2

    def keys_back_some(i):
        for m in range(per_step):
            keys_back(i * per_step + m)

    lines.run(2, keys_back_some)

    def cols_of(j):
        return fetch_cols(n1_ref, j)

    own_qkv = pltpu.make_async_copy(qkv_send.at[0], chunk2.at[outs], r_c2.at[outs])

    def qkv_copy(j):
        return remote(qkv_send.at[j], chunk2.at[outs + j], s_c2.at[j], r_c2.at[outs + j], "fsdp", at.near(j))

    cols_of(0).start()

    def qkv_grad(j):
        @pl.when(j + 1 < n)
        def _():
            cols_of(j + 1).start()

        cols_of(j).wait()
        qkv_send[j] = dot_rows(n1_cols[lax.rem(j, 2)], d_proj[...]).astype(BF)

        @pl.when(j == 0)
        def _():
            own_qkv.start()

        @pl.when(j > 0)
        def _():
            qkv_copy(j).start()

    per_out = n // 4

    def qkv_grads(i):
        for m in range(per_out):
            qkv_grad(i * per_out + m)

    sum_n1 = ScatterSum(at, stage, near, mine, far, s_r.at[1], made=True)

    def n1_part(k):
        q = at.chip_at(k)
        stage[k] = dot_cols(d_proj[rows_of(2 * q + 1 - at.core)], wqkv_ref[...]).astype(BF)
        mine[k] = dot_cols(d_proj[rows_of(2 * q + at.core)], wqkv_ref[...]).astype(BF)

    def both(i):
        qkv_grads(i)
        for r in range(at.chips // 4):
            n1_part(i * (at.chips // 4) + r)

    lines.run(4, both)
    pl.semaphore_wait(done, n - 1)
    sum_n1.start()
    lines.run(1)
    sum_n1.forward()
    lines.run(outs + n - 4 - 1 - 2 - -2)
    sum_n1.wait()

    def back_attn(strip):
        d_n1 = sum_n1.total(strip)
        x = x_ref[strip].astype(F32)
        r1 = rms_of(x)
        u1 = x * r1
        own_gain[0:1] += jnp.sum(d_n1 * u1, axis=0, keepdims=True)
        dx_ref[strip] = (dh[strip] + norm_back(d_n1 * gain1_ref[...], u1, r1)).astype(BF)

    strips(rows, back_attn)
    gains = Exchange(at, [(lambda t: own_gain, lambda s: plane_gain.at[s])], s_p, r_p)
    gains.start()
    lines.run(1)
    gains.wait()
    own_gain[...] = jnp.sum(plane_gain[...], axis=0)
    others = [
        remote(own_gain, all_gain.at[at.z], s_q.at[k], r_q.at[k], "replica", at.plane(k)) for k in range(1, n_z)]
    start_all(others)
    lines.run()
    for c in others:
        c.wait()
    gains_ref[...] = jnp.sum(all_gain[...], axis=0)
    feed.settle()
    for j in range(1, n):
        qkv_copy(j).wait_send()

    @pl.when(not_first)
    def _():
        halo_copy().wait_send()

    lines.settle()


def front(n, n_z, x, gain1, gain2, gain_q, gain_k, place, table, w_out, w_qkv, g, gate, up, down):
    rows, width = x.shape
    chips, share, total = n // 2, gate.shape[1] // n, n * rows
    qw = QUERY_HEADS * HEAD_WIDTH // n
    wide = qw + 2 * HEAD_WIDTH
    block = functools.partial(pltpu.VMEM, dtype=BF)
    shape = jax.ShapeDtypeStruct
    return pl.pallas_call(
        functools.partial(front_kernel, n, n_z),
        out_shape=(
            shape((rows, width), F32), shape((total, qw), BF), shape((n, LMAX + rows, 2 * HEAD_WIDTH), BF),
            shape((total, qw), BF), shape((total, qw + HEAD_WIDTH), F32), shape((total, HEAD_WIDTH), BF),
            shape((total, width), BF), shape((width, wide), BF), shape((total, width), BF), shape((total, width), BF),
        ) + (shape((width, 2 * share), BF), shape((width, share), BF)),
        in_specs=[VMEM] * 8 + [ANY] * 5,
        out_specs=(VMEM,) * 6 + (ANY,) * 6,
        scratch_shapes=[
            block((chips, rows, width)), block((chips, rows, width)), block((chips - 1, rows, width)),
            block((chips, rows, width)), block((rows, width)), block((2, rows, width)), block((width, wide)),
            DMA((3, n)), DMA((3, n)), DMA((1, n)), DMA((1, n)), DMA((6, n)), DMA((2,)), DMA((1,)), DMA((2,)),
            DMA((5, n)), DMA((6, n)), DMA((6, n)), DMA((3, n)), DMA((3, n)), DMA((3, n)), DMA((3, n)),
            DMA((3, n)), DMA((3, n))],
        compiler_params=pltpu.CompilerParams(collective_id=0, has_side_effects=True, vmem_limit_bytes=60 << 20),
        name="front",
    )(x, gain1, gain2, gain_q, gain_k, place, table, w_out, w_qkv, g, gate, up, down)


def back(n, n_z, part, part_y, x, h, g, gain1, gain2, gain_q, gain_k, down, n2, d_gate, d_up, w_out, w_qkv, q, kv, ctx, proj,
         table, places, n1):
    rows, width = x.shape
    chips, share, wide, depth = n // 2, down.shape[1], w_qkv.shape[1], width // n
    outs = -(-width // wide)
    block = functools.partial(pltpu.VMEM, dtype=BF)
    gains = (8, width)
    count2 = outs + n
    slots = 2 + 16 // n
    return pl.pallas_call(
        functools.partial(back_kernel, n, n_z),
        out_shape=(
            jax.ShapeDtypeStruct((rows, width), BF),
            jax.ShapeDtypeStruct((rows, width), BF),
            jax.ShapeDtypeStruct(gains, F32),
            jax.ShapeDtypeStruct((3, depth, n * share), BF),
            jax.ShapeDtypeStruct((depth, count2 * wide), BF),
            jax.ShapeDtypeStruct((n * rows, width), BF),
            jax.ShapeDtypeStruct((width, share), BF),
            jax.ShapeDtypeStruct((width, share), BF),
        ),
        in_specs=[ANY, ANY] + [VMEM] * 7 + [ANY] * 4 + [VMEM] * 8 + [ANY],
        out_specs=(VMEM, VMEM, VMEM, ANY, ANY, ANY, ANY, ANY),
        scratch_shapes=[
            block((chips, rows, width)), block((chips, rows, width)), block((chips - 1, rows, width)),
            block((chips, rows, width)), pltpu.VMEM((rows, width), F32),
            pltpu.VMEM((n,) + gains, F32), pltpu.VMEM((n_z,) + gains, F32),
            block((3 * n, depth, share)), block((2, slots, depth, share)),
            block((count2, depth, wide)), block((2, slots, depth, wide)),
            block((rows, width)), pltpu.VMEM((depth, outs * wide), F32),
            pltpu.VMEM((n, rows, 2 * HEAD_WIDTH), F32), block((n * rows, wide)),
            block((n, LMAX, 2 * HEAD_WIDTH)), block((n, LMAX, 2 * HEAD_WIDTH)),
            block((2, n * rows, depth)), block((n, depth, wide)), block((n * rows, share)), block((2, depth, share)),
            DMA((3, 5, n)), DMA((6, n)), DMA((1, n)), DMA((1, n)), DMA((n_z,)), DMA((n_z,)),
            DMA((3 * n,)), DMA((3 * n,)), DMA((2, 3 * n)), DMA((3, 3 * n)), DMA((3 * n,)),
            DMA((n,)), DMA((count2,)), DMA((2, count2)), DMA((3, count2)), DMA((count2,)),
            pltpu.SemaphoreType.REGULAR((2,)), pltpu.SemaphoreType.REGULAR, DMA((1,)), DMA((2,)), DMA((2,)), DMA((1,)), DMA((2,))],
        compiler_params=pltpu.CompilerParams(collective_id=2, has_side_effects=True, vmem_limit_bytes=511 << 17),
        name="back",
    )(part, part_y, x, h, g, gain1, gain2, gain_q, gain_k, down, n2, d_gate, d_up, w_out, w_qkv, q, kv, ctx, proj, table, places, n1)


def row_positions(flat_lens, ranks, first_row, count):
    earlier = (ranks[:, None] < ranks[None, :]).astype(jnp.int32)
    starts = jnp.sum(flat_lens[:, None] * earlier, axis=0)
    rows = first_row + jnp.arange(count, dtype=jnp.int32)
    begun = jnp.where(starts[None, :] <= rows[:, None], starts[None, :], 0)
    return rows - jnp.max(begun, axis=1)


def per_device(
    n_replica, tokens, cotangent, w_qkv, w_out, w_gate, w_up, w_down_t,
    gain_attn, gain_mlp, gain_query, gain_key, dealt_lens, seq_order,
):
    rows, width = tokens.shape
    n_fsdp = width // w_qkv.shape[0]
    q_w = QUERY_HEADS * HEAD_WIDTH
    k_w = KEY_VALUE_HEADS * HEAD_WIDTH
    replica = lax.axis_index("replica")
    shared = n_fsdp // KEY_VALUE_HEADS
    heads = QUERY_HEADS // n_fsdp
    qw = heads * HEAD_WIDTH

    pos = row_positions(dealt_lens[0].reshape(-1), seq_order[0], replica * rows, rows)
    depth = w_qkv.shape[0]
    place = jnp.broadcast_to(pos.astype(BF)[:, None], (rows, HEAD_WIDTH))
    table = rotation_table()
    gains = (gain_attn[None], gain_mlp[None], gain_query[None], gain_key[None])
    h, q_low, kv_window, ctx_low, proj, places, n1, w_qkv_c, n2, g_all, pair_c, down_c = front(
        n_fsdp, n_replica, tokens, *gains, place, table, w_out, w_qkv, cotangent, w_gate, w_up, w_down_t)

    both = dot(n2, pair_c)
    share = down_c.shape[1]
    gate, up = both[:, :share], both[:, share:]
    sg = jax.nn.sigmoid(gate)
    silu = gate * sg
    act = (silu * up).astype(BF)
    part_y = dot_cols(act, down_c).astype(BF)

    d_act = dot(g_all, down_c)
    d_gate = (d_act * up * sg * (1.0 + gate * (1.0 - sg))).astype(BF)
    d_up = (d_act * silu).astype(BF)
    d_n2 = dot_cols(d_gate, pair_c[:, :share]) + dot_cols(d_up, pair_c[:, share:])

    input_grad, output, gain_sums, g_mlp, g_attn, _, _, _ = back(
        n_fsdp, n_replica, d_n2.astype(BF), part_y, tokens, h, cotangent, *gains,
        dot_rows(g_all, act).astype(BF), n2, d_gate, d_up,
        w_out, w_qkv_c, q_low, kv_window, ctx_low, proj, table, places, n1)
    wide = qw + 2 * HEAD_WIDTH
    g_out = g_attn[:, :width]
    by_device = [g_attn[:, at:at + wide] for at in range(g_attn.shape[1] - n_fsdp * wide, g_attn.shape[1], wide)]

    def of_key_heads(first):
        parts = [part[:, first:first + HEAD_WIDTH].astype(F32) for part in by_device]
        return [sum(parts[i + 1:i + shared], parts[i]) for i in range(0, n_fsdp, shared)]

    g_qkv = jnp.concatenate(
        [part[:, :qw].astype(F32) for part in by_device] + of_key_heads(qw) + of_key_heads(qw + HEAD_WIDTH), axis=1)
    return (
        output, input_grad, g_qkv, g_out.astype(F32), g_mlp[1].astype(F32), g_mlp[2].astype(F32), g_mlp[0].astype(F32),
        gain_sums[0], gain_sums[1], gain_sums[2, :HEAD_WIDTH], gain_sums[2, HEAD_WIDTH:2 * HEAD_WIDTH])


def solution(mesh):
    n_replica = mesh.shape["replica"]

    def program(*args):
        return per_device(n_replica, *args)

    rows = P(("fsdp", "replica"), None)
    weight = P("fsdp", None)
    return jax.shard_map(
        program,
        mesh=mesh,
        in_specs=(rows, rows) + (weight,) * 5 + (P(),) * 4 + (P("fsdp", None, None), P("fsdp", None)),
        out_specs=(rows, rows) + (weight,) * 5 + (P(),) * 4,
        check_vma=False,
    )
```
